512 devices in a mesh: dp: 32 (over y_lo, z, core), section: 4 (over x), mp: 4 (over y_hi).
Axes of the slice: x: 4, y: 8 (y_hi: 4, y_lo: 2; y = y_hi * 2 + y_lo), z: 8, core: 2. Of those that a mesh axis runs over, the one named last changes fastest.
Arguments:
- saved_inputs: bfloat16 [4, 2, 384, 16, 5120], P('section', None, 'dp', None, 'mp'), may hold values from -150 to 150
- norm_gains: float32 [4, 5120], P('section', 'mp'), may hold values from 0.1 to 1.9
- conv_taps: bfloat16 [4, 15, 5120], P('section', None, 'mp'), may hold values from -1 to 1
- head_weight: bfloat16 [5120, 1024], P('mp'), as said below
- queries: bfloat16 [2, 384, 1024], P(None, 'dp', 'mp'), may hold values from -12 to 12
- key_embeds: bfloat16 [2, 384, 1024], P(None, 'dp', 'mp'), may hold values from -12 to 12
- positives: int32 [2, 384], P(None, 'dp'), may hold values from 0 to 383, each once within a row
- pair_weights: float32 [2, 384], P(None, 'dp'), may hold values from 64 to 256
Outputs:
- input_grads: bfloat16 [4, 2, 384, 16, 5120], P('section', None, 'dp', None, 'mp')
- tap_grads: float32 [4, 15, 5120], P('section', None, 'mp')
- key_grads: float32 [2, 384, 1024], P(None, 'dp', 'mp')
The draws below stay inside these ranges and needn't reach their ends.
Inputs may be any that keep to these rules, and one draw needn't show every extreme that they name: positives[m] names each of the 384 texts of micro-batch m exactly once. `head_weight`: every entry lies within -6 / sqrt(5120) and 6 / sqrt(5120).
All inputs are finite; a program needn't handle non-finite values.
Results may differ from the reference program's by a relative error of at most 0.025.
Values may be sent and summed in bfloat16 or wider, within the bound.
No kernel may reach another device: no remote copies, remote signals or barrier semaphores. Data moves between devices by JAX's collectives and lax.ppermute only.
A program may use at most 64 MiB of HBM per device.

```python
import math
import jax
import jax.numpy as jnp
from jax import lax

D = 5120
EMB = 1024
FRAMES = 16
MICRO = 2
KERNEL = 15
SECTIONS = 4
CLIPS = 384


def draw_queries(key, part):
    key = jax.random.fold_in(key, 11)
    first_key, second_key = jax.random.split(key, 2)
    noise_base = jax.random.truncated_normal(first_key, -4.0, 4.0, (MICRO, CLIPS, EMB), jnp.float32)
    row_scale = jnp.exp(jax.random.uniform(second_key, (MICRO, CLIPS, 1), jnp.float32, math.log(0.3), math.log(3.0)))
    return (noise_base * row_scale).astype(jnp.bfloat16)


def draw_key_embeds(key, part):
    key = jax.random.fold_in(key, 12)
    first_key, second_key = jax.random.split(key, 2)
    noise_base = jax.random.truncated_normal(first_key, -4.0, 4.0, (MICRO, CLIPS, EMB), jnp.float32)
    row_scale = jnp.exp(jax.random.uniform(second_key, (MICRO, CLIPS, 1), jnp.float32, math.log(0.3), math.log(3.0)))
    return (noise_base * row_scale).astype(jnp.bfloat16)


def draw_saved_inputs(key, part):
    key = jax.random.fold_in(key, 13)
    first_key, second_key, third_key = jax.random.split(key, 3)
    full_shape = (SECTIONS, MICRO, CLIPS, FRAMES, D)
    rising = jnp.exp(math.log(3.0) * jnp.arange(D, dtype=jnp.float32) / (D - 1))
    channel_scale = jnp.exp(jax.random.uniform(third_key, (D,), jnp.float32, 0.0, math.log(10.0 / 3.0)))
    noise_base = jax.random.truncated_normal(first_key, -4.0, 4.0, full_shape, jnp.float32)
    row_scale = jnp.exp(jax.random.uniform(second_key, (SECTIONS, MICRO, CLIPS, FRAMES, 1), jnp.float32, math.log(0.3), math.log(3.0)))
    return (noise_base * row_scale * rising * channel_scale).astype(jnp.bfloat16)


def draw_head_weight(key, part):
    key = jax.random.fold_in(key, 14)
    first_key, second_key = jax.random.split(key, 2)
    column_signs = jnp.sign(jax.random.normal(second_key, (EMB,), jnp.float32))
    column_signs = jnp.where(column_signs == 0.0, 1.0, column_signs)
    noise_base = jax.random.truncated_normal(first_key, -4.0, 4.0, (D, EMB), jnp.float32)
    return ((noise_base + 2.0 * column_signs[None, :]) / math.sqrt(D)).astype(jnp.bfloat16)


def draw_conv_taps(key, part):
    key = jax.random.fold_in(key, 15)
    first_key, second_key = jax.random.split(key, 2)
    section_signs = jnp.sign(jax.random.normal(second_key, (SECTIONS, 1, 1), jnp.float32))
    section_signs = jnp.where(section_signs == 0.0, 1.0, section_signs)
    noise_base = 0.3 * jax.random.normal(first_key, (SECTIONS, KERNEL, D), jnp.float32)
    return jnp.clip(noise_base + 0.06 * section_signs, -1.0, 1.0).astype(jnp.bfloat16)


def block_levels(stream_key, shape, cuts, least, largest):
    def one(dim, shards_of):
        heights = jax.random.uniform(jax.random.fold_in(jax.random.fold_in(stream_key, 6), dim), (shards_of,), jnp.float32, least / len(cuts), largest / len(cuts))
        return jnp.repeat(jnp.exp(heights), shape[dim] // shards_of).reshape((-1,) + (1,) * (len(shape) - dim - 1))

    level = one(*cuts[0])
    for cut in cuts[1:]:
        level = level * one(*cut)
    return level


def setup_inputs(seed: int = 0) -> dict:
    streams_of = jax.random.split(jax.random.key(seed), 9)
    saved_inputs = draw_saved_inputs(jax.random.fold_in(streams_of[8], 71), 0)
    norm_gains = jnp.clip(1.0 + 0.18 * jax.random.normal(streams_of[1], (SECTIONS, D), jnp.float32), 0.1, 1.9)
    conv_taps = draw_conv_taps(jax.random.fold_in(streams_of[8], 71), 0)
    head_weight = draw_head_weight(jax.random.fold_in(streams_of[8], 71), 0)
    queries = draw_queries(jax.random.fold_in(streams_of[8], 71), 0)
    key_embeds = draw_key_embeds(jax.random.fold_in(streams_of[8], 71), 0)
    positives = jax.vmap(lambda own: jax.random.permutation(own, CLIPS))(jax.random.split(streams_of[6], MICRO)).reshape((MICRO, CLIPS)).astype(jnp.int32)
    pair_weights = jnp.clip(jnp.exp(math.log(256.0) - 1.3862944 * jax.random.uniform(streams_of[7], (MICRO, CLIPS), jnp.float32) ** block_levels(streams_of[7], (MICRO, CLIPS), ((1, 32),), -0.2, 0.2)), 64.0, 256.0)
    return {"saved_inputs": saved_inputs, "norm_gains": norm_gains, "conv_taps": conv_taps, "head_weight": head_weight, "queries": queries, "key_embeds": key_embeds, "positives": positives, "pair_weights": pair_weights}


epsilon = 1e-05

def frame_conv(signal, weights_wide):
    half_width = KERNEL // 2
    padded = jnp.pad(signal, ((0, 0), (half_width, half_width), (0, 0)))
    running = jnp.zeros_like(signal)
    for offset in range(KERNEL):
        running = running + weights_wide[offset] * padded[:, offset:offset + FRAMES, :]
    return (running, padded)

def frame_conv_back(incoming, weights_wide):
    half_width = KERNEL // 2
    padded = jnp.pad(incoming, ((0, 0), (half_width, half_width), (0, 0)))
    running = jnp.zeros_like(incoming)
    for offset in range(KERNEL):
        start_at = 2 * half_width - offset
        running = running + weights_wide[offset] * padded[:, start_at:start_at + FRAMES, :]
    return running

def section_backward(inputs, norm_gain, conv_weights, upstream):
    inputs_wide = inputs.astype(jnp.float32)
    row_mean = lax.optimization_barrier(jnp.mean(inputs_wide, axis=-1, keepdims=True))
    variance = lax.optimization_barrier(jnp.mean(inputs_wide * inputs_wide, axis=-1, keepdims=True)) - row_mean * row_mean
    inv_std = lax.rsqrt(variance + epsilon)
    normed = (inputs_wide - row_mean) * inv_std
    hidden = normed * norm_gain
    weights_wide = conv_weights.astype(jnp.float32)
    conv_out, padded = frame_conv(hidden, weights_wide)
    sigmoid_gate = jax.nn.sigmoid(conv_out)
    upstream_wide = upstream.astype(jnp.float32)
    grad_conv = upstream_wide * sigmoid_gate * (1.0 + conv_out * (1.0 - sigmoid_gate))
    tap_grad = jnp.stack([lax.optimization_barrier(jnp.sum(grad_conv * padded[:, offset:offset + FRAMES, :], axis=(0, 1))) for offset in range(KERNEL)])
    grad_normed = frame_conv_back(grad_conv, weights_wide) * norm_gain
    first_mean = lax.optimization_barrier(jnp.mean(grad_normed, axis=-1, keepdims=True))
    second_mean = lax.optimization_barrier(jnp.mean(grad_normed * normed, axis=-1, keepdims=True))
    grad_in = upstream_wide + inv_std * (grad_normed - first_mean - normed * second_mean)
    return (grad_in.astype(jnp.bfloat16), tap_grad)

def reference(saved_inputs, norm_gains, conv_taps, head_weight, queries, key_embeds, positives, pair_weights):
    score_scale = 1.0 / math.sqrt(EMB)
    key_list = []
    frame_list = []
    for micro_index in range(MICRO):
        scores = jnp.dot(queries[micro_index], key_embeds[micro_index].T, preferred_element_type=jnp.float32) * score_scale
        row_max = lax.optimization_barrier(jnp.max(scores, axis=1, keepdims=True))
        exp_scores = jnp.exp(scores - row_max)
        softmax_probs = exp_scores / lax.optimization_barrier(jnp.sum(exp_scores, axis=1, keepdims=True))
        positive_hot = (positives[micro_index][:, None] == jnp.arange(CLIPS, dtype=jnp.int32)[None, :]).astype(jnp.float32)
        pair_grad = (pair_weights[micro_index][:, None] * (softmax_probs - positive_hot)).astype(jnp.bfloat16)
        query_grad = (jnp.dot(pair_grad, key_embeds[micro_index], preferred_element_type=jnp.float32) * score_scale).astype(jnp.bfloat16)
        key_list.append(jnp.dot(pair_grad.T, queries[micro_index], preferred_element_type=jnp.float32) * score_scale)
        pooled = jnp.dot(query_grad, head_weight.T, preferred_element_type=jnp.float32)
        frame_list.append((pooled / FRAMES).astype(jnp.bfloat16))
    section_results = [[None] * MICRO for section_index in range(SECTIONS)]
    tap_totals = [jnp.zeros((KERNEL, D), jnp.float32) for section_index in range(SECTIONS)]
    for micro_index in range(MICRO):
        upstream = jnp.broadcast_to(frame_list[micro_index][:, None, :], (CLIPS, FRAMES, D))
        for section_index in reversed(range(SECTIONS)):
            grad_in, tap_grad = section_backward(saved_inputs[section_index, micro_index], norm_gains[section_index], conv_taps[section_index], upstream)
            section_results[section_index][micro_index] = grad_in
            tap_totals[section_index] = tap_totals[section_index] + tap_grad
            upstream = grad_in
    input_grads = jnp.stack([jnp.stack(section_results[section_index]) for section_index in range(SECTIONS)])
    tap_grads = jnp.stack(tap_totals)
    key_grads = jnp.stack(key_list)
    return (input_grads, tap_grads, key_grads)
```

```python
import functools

import jax
import jax.numpy as jnp
from jax import lax
from jax.experimental import pallas as pl
from jax.experimental.pallas import tpu as pltpu
from jax.sharding import PartitionSpec as P

D = 5120
EMB = 1024
FRAMES = 16
KERNEL = 15
HALF = KERNEL // 2
SECTIONS = 4
MP = 4
DP = 32
MICRO = 2
SHARD = 12
OWN = SHARD // SECTIONS
CLIPS = MICRO * OWN
ROWS = CLIPS * FRAMES
TEXTS = DP * MICRO * SHARD
WIDE = D // MP
SLICE = EMB // MP
LANES = 128
BLOCKS = WIDE // LANES
PAD = 8
SCORE_SCALE = 1.0 / 32.0
EPSILON = 1e-05
F32 = jnp.float32
BF16 = jnp.bfloat16

NT = (((1,), (1,)), ((), ()))
VMEM = pl.BlockSpec(memory_space=pltpu.VMEM)
PARAMS = pltpu.CompilerParams(vmem_limit_bytes=40 * 1024 * 1024)


def lane_sums(partial):
    ones = jnp.ones((PAD, LANES), F32)
    return lax.dot_general(
        ones, partial, NT, preferred_element_type=F32, precision=lax.Precision.HIGHEST
    )


def lanes_of(block):
    return pl.ds(pl.multiple_of(block * LANES, LANES), LANES)


def wide_rows(row):
    turned = jnp.concatenate([row, jnp.zeros((PAD - 1, LANES), F32)], 0).T
    return jnp.broadcast_to(turned[:, 0:1], (LANES, LANES))


def sums_kernel(x0, x1, x2, x3, texts, query, out):
    rows = []
    for x in (x0, x1, x2, x3):
        total = jnp.zeros((ROWS, LANES), F32)
        square = jnp.zeros((ROWS, LANES), F32)
        for block in range(BLOCKS):
            value = x[0:ROWS, block * LANES : (block + 1) * LANES].astype(F32)
            total = total + value
            square = square + value * value
        rows.append(lane_sums(total)[0:1])
        rows.append(lane_sums(square)[0:1])
    stats = jnp.concatenate(rows, 0)
    stats = jnp.concatenate([stats, jnp.zeros((PAD, LANES - ROWS), F32)], 1)
    scores = lax.dot_general(
        query[...], texts[:, 0:SLICE], NT, preferred_element_type=F32
    )[0:PAD]
    for peer in range(MP):
        out[peer, :, 0:TEXTS] = scores
        out[peer, :, TEXTS:] = stats


def softmax_kernel(parts, texts, valid, positive, weight, query_grad, pair_grad):
    scores = parts[0, :, 0:TEXTS]
    for peer in range(1, MP):
        scores = scores + parts[peer, :, 0:TEXTS]
    scores = jnp.where(valid[...] > 0.0, scores * SCORE_SCALE, -1e30)
    exp_scores = jnp.exp(scores - jnp.max(scores, axis=1, keepdims=True))
    probs = exp_scores / jnp.sum(exp_scores, axis=1, keepdims=True)
    column = lax.broadcasted_iota(jnp.int32, (PAD, TEXTS), 1)
    hot = jnp.where(column == positive[:, 0:1], 1.0, 0.0)
    grad = weight[:, 0:1] * (probs - hot)
    grad = jnp.concatenate([grad, jnp.zeros((PAD, TEXTS), F32)], 0).astype(BF16)
    pair_grad[...] = grad
    result = jnp.dot(grad, texts[:, 0:SLICE], preferred_element_type=F32) * SCORE_SCALE
    result = result.astype(BF16)
    for peer in range(MP):
        query_grad[peer] = result


def forward_kernel(
    parts, x0, x1, x2, x3, normed_out, gate_out, inv_out, taps_out, natural, mean_rows, inv_rows
):
    stats = parts[0, :, TEXTS:]
    for peer in range(1, MP):
        stats = stats + parts[peer, :, TEXTS:]
    natural[...] = jnp.zeros_like(natural)
    for hop, x in enumerate((x0, x1, x2, x3)):
        mean = stats[2 * hop : 2 * hop + 1] / D
        variance = stats[2 * hop + 1 : 2 * hop + 2] / D - mean * mean
        mean_rows[...] = wide_rows(mean)
        inv_rows[...] = wide_rows(lax.rsqrt(variance + EPSILON))
        for f in range(FRAMES):
            inv_out[hop, f] = inv_rows[pl.ds(f, PAD, stride=FRAMES), :]

        def block_step(block, carry, hop=hop, x=x):
            lanes = lanes_of(block)
            value = x[0:ROWS, lanes].astype(F32)
            natural[0:ROWS, :] = (value - mean_rows[0:ROWS, :]) * inv_rows[0:ROWS, :]
            weights = x[ROWS : ROWS + 16, lanes].astype(F32)
            taps_out[hop, :, lanes] = weights
            taps = [
                jnp.broadcast_to(weights[k : k + 1], (PAD, LANES)) for k in range(KERNEL + 1)
            ]
            hidden = []
            for f in range(FRAMES):
                normed = natural[pl.ds(f, PAD, stride=FRAMES), :]
                normed_out[hop, block, f] = normed
                hidden.append(normed * taps[KERNEL])
            for f in range(FRAMES):
                conv = None
                for k in range(KERNEL):
                    if 0 <= f + k - HALF < FRAMES:
                        term = taps[k] * hidden[f + k - HALF]
                        conv = term if conv is None else conv + term
                gate = jax.nn.sigmoid(conv)
                gate_out[hop, block, f] = gate * (1.0 + conv * (1.0 - gate))
            return carry

        lax.fori_loop(0, BLOCKS, block_step, 0)


def back_block(upstream, block, normed, gate, taps_in, grad_out, tap_out, first, second):
    lanes = lanes_of(block)
    weights = taps_in[0, :, lanes]
    taps = [jnp.broadcast_to(weights[k : k + 1], (PAD, LANES)) for k in range(KERNEL + 1)]
    gain = taps[KERNEL]
    grad_conv = [upstream[f] * gate[0, block, f] for f in range(FRAMES)]
    for f in range(FRAMES):
        conv = None
        for k in range(KERNEL):
            if 0 <= f - k + HALF < FRAMES:
                term = taps[k] * grad_conv[f - k + HALF]
                conv = term if conv is None else conv + term
        conv = conv * gain
        grad_out[block, f] = conv
        first[f] += conv
        second[f] += conv * normed[0, block, f]
    hidden = [normed[0, block, f] * gain for f in range(FRAMES)]
    for k in range(KERNEL):
        total = None
        for f in range(FRAMES):
            if 0 <= f + k - HALF < FRAMES:
                term = grad_conv[f] * hidden[f + k - HALF]
                total = term if total is None else total + term
        tap_out[k : k + 1, lanes] = jnp.sum(total, axis=0, keepdims=True)
    tap_out[KERNEL : KERNEL + 1, lanes] = jnp.zeros((1, LANES), F32)


def write_sums(first, second, sums_out):
    row = lax.broadcasted_iota(jnp.int32, (PAD, LANES), 0)
    sums = jnp.where(
        row == 0,
        lane_sums(first[...].reshape(LANES, LANES)),
        lane_sums(second[...].reshape(LANES, LANES)),
    )
    for peer in range(MP):
        sums_out[peer] = sums


def head_kernel(
    hops, query_grad, weight, normed, gate, taps_in, up_out, grad_out, tap_out, sums_out, first, second
):
    first[...] = jnp.zeros_like(first)
    second[...] = jnp.zeros_like(second)

    def block_step(block, carry):
        rows = weight[pl.ds(pl.multiple_of(block * LANES, LANES), LANES), :]
        pooled = None
        for peer in range(MP):
            term = lax.dot_general(
                query_grad[peer],
                rows[:, peer * SLICE : (peer + 1) * SLICE],
                NT,
                preferred_element_type=F32,
            )
            pooled = term if pooled is None else pooled + term
        head = (pooled[0:PAD] / FRAMES).astype(BF16).astype(F32)
        for f in range(FRAMES):
            up_out[block, f] = head
        back_block(
            [head] * FRAMES, block, normed, gate, taps_in, grad_out, tap_out, first, second
        )
        return carry

    lax.fori_loop(0, BLOCKS, block_step, 0)
    write_sums(first, second, sums_out)


def read_sums(parts, inv, first_rows, second_rows):
    sums = parts[0]
    for peer in range(1, MP):
        sums = sums + parts[peer]
    sums = sums / D
    first_rows[...] = inv[0] * wide_rows(sums[0:1]).reshape(FRAMES, PAD, LANES)
    second_rows[...] = inv[0] * wide_rows(sums[1:2]).reshape(FRAMES, PAD, LANES)


def corrected(block, up, grad, normed, inv, first_rows, second_rows, natural, result):
    values = []
    for f in range(FRAMES):
        value = (
            up[block, f]
            + inv[0, f] * grad[block, f]
            - first_rows[f]
            - normed[0, block, f] * second_rows[f]
        )
        natural[pl.ds(f, PAD, stride=FRAMES), :] = value
        values.append(value)
    result[:, lanes_of(block)] = natural[0:ROWS, :].astype(BF16)
    return values


def step_kernel(
    hops, parts, up, grad, normed_before, inv_before, normed, gate, taps_in,
    result, up_out, grad_out, tap_out, sums_out,
    first, second, first_rows, second_rows, natural,
):
    first[...] = jnp.zeros_like(first)
    second[...] = jnp.zeros_like(second)
    read_sums(parts, inv_before, first_rows, second_rows)

    def block_step(block, carry):
        values = corrected(
            block, up, grad, normed_before, inv_before, first_rows, second_rows, natural, result
        )
        for f in range(FRAMES):
            up_out[block, f] = values[f]
        back_block(values, block, normed, gate, taps_in, grad_out, tap_out, first, second)
        return carry

    lax.fori_loop(0, BLOCKS, block_step, 0)
    write_sums(first, second, sums_out)


def last_kernel(
    hops, parts, up, grad, normed_before, inv_before, result, first_rows, second_rows, natural
):
    read_sums(parts, inv_before, first_rows, second_rows)

    def block_step(block, carry):
        corrected(
            block, up, grad, normed_before, inv_before, first_rows, second_rows, natural, result
        )
        return carry

    lax.fori_loop(0, BLOCKS, block_step, 0)


FRAME_MAJOR = (BLOCKS, FRAMES, PAD, LANES)
ROW_TILE = pltpu.VMEM((FRAMES, PAD, LANES), F32)
NATURAL = pltpu.VMEM((LANES, LANES), F32)


def shape(dims, dtype=F32):
    return jax.ShapeDtypeStruct(dims, dtype)


def cost(flops, moved):
    return pl.CostEstimate(flops=flops, bytes_accessed=moved, transcendentals=0)


def whole(*dims):
    return pl.BlockSpec(dims, lambda i, hops: (0,) * len(dims))


def at_hop(section, *dims):
    return pl.BlockSpec(
        (1,) + dims, lambda i, hops: (hops[section],) + (0,) * len(dims)
    )


def section_call(kernel, hops, operands, in_specs, outs, scratch, name):
    return pl.pallas_call(
        kernel,
        out_shape=outs,
        grid_spec=pltpu.PrefetchScalarGridSpec(
            num_scalar_prefetch=1,
            grid=(1,),
            in_specs=in_specs,
            out_specs=[whole(*out.shape) for out in outs],
            scratch_shapes=scratch,
        ),
        compiler_params=PARAMS,
        name=name,
    )(hops, *operands)


def rotate(value, steps):
    pairs = [(source, (source + steps) % SECTIONS) for source in range(SECTIONS)]
    return lax.ppermute(value, "section", pairs)


def per_device(
    saved_inputs, norm_gains, conv_taps, head_weight, queries, key_embeds, positives, pair_weights
):
    section_now = lax.axis_index("section")
    hops = jnp.stack([(section_now - t) % SECTIONS for t in range(SECTIONS)]).astype(jnp.int32)
    inputs_all = saved_inputs[0]

    small = jnp.concatenate([conv_taps[0], norm_gains.astype(BF16)], 0)
    sections = []
    for steps in range(SECTIONS):
        target = (section_now + steps) % SECTIONS
        block = lax.dynamic_slice_in_dim(inputs_all, OWN * target, OWN, 1)
        block = jnp.concatenate([block.reshape(ROWS, WIDE), small], 0)
        sections.append(rotate(block, steps) if steps else block)

    pairs = jnp.concatenate([key_embeds, queries], -1).reshape(MICRO * SHARD, 2 * SLICE)
    pairs = jnp.broadcast_to(pairs[None], (DP,) + pairs.shape)
    texts = lax.all_to_all(pairs, "dp", 0, 0).reshape(TEXTS, 2 * SLICE)

    own_queries = lax.dynamic_slice_in_dim(queries, OWN * section_now, OWN, 1)
    own_queries = jnp.pad(own_queries.reshape(CLIPS, SLICE), ((0, 16 - CLIPS), (0, 0)))
    own_positives = lax.dynamic_slice_in_dim(positives, OWN * section_now, OWN, 1)
    own_weights = lax.dynamic_slice_in_dim(pair_weights, OWN * section_now, OWN, 1)
    micro = jnp.arange(MICRO, dtype=jnp.int32)[:, None]
    column = (own_positives // SHARD) * (MICRO * SHARD) + micro * SHARD + own_positives % SHARD
    column = jnp.pad(column.reshape(CLIPS), (0, PAD - CLIPS), constant_values=-1)
    column = jnp.broadcast_to(column[:, None], (PAD, LANES))
    own_weights = jnp.pad(own_weights.reshape(CLIPS), (0, PAD - CLIPS))
    own_weights = jnp.broadcast_to(own_weights[:, None], (PAD, LANES))
    text_micro = (jnp.arange(TEXTS) // SHARD) % MICRO
    clip_micro = jnp.minimum(jnp.arange(PAD) // OWN, MICRO - 1)
    valid = (clip_micro[:, None] == text_micro[None, :]).astype(F32)

    parts = pl.pallas_call(
        sums_kernel,
        out_shape=shape((MP, PAD, TEXTS + LANES)),
        in_specs=[VMEM] * 6,
        out_specs=VMEM,
        compiler_params=PARAMS,
        name="row_sums_and_scores",
    )(*sections, texts, own_queries)
    parts = lax.all_to_all(parts, "mp", 0, 0)

    query_grad, pair_grad = pl.pallas_call(
        softmax_kernel,
        out_shape=(shape((MP, 16, SLICE), BF16), shape((16, TEXTS), BF16)),
        in_specs=[VMEM] * 5,
        out_specs=(VMEM, VMEM),
        compiler_params=PARAMS,
        name="softmax_grads",
    )(parts, texts, valid, column, own_weights)
    query_grad = lax.all_to_all(query_grad, "mp", 0, 0)

    normed, gate, inv, taps = pl.pallas_call(
        forward_kernel,
        out_shape=(
            shape((SECTIONS,) + FRAME_MAJOR),
            shape((SECTIONS,) + FRAME_MAJOR),
            shape((SECTIONS, FRAMES, PAD, LANES)),
            shape((SECTIONS, 16, WIDE)),
        ),
        in_specs=[VMEM] * 5,
        out_specs=(VMEM,) * 4,
        scratch_shapes=[NATURAL] * 3,
        compiler_params=PARAMS,
        cost_estimate=cost(10**9, 6 * 10**6),
        name="sections_forward",
    )(parts, *sections)

    outs = [shape(FRAME_MAJOR), shape(FRAME_MAJOR), shape((16, WIDE)), shape((MP, PAD, LANES))]
    now = lambda t: [
        at_hop(t, *FRAME_MAJOR),
        at_hop(t, *FRAME_MAJOR),
        at_hop(t, 16, WIDE),
    ]
    before = lambda t: [
        whole(MP, PAD, LANES),
        whole(*FRAME_MAJOR),
        whole(*FRAME_MAJOR),
        at_hop(t, *FRAME_MAJOR),
        at_hop(t, FRAMES, PAD, LANES),
    ]
    tap_list = [None] * SECTIONS
    result_list = [None] * SECTIONS
    up, grad, tap_list[3], sums = section_call(
        head_kernel,
        hops,
        (query_grad, head_weight, normed, gate, taps),
        [whole(MP, 16, SLICE), whole(WIDE, EMB)] + now(3),
        outs,
        [ROW_TILE] * 2,
        "head_and_section",
    )
    for t in (2, 1, 0):
        sums = lax.all_to_all(sums, "mp", 0, 0)
        result_list[t + 1], up, grad, tap_list[t], sums = section_call(
            step_kernel,
            hops,
            (sums, up, grad, normed, inv, normed, gate, taps),
            before(t + 1) + now(t),
            [shape((ROWS, WIDE), BF16)] + outs,
            [ROW_TILE] * 4 + [NATURAL],
            "section_step",
        )

    tap_parts = jnp.stack(tap_list).astype(BF16).reshape(SECTIONS, DP, 5, LANES)
    tap_parts = tap_parts.transpose(1, 0, 2, 3)
    pair_parts = pair_grad[0:CLIPS].reshape(CLIPS, DP, MICRO * SHARD).transpose(1, 0, 2)
    pair_parts = jnp.pad(pair_parts.reshape(DP, -1), ((0, 0), (0, 2 * LANES - CLIPS * MICRO * SHARD)))
    pair_parts = jnp.broadcast_to(
        pair_parts.reshape(DP, 1, 2, LANES), (DP, SECTIONS, 2, LANES)
    )
    message = jnp.concatenate([tap_parts, pair_parts], 2).reshape(DP * SECTIONS, 7, LANES)
    message = jnp.pad(message, ((0, 0), (0, 1), (0, 0)))
    message = lax.all_to_all(message, ("dp", "section"), 0, 0)

    own = sums[0]
    shifted = [own]
    for steps in range(1, MP):
        shifted.append(
            lax.ppermute(own, "mp", [(source, (source + steps) % MP) for source in range(MP)])
        )
    sums = jnp.stack(shifted)
    (result_list[0],) = section_call(
        last_kernel,
        hops,
        (sums, up, grad, normed, inv),
        before(0),
        [shape((ROWS, WIDE), BF16)],
        [ROW_TILE] * 2 + [NATURAL],
        "section_end",
    )

    tap_sum = jnp.sum(message[:, 0:5].astype(F32), axis=0).astype(BF16)
    tap_grads = lax.all_to_all(jnp.broadcast_to(tap_sum[None], (DP, 5, LANES)), "dp", 0, 0)
    tap_grads = tap_grads.reshape(16, WIDE)[0:KERNEL].astype(F32)

    columns = message[:, 5:7].reshape(DP, SECTIONS, 2 * LANES)[..., : CLIPS * MICRO * SHARD]
    columns = columns.reshape(DP, SECTIONS, MICRO, OWN, MICRO * SHARD)
    columns = columns.transpose(0, 2, 1, 3, 4).reshape(TEXTS, MICRO * SHARD)
    key_grads = (
        lax.dot_general(
            columns, texts[:, SLICE:], (((0,), (0,)), ((), ())), preferred_element_type=F32
        )
        * SCORE_SCALE
    ).reshape(MICRO, SHARD, SLICE)

    stacked = jnp.stack(result_list)
    results = jnp.zeros(inputs_all.shape, BF16)
    for steps in range(SECTIONS):
        target = (section_now + steps) % SECTIONS
        source = (section_now - steps) % SECTIONS
        block = lax.dynamic_index_in_dim(stacked, target, 0, keepdims=False)
        block = rotate(block, steps) if steps else block
        block = block.reshape(MICRO, OWN, FRAMES, WIDE)
        results = lax.dynamic_update_slice_in_dim(results, block, OWN * source, 1)
    return (results[None], tap_grads[None], key_grads)


def solution(mesh):
    return jax.shard_map(
        per_device,
        mesh=mesh,
        in_specs=(
            P("section", None, "dp", None, "mp"),
            P("section", "mp"),
            P("section", None, "mp"),
            P("mp", None),
            P(None, "dp", "mp"),
            P(None, "dp", "mp"),
            P(None, "dp"),
            P(None, "dp"),
        ),
        out_specs=(
            P("section", None, "dp", None, "mp"),
            P("section", None, "mp"),
            P(None, "dp", "mp"),
        ),
        check_vma=False,
    )
```

```python
import jax
import jax.numpy as jnp
from jax import lax
from jax.experimental import pallas as pl
from jax.experimental.pallas import tpu as pltpu
from jax.sharding import PartitionSpec as P

D = 5120
EMB = 1024
FRAMES = 16
KERNEL = 15
HALF = KERNEL // 2
SECTIONS = 4
MP = 4
DP = 32
MICRO = 2
SHARD = 12
OWN = SHARD // SECTIONS
CLIPS = MICRO * OWN
ROWS = CLIPS * FRAMES
TEXTS = DP * MICRO * SHARD
WIDE = D // MP
SLICE = EMB // MP
LANES = 128
BLOCKS = WIDE // LANES
PAD = 8
SCORE_SCALE = 1.0 / 32.0
EPSILON = 1e-05
F32 = jnp.float32
BF16 = jnp.bfloat16

NT = (((1,), (1,)), ((), ()))
VMEM = pl.BlockSpec(memory_space=pltpu.VMEM)
PARAMS = pltpu.CompilerParams(vmem_limit_bytes=24 * 1024 * 1024)


def lane_sums(partial):
    ones = jnp.ones((PAD, LANES), F32)
    return lax.dot_general(
        ones, partial, NT, preferred_element_type=F32, precision=lax.Precision.HIGHEST
    )


def lanes_of(block):
    return pl.ds(pl.multiple_of(block * LANES, LANES), LANES)


def wide_rows(row):
    turned = jnp.concatenate([row, jnp.zeros((PAD - 1, LANES), F32)], 0).T
    return jnp.broadcast_to(turned[:, 0:1], (LANES, LANES))


def sums_kernel(x0, x1, x2, x3, texts, query, out):
    rows = []
    for x in (x0, x1, x2, x3):
        total = jnp.zeros((ROWS, LANES), F32)
        square = jnp.zeros((ROWS, LANES), F32)
        for block in range(BLOCKS):
            value = x[0:ROWS, block * LANES : (block + 1) * LANES].astype(F32)
            total = total + value
            square = square + value * value
        rows.append(lane_sums(total)[0:1])
        rows.append(lane_sums(square)[0:1])
    stats = jnp.concatenate(rows, 0)
    stats = jnp.concatenate([stats, jnp.zeros((PAD, LANES - ROWS), F32)], 1)
    scores = lax.dot_general(
        query[...], texts[:, 0:SLICE], NT, preferred_element_type=F32
    )[0:PAD]
    for peer in range(MP):
        out[peer, :, 0:TEXTS] = scores
        out[peer, :, TEXTS:] = stats


def softmax_kernel(parts, texts, valid, positive, weight, query_grad, pair_grad):
    scores = parts[0, :, 0:TEXTS]
    for peer in range(1, MP):
        scores = scores + parts[peer, :, 0:TEXTS]
    scores = jnp.where(valid[...] > 0.0, scores * SCORE_SCALE, -1e30)
    exp_scores = jnp.exp(scores - jnp.max(scores, axis=1, keepdims=True))
    probs = exp_scores / jnp.sum(exp_scores, axis=1, keepdims=True)
    column = lax.broadcasted_iota(jnp.int32, (PAD, TEXTS), 1)
    hot = jnp.where(column == positive[:, 0:1], 1.0, 0.0)
    grad = weight[:, 0:1] * (probs - hot)
    grad = jnp.concatenate([grad, jnp.zeros((PAD, TEXTS), F32)], 0).astype(BF16)
    pair_grad[...] = grad
    result = jnp.dot(grad, texts[:, 0:SLICE], preferred_element_type=F32) * SCORE_SCALE
    result = result.astype(BF16)
    for peer in range(MP):
        query_grad[peer] = result


def spread(row, rows_out, natural):
    natural[...] = wide_rows(row)
    for f in range(FRAMES):
        rows_out[f] = natural[pl.ds(f, PAD, stride=FRAMES), :]


def forward_kernel(
    parts, x0, x1, x2, x3,
    normed_out, gate_out, inv_out, inv_row_out, taps_out,
    natural, mean_rows, inv_rows,
):
    stats = parts[0, :, TEXTS:]
    for peer in range(1, MP):
        stats = stats + parts[peer, :, TEXTS:]
    natural[...] = jnp.zeros_like(natural)
    for hop, x in enumerate((x0, x1, x2, x3)):
        mean = stats[2 * hop : 2 * hop + 1] / D
        variance = stats[2 * hop + 1 : 2 * hop + 2] / D - mean * mean
        inv = lax.rsqrt(variance + EPSILON)
        inv_row_out[hop : hop + 1, :] = inv
        mean_rows[...] = wide_rows(mean)
        inv_rows[...] = wide_rows(inv)
        for f in range(FRAMES):
            inv_out[hop, f] = inv_rows[pl.ds(f, PAD, stride=FRAMES), :]

        def block_step(block, carry, hop=hop, x=x):
            lanes = lanes_of(block)
            value = x[0:ROWS, lanes].astype(F32)
            natural[0:ROWS, :] = (value - mean_rows[0:ROWS, :]) * inv_rows[0:ROWS, :]
            weights = x[ROWS : ROWS + 16, lanes].astype(F32)
            taps_out[hop, :, lanes] = weights
            taps = [
                jnp.broadcast_to(weights[k : k + 1], (PAD, LANES)) for k in range(KERNEL + 1)
            ]
            hidden = []
            for f in range(FRAMES):
                normed = natural[pl.ds(f, PAD, stride=FRAMES), :]
                normed_out[hop, block, f] = normed
                hidden.append(normed * taps[KERNEL])
            for f in range(FRAMES):
                conv = None
                for k in range(KERNEL):
                    if 0 <= f + k - HALF < FRAMES:
                        term = taps[k] * hidden[f + k - HALF]
                        conv = term if conv is None else conv + term
                gate = jax.nn.sigmoid(conv)
                gate_out[hop, block, f] = gate * (1.0 + conv * (1.0 - gate))
            return carry

        lax.fori_loop(0, BLOCKS, block_step, 0)


def pair_kernel(
    hops, normed, gate, taps_in, out, normed_rows, gate_rows, both_rows, left, right, plain
):
    frame = lax.broadcasted_iota(jnp.int32, (FRAMES, 2 * LANES), 0)
    lane = lax.broadcasted_iota(jnp.int32, (FRAMES, 2 * LANES), 1)
    lane_frame = lane & (FRAMES - 1)
    lane_clip = (lane & (LANES - 1)) >> 4
    for pair, section in enumerate((2, 0)):
        here = hops[section]
        above = hops[section + 1]

        def block_step(block, carry, here=here, above=above):
            lanes = lanes_of(block)
            weights = taps_in[here, :, lanes]
            weights = weights * weights[KERNEL : KERNEL + 1]
            plain[:, lanes] = weights.astype(BF16)
            for f in range(FRAMES):
                rows = pl.ds(f, PAD, stride=FRAMES)
                value = gate[here, block, f]
                normed_rows[rows, :] = normed[here, block, f]
                gate_rows[rows, :] = value
                both_rows[rows, :] = value * normed[above, block, f]
            right[0:LANES, lanes] = gate_rows[...].astype(BF16)
            right[LANES : 2 * LANES, lanes] = both_rows[...].astype(BF16)
            for c in range(CLIPS):
                value = normed_rows[c * FRAMES : (c + 1) * FRAMES, :]
                for k in range(KERNEL):
                    start = (c * KERNEL + k) * FRAMES
                    left[start : start + FRAMES, lanes] = (value * weights[k : k + 1]).astype(
                        BF16
                    )
            return carry

        lax.fori_loop(0, BLOCKS, block_step, 0)
        columns = right[...]
        sums = lax.dot_general(plain[...], columns, NT, preferred_element_type=F32)
        first = jnp.zeros((FRAMES, 2 * LANES), F32)
        second = jnp.zeros((FRAMES, 2 * LANES), F32)
        for k in range(KERNEL):
            first = first + jnp.where(lane_frame == frame - k + HALF, sums[k : k + 1], 0.0)
        for c in range(CLIPS):
            start = c * KERNEL * FRAMES
            sums = lax.dot_general(
                left[start : start + KERNEL * FRAMES, :], columns, NT, preferred_element_type=F32
            )
            total = jnp.zeros((FRAMES, 2 * LANES), F32)
            for k in range(KERNEL):
                total = total + jnp.where(
                    lane_frame == frame - k + HALF, sums[k * FRAMES : (k + 1) * FRAMES], 0.0
                )
            second = second + jnp.where(lane_clip == c, total, 0.0)
        out[pair, 0:16, :] = first[:, 0:LANES]
        out[pair, 16:32, :] = second[:, 0:LANES]
        out[pair, 32:48, :] = first[:, LANES:]
        out[pair, 48:64, :] = second[:, LANES:]


def tap_rows(taps_in, hop, block):
    weights = taps_in[hop, :, lanes_of(block)]
    return [jnp.broadcast_to(weights[k : k + 1], (PAD, LANES)) for k in range(KERNEL + 1)]


def conv_back(grad_conv, taps):
    out = []
    for f in range(FRAMES):
        conv = None
        for k in range(KERNEL):
            if 0 <= f - k + HALF < FRAMES:
                term = taps[k] * grad_conv[f - k + HALF]
                conv = term if conv is None else conv + term
        out.append(conv * taps[KERNEL])
    return out


def add_taps(grad_conv, normed, hop, block, taps, tap_out):
    hidden = [normed[hop, block, f] * taps[KERNEL] for f in range(FRAMES)]
    for k in range(KERNEL):
        total = None
        for f in range(FRAMES):
            if 0 <= f + k - HALF < FRAMES:
                term = grad_conv[f] * hidden[f + k - HALF]
                total = term if total is None else total + term
        tap_out[k : k + 1, lanes_of(block)] = jnp.sum(total, axis=0, keepdims=True)


def add_sums(grads, normed, hop, block, first, second):
    for f in range(FRAMES):
        first[f] += grads[f]
        second[f] += grads[f] * normed[hop, block, f]


def write_sums(sums, matrices, out, natural):
    row = lax.broadcasted_iota(jnp.int32, (PAD, LANES), 0)
    packed = jnp.zeros((PAD, LANES), F32)
    for index, total in enumerate(sums):
        for f in range(FRAMES):
            natural[pl.ds(f, PAD, stride=FRAMES), :] = total[f]
        packed = jnp.where(row == index, lane_sums(natural[...]), packed)
    for peer in range(MP):
        out[peer, 0:PAD, :] = packed
        out[peer, PAD:, :] = matrices


def read_sums(parts, inv_row, above, here, natural, above_first, above_second, here_first, here_second):
    total = parts[0]
    for peer in range(1, MP):
        total = total + parts[peer]
    scale = inv_row[pl.ds(above, 1), :] / D
    first = total[0:1] * scale
    second = total[1:2] * scale
    matrix = total[PAD:]
    products = matrix[0:32] * first + matrix[32:64] * second
    row = lax.broadcasted_iota(jnp.int32, (LANES, LANES), 0)
    column = lax.broadcasted_iota(jnp.int32, (LANES, LANES), 1)
    same = jnp.where((row >> 4) == (column >> 4), 1.0, 0.0)
    products = jnp.dot(
        products, same, preferred_element_type=F32, precision=lax.Precision.HIGHEST
    )
    keep = (row & (FRAMES - 1)) == (column & (FRAMES - 1))
    keep = keep[0:FRAMES]
    change_first = jnp.sum(jnp.where(keep, products[0:16], 0.0), axis=0, keepdims=True)
    change_second = jnp.sum(jnp.where(keep, products[16:32], 0.0), axis=0, keepdims=True)
    spread(first, above_first, natural)
    spread(second, above_second, natural)
    scale = inv_row[pl.ds(here, 1), :] / D
    spread((total[2:3] - change_first) * scale, here_first, natural)
    spread((total[3:4] - change_second) * scale, here_second, natural)


def write_result(values, natural, result, index, block):
    for f in range(FRAMES):
        natural[pl.ds(f, PAD, stride=FRAMES), :] = values[f]
    result[index, :, lanes_of(block)] = natural[0:ROWS, :].astype(BF16)


def head_kernel(
    hops, query_grad, weight, normed, gate, inv, taps_in, matrices,
    up_out, tap_out, sums_out,
    s0, s1, s2, s3, natural,
):
    for total in (s0, s1, s2, s3):
        total[...] = jnp.zeros_like(total)
    three, two = hops[3], hops[2]

    def block_step(block, carry):
        rows = weight[pl.ds(pl.multiple_of(block * LANES, LANES), LANES), :]
        pooled = None
        for peer in range(MP):
            term = lax.dot_general(
                query_grad[peer],
                rows[:, peer * SLICE : (peer + 1) * SLICE],
                NT,
                preferred_element_type=F32,
            )
            pooled = term if pooled is None else pooled + term
        head = (pooled[0:PAD] / FRAMES).astype(BF16).astype(F32)
        taps = tap_rows(taps_in, three, block)
        grad_conv = [head * gate[three, block, f] for f in range(FRAMES)]
        grads = conv_back(grad_conv, taps)
        add_taps(grad_conv, normed, three, block, taps, tap_out)
        add_sums(grads, normed, three, block, s0, s1)
        ups = [head + inv[three, f] * grads[f] for f in range(FRAMES)]
        for f in range(FRAMES):
            up_out[block, f] = ups[f]
        grads = conv_back(
            [ups[f] * gate[two, block, f] for f in range(FRAMES)], tap_rows(taps_in, two, block)
        )
        add_sums(grads, normed, two, block, s2, s3)
        return carry

    lax.fori_loop(0, BLOCKS, block_step, 0)
    write_sums((s0, s1, s2, s3), matrices[0], sums_out, natural)


def corrected(up, normed, hop, block, first_rows, second_rows):
    return [
        up[f] - first_rows[f] - normed[hop, block, f] * second_rows[f] for f in range(FRAMES)
    ]


def middle_kernel(
    hops, parts, up, normed, gate, inv, inv_row, taps_in, matrices,
    result, up_out, tap_two, tap_one, sums_out,
    s0, s1, s2, s3, a0, a1, b0, b1, natural,
):
    for total in (s0, s1, s2, s3):
        total[...] = jnp.zeros_like(total)
    three, two, one, zero = hops[3], hops[2], hops[1], hops[0]
    read_sums(parts, inv_row, three, two, natural, a0, a1, b0, b1)

    def block_step(block, carry):
        ups = corrected([up[block, f] for f in range(FRAMES)], normed, three, block, a0, a1)
        write_result(ups, natural, result, 0, block)
        taps = tap_rows(taps_in, two, block)
        grad_conv = [ups[f] * gate[two, block, f] for f in range(FRAMES)]
        grads = conv_back(grad_conv, taps)
        add_taps(grad_conv, normed, two, block, taps, tap_two)
        ups = [ups[f] + inv[two, f] * grads[f] for f in range(FRAMES)]
        ups = corrected(ups, normed, two, block, b0, b1)
        write_result(ups, natural, result, 1, block)
        taps = tap_rows(taps_in, one, block)
        grad_conv = [ups[f] * gate[one, block, f] for f in range(FRAMES)]
        grads = conv_back(grad_conv, taps)
        add_taps(grad_conv, normed, one, block, taps, tap_one)
        add_sums(grads, normed, one, block, s0, s1)
        ups = [ups[f] + inv[one, f] * grads[f] for f in range(FRAMES)]
        for f in range(FRAMES):
            up_out[block, f] = ups[f]
        grads = conv_back(
            [ups[f] * gate[zero, block, f] for f in range(FRAMES)],
            tap_rows(taps_in, zero, block),
        )
        add_sums(grads, normed, zero, block, s2, s3)
        return carry

    lax.fori_loop(0, BLOCKS, block_step, 0)
    write_sums((s0, s1, s2, s3), matrices[1], sums_out, natural)


def end_kernel(
    hops, parts, up, normed, gate, inv, inv_row, taps_in,
    before, tap_three, tap_two, tap_one, pair_parts,
    result, message,
    a0, a1, b0, b1, natural, tap_zero, wide,
):
    three, two, one, zero = hops[3], hops[2], hops[1], hops[0]
    slots = [(SECTIONS - hop) & (SECTIONS - 1) for hop in (zero, one, two, three)]
    read_sums(parts, inv_row, one, zero, natural, a0, a1, b0, b1)
    result[slots[3]] = before[0]
    result[slots[2]] = before[1]

    def block_step(block, carry):
        ups = corrected([up[block, f] for f in range(FRAMES)], normed, one, block, a0, a1)
        write_result(ups, natural, result, slots[1], block)
        taps = tap_rows(taps_in, zero, block)
        grad_conv = [ups[f] * gate[zero, block, f] for f in range(FRAMES)]
        grads = conv_back(grad_conv, taps)
        add_taps(grad_conv, normed, zero, block, taps, tap_zero)
        ups = [ups[f] + inv[zero, f] * grads[f] for f in range(FRAMES)]
        ups = corrected(ups, normed, zero, block, b0, b1)
        write_result(ups, natural, result, slots[0], block)
        return carry

    lax.fori_loop(0, BLOCKS, block_step, 0)

    wide[...] = jnp.zeros_like(wide)
    for target in range(DP):
        for section, source in enumerate((tap_zero, tap_one, tap_two, tap_three)):
            row = target // 2
            if row < KERNEL:
                for piece in range(5):
                    start = ((target % 2) * 5 + piece) * LANES
                    wide[target * SECTIONS + section, piece : piece + 1, :] = source[
                        row : row + 1, start : start + LANES
                    ]
            wide[target * SECTIONS + section, 5:7, :] = pair_parts[target]
    half = DP * SECTIONS // 2
    message[...] = wide[...].reshape(2 * half * PAD, LANES).astype(BF16)


FRAME_MAJOR = (BLOCKS, FRAMES, PAD, LANES)
ROW_TILE = pltpu.VMEM((FRAMES, PAD, LANES), F32)
NATURAL = pltpu.VMEM((LANES, LANES), F32)
MATRIX_ROWS = 64
SMEM = pl.BlockSpec(memory_space=pltpu.SMEM)


def shape(dims, dtype=F32):
    return jax.ShapeDtypeStruct(dims, dtype)


def cost(flops, moved):
    return pl.CostEstimate(flops=flops, bytes_accessed=moved, transcendentals=0)


def local_call(kernel, hops, operands, outs, scratch, name, estimate=None):
    return pl.pallas_call(
        kernel,
        out_shape=outs,
        in_specs=[SMEM] + [VMEM] * len(operands),
        out_specs=[VMEM] * len(outs),
        scratch_shapes=scratch,
        compiler_params=PARAMS,
        cost_estimate=estimate,
        name=name,
    )(hops, *operands)


def rotate(value, steps):
    pairs = [(source, (source + steps) % SECTIONS) for source in range(SECTIONS)]
    return lax.ppermute(value, "section", pairs)


def per_device(
    saved_inputs, norm_gains, conv_taps, head_weight, queries, key_embeds, positives, pair_weights
):
    section_now = lax.axis_index("section")
    hops = jnp.stack([(section_now - t) % SECTIONS for t in range(SECTIONS)]).astype(jnp.int32)
    inputs_all = saved_inputs[0]

    small = jnp.concatenate([conv_taps[0], norm_gains.astype(BF16)], 0)
    sections = []
    for steps in range(SECTIONS):
        target = (section_now + steps) % SECTIONS
        block = lax.dynamic_slice_in_dim(inputs_all, OWN * target, OWN, 1)
        block = jnp.concatenate([block.reshape(ROWS, WIDE), small], 0)
        sections.append(rotate(block, steps) if steps else block)

    pairs = jnp.concatenate([key_embeds, queries], -1).reshape(MICRO * SHARD, 2 * SLICE)
    pairs = jnp.broadcast_to(pairs[None], (DP,) + pairs.shape)
    texts = lax.all_to_all(pairs, "dp", 0, 0).reshape(TEXTS, 2 * SLICE)

    own_queries = lax.dynamic_slice_in_dim(queries, OWN * section_now, OWN, 1)
    own_queries = jnp.pad(own_queries.reshape(CLIPS, SLICE), ((0, 16 - CLIPS), (0, 0)))
    own_positives = lax.dynamic_slice_in_dim(positives, OWN * section_now, OWN, 1)
    own_weights = lax.dynamic_slice_in_dim(pair_weights, OWN * section_now, OWN, 1)
    micro = jnp.arange(MICRO, dtype=jnp.int32)[:, None]
    column = (own_positives // SHARD) * (MICRO * SHARD) + micro * SHARD + own_positives % SHARD
    column = jnp.pad(column.reshape(CLIPS), (0, PAD - CLIPS), constant_values=-1)
    column = jnp.broadcast_to(column[:, None], (PAD, LANES))
    own_weights = jnp.pad(own_weights.reshape(CLIPS), (0, PAD - CLIPS))
    own_weights = jnp.broadcast_to(own_weights[:, None], (PAD, LANES))
    text_micro = (jnp.arange(TEXTS) // SHARD) % MICRO
    clip_micro = jnp.minimum(jnp.arange(PAD) // OWN, MICRO - 1)
    valid = (clip_micro[:, None] == text_micro[None, :]).astype(F32)

    parts = pl.pallas_call(
        sums_kernel,
        out_shape=shape((MP, PAD, TEXTS + LANES)),
        in_specs=[VMEM] * 6,
        out_specs=VMEM,
        compiler_params=PARAMS,
        name="row_sums_and_scores",
    )(*sections, texts, own_queries)
    parts = lax.all_to_all(parts, "mp", 0, 0)

    query_grad, pair_grad = pl.pallas_call(
        softmax_kernel,
        out_shape=(shape((MP, 16, SLICE), BF16), shape((16, TEXTS), BF16)),
        in_specs=[VMEM] * 5,
        out_specs=(VMEM, VMEM),
        compiler_params=PARAMS,
        name="softmax_grads",
    )(parts, texts, valid, column, own_weights)
    query_grad = lax.all_to_all(query_grad, "mp", 0, 0)

    normed, gate, inv, inv_row, taps = pl.pallas_call(
        forward_kernel,
        out_shape=(
            shape((SECTIONS,) + FRAME_MAJOR),
            shape((SECTIONS,) + FRAME_MAJOR),
            shape((SECTIONS, FRAMES, PAD, LANES)),
            shape((PAD, LANES)),
            shape((SECTIONS, 16, WIDE)),
        ),
        in_specs=[VMEM] * 5,
        out_specs=(VMEM,) * 5,
        scratch_shapes=[NATURAL] * 3,
        compiler_params=PARAMS,
        cost_estimate=cost(10**9, 6 * 10**6),
        name="sections_forward",
    )(parts, *sections)
    (matrices,) = local_call(
        pair_kernel,
        hops,
        (normed, gate, taps),
        [shape((2, MATRIX_ROWS, LANES))],
        [NATURAL] * 3
        + [
            pltpu.VMEM((CLIPS * KERNEL * FRAMES, WIDE), BF16),
            pltpu.VMEM((2 * LANES, WIDE), BF16),
            pltpu.VMEM((16, WIDE), BF16),
        ],
        "pair_matrices",
        cost(3 * 10**9, 6 * 10**6),
    )

    sums_shape = shape((MP, PAD + MATRIX_ROWS, LANES))
    tap_shape = shape((16, WIDE))
    up, tap_three, sums = local_call(
        head_kernel,
        hops,
        (query_grad, head_weight, normed, gate, inv, taps, matrices),
        [shape(FRAME_MAJOR), tap_shape, sums_shape],
        [ROW_TILE] * 4 + [NATURAL],
        "head_and_sections",
    )
    sums = lax.all_to_all(sums, "mp", 0, 0)
    before, up, tap_two, tap_one, sums = local_call(
        middle_kernel,
        hops,
        (sums, up, normed, gate, inv, inv_row, taps, matrices),
        [shape((2, ROWS, WIDE), BF16), shape(FRAME_MAJOR), tap_shape, tap_shape, sums_shape],
        [ROW_TILE] * 8 + [NATURAL],
        "middle_sections",
    )
    sums = lax.all_to_all(sums, "mp", 0, 0)

    pair_parts = pair_grad[0:CLIPS].astype(F32).reshape(CLIPS, DP, MICRO * SHARD)
    pair_parts = pair_parts.transpose(1, 0, 2).reshape(DP, -1)
    pair_parts = jnp.pad(pair_parts, ((0, 0), (0, 2 * LANES - CLIPS * MICRO * SHARD)))
    pair_parts = pair_parts.reshape(DP, 2, LANES)
    results_out, message = local_call(
        end_kernel,
        hops,
        (sums, up, normed, gate, inv, inv_row, taps, before, tap_three, tap_two, tap_one, pair_parts),
        [shape((SECTIONS, ROWS, WIDE), BF16), shape((DP * SECTIONS * PAD, LANES), BF16)],
        [ROW_TILE] * 4
        + [NATURAL, pltpu.VMEM((16, WIDE), F32), pltpu.VMEM((DP * SECTIONS, PAD, LANES), F32)],
        "end_sections",
    )
    message = lax.all_to_all(
        message.reshape(DP * SECTIONS, PAD, LANES), ("dp", "section"), 0, 0
    )

    tap_sum = jnp.sum(message[:, 0:5].astype(F32), axis=0).astype(BF16)
    tap_grads = lax.all_to_all(jnp.broadcast_to(tap_sum[None], (DP, 5, LANES)), "dp", 0, 0)
    tap_grads = tap_grads.reshape(16, WIDE)[0:KERNEL].astype(F32)

    columns = message[:, 5:7].reshape(DP, SECTIONS, 2 * LANES)[..., : CLIPS * MICRO * SHARD]
    columns = columns.reshape(DP, SECTIONS, MICRO, OWN, MICRO * SHARD)
    columns = columns.transpose(0, 2, 1, 3, 4).reshape(TEXTS, MICRO * SHARD)
    key_grads = (
        lax.dot_general(
            columns, texts[:, SLICE:], (((0,), (0,)), ((), ())), preferred_element_type=F32
        )
        * SCORE_SCALE
    ).reshape(MICRO, SHARD, SLICE)

    results = jnp.zeros(inputs_all.shape, BF16)
    for steps in range(SECTIONS):
        source = (section_now - steps) % SECTIONS
        block = results_out[steps]
        block = rotate(block, steps) if steps else block
        block = block.reshape(MICRO, OWN, FRAMES, WIDE)
        results = lax.dynamic_update_slice_in_dim(results, block, OWN * source, 1)
    return (results[None], tap_grads[None], key_grads)


def solution(mesh):
    return jax.shard_map(
        per_device,
        mesh=mesh,
        in_specs=(
            P("section", None, "dp", None, "mp"),
            P("section", "mp"),
            P("section", None, "mp"),
            P("mp", None),
            P(None, "dp", "mp"),
            P(None, "dp", "mp"),
            P(None, "dp"),
            P(None, "dp"),
        ),
        out_specs=(
            P("section", None, "dp", None, "mp"),
            P("section", None, "mp"),
            P(None, "dp", "mp"),
        ),
        check_vma=False,
    )
```

```python
import jax
import jax.numpy as jnp
from jax import lax
from jax.experimental import pallas as pl
from jax.experimental.pallas import tpu as pltpu
from jax.sharding import PartitionSpec as P

D = 5120
EMB = 1024
FRAMES = 16
KERNEL = 15
HALF = KERNEL // 2
SECTIONS = 4
MP = 4
DP = 32
MICRO = 2
SHARD = 12
OWN = SHARD // SECTIONS
CLIPS = MICRO * OWN
ROWS = CLIPS * FRAMES
TEXTS = DP * MICRO * SHARD
WIDE = D // MP
SLICE = EMB // MP
LANES = 128
BLOCKS = WIDE // LANES
PAD = 8
SCORE_SCALE = 1.0 / 32.0
EPSILON = 1e-05
F32 = jnp.float32
BF16 = jnp.bfloat16

NT = (((1,), (1,)), ((), ()))
VMEM = pl.BlockSpec(memory_space=pltpu.VMEM)
PARAMS = pltpu.CompilerParams(vmem_limit_bytes=24 * 1024 * 1024)


def lane_sums(partial):
    ones = jnp.ones((PAD, LANES), F32)
    return lax.dot_general(
        ones, partial, NT, preferred_element_type=F32, precision=lax.Precision.HIGHEST
    )


def lanes_of(block):
    return pl.ds(pl.multiple_of(block * LANES, LANES), LANES)


def wide_rows(row):
    turned = jnp.concatenate([row, jnp.zeros((PAD - 1, LANES), F32)], 0).T
    return jnp.broadcast_to(turned[:, 0:1], (LANES, LANES))


def sums_kernel(hops, positives, weights, x0, x1, x2, x3, texts, query, out):
    rows = []
    for x in (x0, x1, x2, x3):
        total = jnp.zeros((ROWS, LANES), F32)
        square = jnp.zeros((ROWS, LANES), F32)
        for block in range(BLOCKS):
            value = x[0:ROWS, block * LANES : (block + 1) * LANES].astype(F32)
            total = total + value
            square = square + value * value
        rows.append(lane_sums(total)[0:1])
        rows.append(lane_sums(square)[0:1])
    stats = jnp.concatenate(rows, 0)
    stats = jnp.concatenate([stats, jnp.zeros((PAD, LANES - ROWS), F32)], 1)
    scores = lax.dot_general(
        query[...], texts[:, 0:SLICE], NT, preferred_element_type=F32
    )[0:PAD]
    for peer in range(MP):
        out[peer, :, 0:TEXTS] = scores
        out[peer, :, TEXTS:] = stats


def softmax_kernel(
    hops, positives, weights, parts, texts, query_grad, pair_parts
):
    scores = parts[0, :, 0:TEXTS]
    for peer in range(1, MP):
        scores = scores + parts[peer, :, 0:TEXTS]
    row = lax.broadcasted_iota(jnp.int32, (PAD, TEXTS), 0)
    column = lax.broadcasted_iota(jnp.int32, (PAD, TEXTS), 1)
    text_micro = ((column * 10923) >> 17) & 1
    clip_micro = jnp.where(row >= OWN, 1, 0)
    scores = jnp.where(text_micro == clip_micro, scores * SCORE_SCALE, -1e30)
    exp_scores = jnp.exp(scores - jnp.max(scores, axis=1, keepdims=True))
    probs = exp_scores / jnp.sum(exp_scores, axis=1, keepdims=True)
    base = hops[SECTIONS] * OWN
    positive = jnp.full((PAD, TEXTS), -1, jnp.int32)
    weight = jnp.zeros((PAD, TEXTS), F32)
    for micro in range(MICRO):
        for own in range(OWN):
            index = positives[micro, base + own]
            owner = (index * 10923) >> 17
            index = owner * (MICRO * SHARD) + micro * SHARD + (index - owner * SHARD)
            here = row == micro * OWN + own
            positive = jnp.where(here, index, positive)
            weight = jnp.where(here, weights[micro, base + own], weight)
    hot = jnp.where(column == positive, 1.0, 0.0)
    grad = weight * (probs - hot)
    grad = jnp.concatenate([grad, jnp.zeros((PAD, TEXTS), F32)], 0).astype(BF16)
    result = jnp.dot(grad, texts[:, 0:SLICE], preferred_element_type=F32) * SCORE_SCALE
    result = result.astype(BF16)
    for peer in range(MP):
        query_grad[peer] = result
    grad = grad.astype(F32)
    gap = jnp.zeros((1, 32 - MICRO * SHARD), F32)
    tail = jnp.zeros((1, LANES - OWN * 32), F32)
    for target in range(DP):
        start = target * MICRO * SHARD
        for micro in range(MICRO):
            pieces = []
            for own in range(OWN):
                clip = micro * OWN + own
                pieces += [grad[clip : clip + 1, start : start + MICRO * SHARD], gap]
            pair_parts[target, micro : micro + 1, :] = jnp.concatenate(pieces + [tail], 1)


def spread(row, rows_out, natural):
    natural[...] = wide_rows(row)
    for f in range(FRAMES):
        rows_out[f] = natural[pl.ds(f, PAD, stride=FRAMES), :]


def forward_kernel(
    query_grad, parts, x0, x1, x2, x3,
    normed_out, gate_out, inv_out, inv_row_out, taps_out,
    natural, mean_rows, inv_rows,
):
    stats = parts[0, :, TEXTS:]
    for peer in range(1, MP):
        stats = stats + parts[peer, :, TEXTS:]
    natural[...] = jnp.zeros_like(natural)
    for hop, x in enumerate((x0, x1, x2, x3)):
        mean = stats[2 * hop : 2 * hop + 1] / D
        variance = stats[2 * hop + 1 : 2 * hop + 2] / D - mean * mean
        inv = lax.rsqrt(variance + EPSILON)
        inv_row_out[hop : hop + 1, :] = inv
        mean_rows[...] = wide_rows(mean)
        inv_rows[...] = wide_rows(inv)
        for f in range(FRAMES):
            inv_out[hop, f] = inv_rows[pl.ds(f, PAD, stride=FRAMES), :]

        def block_step(block, carry, hop=hop, x=x):
            lanes = lanes_of(block)
            value = x[0:ROWS, lanes].astype(F32)
            natural[0:ROWS, :] = (value - mean_rows[0:ROWS, :]) * inv_rows[0:ROWS, :]
            weights = x[ROWS : ROWS + 16, lanes].astype(F32)
            taps_out[hop, :, lanes] = weights
            taps = [
                jnp.broadcast_to(weights[k : k + 1], (PAD, LANES)) for k in range(KERNEL + 1)
            ]
            hidden = []
            for f in range(FRAMES):
                normed = natural[pl.ds(f, PAD, stride=FRAMES), :]
                normed_out[hop, block, f] = normed
                hidden.append(normed * taps[KERNEL])
            for f in range(FRAMES):
                conv = None
                for k in range(KERNEL):
                    if 0 <= f + k - HALF < FRAMES:
                        term = taps[k] * hidden[f + k - HALF]
                        conv = term if conv is None else conv + term
                gate = jax.nn.sigmoid(conv)
                gate_out[hop, block, f] = gate * (1.0 + conv * (1.0 - gate))
            return carry

        lax.fori_loop(0, BLOCKS, block_step, 0)


def pair_kernel(
    hops, normed, gate, taps_in, out, normed_rows, gate_rows, both_rows, left, right, plain
):
    frame = lax.broadcasted_iota(jnp.int32, (FRAMES, 2 * LANES), 0)
    lane = lax.broadcasted_iota(jnp.int32, (FRAMES, 2 * LANES), 1)
    lane_frame = lane & (FRAMES - 1)
    lane_clip = (lane & (LANES - 1)) >> 4
    for pair, section in enumerate((2, 0)):
        here = hops[section]
        above = hops[section + 1]

        def block_step(block, carry, here=here, above=above):
            lanes = lanes_of(block)
            weights = taps_in[here, :, lanes]
            weights = weights * weights[KERNEL : KERNEL + 1]
            plain[:, lanes] = weights.astype(BF16)
            for f in range(FRAMES):
                rows = pl.ds(f, PAD, stride=FRAMES)
                value = gate[here, block, f]
                normed_rows[rows, :] = normed[here, block, f]
                gate_rows[rows, :] = value
                both_rows[rows, :] = value * normed[above, block, f]
            right[0:LANES, lanes] = gate_rows[...].astype(BF16)
            right[LANES : 2 * LANES, lanes] = both_rows[...].astype(BF16)
            for c in range(CLIPS):
                value = normed_rows[c * FRAMES : (c + 1) * FRAMES, :]
                for k in range(KERNEL):
                    start = (c * KERNEL + k) * FRAMES
                    left[start : start + FRAMES, lanes] = (value * weights[k : k + 1]).astype(
                        BF16
                    )
            return carry

        lax.fori_loop(0, BLOCKS, block_step, 0)
        columns = right[...]
        sums = lax.dot_general(plain[...], columns, NT, preferred_element_type=F32)
        first = jnp.zeros((FRAMES, 2 * LANES), F32)
        second = jnp.zeros((FRAMES, 2 * LANES), F32)
        for k in range(KERNEL):
            first = first + jnp.where(lane_frame == frame - k + HALF, sums[k : k + 1], 0.0)
        for c in range(CLIPS):
            start = c * KERNEL * FRAMES
            sums = lax.dot_general(
                left[start : start + KERNEL * FRAMES, :], columns, NT, preferred_element_type=F32
            )
            total = jnp.zeros((FRAMES, 2 * LANES), F32)
            for k in range(KERNEL):
                total = total + jnp.where(
                    lane_frame == frame - k + HALF, sums[k * FRAMES : (k + 1) * FRAMES], 0.0
                )
            second = second + jnp.where(lane_clip == c, total, 0.0)
        out[pair, 0:16, :] = first[:, 0:LANES]
        out[pair, 16:32, :] = second[:, 0:LANES]
        out[pair, 32:48, :] = first[:, LANES:]
        out[pair, 48:64, :] = second[:, LANES:]


def tap_rows(taps_in, hop, block):
    weights = taps_in[hop, :, lanes_of(block)]
    return [jnp.broadcast_to(weights[k : k + 1], (PAD, LANES)) for k in range(KERNEL + 1)]


def conv_back(grad_conv, taps):
    out = []
    for f in range(FRAMES):
        conv = None
        for k in range(KERNEL):
            if 0 <= f - k + HALF < FRAMES:
                term = taps[k] * grad_conv[f - k + HALF]
                conv = term if conv is None else conv + term
        out.append(conv * taps[KERNEL])
    return out


def add_taps(grad_conv, normed, hop, block, taps, tap_out):
    hidden = [normed[hop, block, f] * taps[KERNEL] for f in range(FRAMES)]
    for k in range(KERNEL):
        total = None
        for f in range(FRAMES):
            if 0 <= f + k - HALF < FRAMES:
                term = grad_conv[f] * hidden[f + k - HALF]
                total = term if total is None else total + term
        tap_out[k : k + 1, lanes_of(block)] = jnp.sum(total, axis=0, keepdims=True)


def add_sums(grads, normed, hop, block, first, second):
    for f in range(FRAMES):
        first[f] += grads[f]
        second[f] += grads[f] * normed[hop, block, f]


def write_sums(sums, matrices, out, natural):
    row = lax.broadcasted_iota(jnp.int32, (PAD, LANES), 0)
    packed = jnp.zeros((PAD, LANES), F32)
    for index, total in enumerate(sums):
        for f in range(FRAMES):
            natural[pl.ds(f, PAD, stride=FRAMES), :] = total[f]
        packed = jnp.where(row == index, lane_sums(natural[...]), packed)
    for peer in range(MP):
        out[peer, 0:PAD, :] = packed
        out[peer, PAD:, :] = matrices


def read_sums(parts, inv_row, above, here, natural, above_first, above_second, here_first, here_second):
    total = parts[0]
    for peer in range(1, MP):
        total = total + parts[peer]
    scale = inv_row[pl.ds(above, 1), :] / D
    first = total[0:1] * scale
    second = total[1:2] * scale
    matrix = total[PAD:]
    products = matrix[0:32] * first + matrix[32:64] * second
    row = lax.broadcasted_iota(jnp.int32, (LANES, LANES), 0)
    column = lax.broadcasted_iota(jnp.int32, (LANES, LANES), 1)
    same = jnp.where((row >> 4) == (column >> 4), 1.0, 0.0)
    products = jnp.dot(
        products, same, preferred_element_type=F32, precision=lax.Precision.HIGHEST
    )
    keep = (row & (FRAMES - 1)) == (column & (FRAMES - 1))
    keep = keep[0:FRAMES]
    change_first = jnp.sum(jnp.where(keep, products[0:16], 0.0), axis=0, keepdims=True)
    change_second = jnp.sum(jnp.where(keep, products[16:32], 0.0), axis=0, keepdims=True)
    spread(first, above_first, natural)
    spread(second, above_second, natural)
    scale = inv_row[pl.ds(here, 1), :] / D
    spread((total[2:3] - change_first) * scale, here_first, natural)
    spread((total[3:4] - change_second) * scale, here_second, natural)


def write_result(values, natural, result, index, block):
    for f in range(FRAMES):
        natural[pl.ds(f, PAD, stride=FRAMES), :] = values[f]
    result[index, :, lanes_of(block)] = natural[0:ROWS, :].astype(BF16)


def head_kernel(
    hops, query_grad, weight, normed, gate, inv, taps_in, matrices,
    up_out, tap_out, sums_out,
    s0, s1, s2, s3, natural,
):
    for total in (s0, s1, s2, s3):
        total[...] = jnp.zeros_like(total)
    three, two = hops[3], hops[2]

    def block_step(block, carry):
        rows = weight[pl.ds(pl.multiple_of(block * LANES, LANES), LANES), :]
        pooled = None
        for peer in range(MP):
            term = lax.dot_general(
                query_grad[peer],
                rows[:, peer * SLICE : (peer + 1) * SLICE],
                NT,
                preferred_element_type=F32,
            )
            pooled = term if pooled is None else pooled + term
        head = (pooled[0:PAD] / FRAMES).astype(BF16).astype(F32)
        taps = tap_rows(taps_in, three, block)
        grad_conv = [head * gate[three, block, f] for f in range(FRAMES)]
        grads = conv_back(grad_conv, taps)
        add_taps(grad_conv, normed, three, block, taps, tap_out)
        add_sums(grads, normed, three, block, s0, s1)
        ups = [head + inv[three, f] * grads[f] for f in range(FRAMES)]
        for f in range(FRAMES):
            up_out[block, f] = ups[f]
        grads = conv_back(
            [ups[f] * gate[two, block, f] for f in range(FRAMES)], tap_rows(taps_in, two, block)
        )
        add_sums(grads, normed, two, block, s2, s3)
        return carry

    lax.fori_loop(0, BLOCKS, block_step, 0)
    write_sums((s0, s1, s2, s3), matrices[0], sums_out, natural)


def corrected(up, normed, hop, block, first_rows, second_rows):
    return [
        up[f] - first_rows[f] - normed[hop, block, f] * second_rows[f] for f in range(FRAMES)
    ]


def middle_kernel(
    hops, parts, up, normed, gate, inv, inv_row, taps_in, matrices,
    result, up_out, tap_two, tap_one, sums_out,
    s0, s1, s2, s3, a0, a1, b0, b1, natural,
):
    for total in (s0, s1, s2, s3):
        total[...] = jnp.zeros_like(total)
    three, two, one, zero = hops[3], hops[2], hops[1], hops[0]
    read_sums(parts, inv_row, three, two, natural, a0, a1, b0, b1)

    def block_step(block, carry):
        ups = corrected([up[block, f] for f in range(FRAMES)], normed, three, block, a0, a1)
        write_result(ups, natural, result, 0, block)
        taps = tap_rows(taps_in, two, block)
        grad_conv = [ups[f] * gate[two, block, f] for f in range(FRAMES)]
        grads = conv_back(grad_conv, taps)
        add_taps(grad_conv, normed, two, block, taps, tap_two)
        ups = [ups[f] + inv[two, f] * grads[f] for f in range(FRAMES)]
        ups = corrected(ups, normed, two, block, b0, b1)
        write_result(ups, natural, result, 1, block)
        taps = tap_rows(taps_in, one, block)
        grad_conv = [ups[f] * gate[one, block, f] for f in range(FRAMES)]
        grads = conv_back(grad_conv, taps)
        add_taps(grad_conv, normed, one, block, taps, tap_one)
        add_sums(grads, normed, one, block, s0, s1)
        ups = [ups[f] + inv[one, f] * grads[f] for f in range(FRAMES)]
        for f in range(FRAMES):
            up_out[block, f] = ups[f]
        grads = conv_back(
            [ups[f] * gate[zero, block, f] for f in range(FRAMES)],
            tap_rows(taps_in, zero, block),
        )
        add_sums(grads, normed, zero, block, s2, s3)
        return carry

    lax.fori_loop(0, BLOCKS, block_step, 0)
    write_sums((s0, s1, s2, s3), matrices[1], sums_out, natural)


def end_kernel(
    hops, parts, up, normed, gate, inv, inv_row, taps_in,
    before, tap_three, tap_two, tap_one, pair_parts,
    result, message,
    a0, a1, b0, b1, natural, tap_zero, wide,
):
    three, two, one, zero = hops[3], hops[2], hops[1], hops[0]
    slots = [(SECTIONS - hop) & (SECTIONS - 1) for hop in (zero, one, two, three)]
    read_sums(parts, inv_row, one, zero, natural, a0, a1, b0, b1)
    result[slots[3]] = before[0]
    result[slots[2]] = before[1]

    def block_step(block, carry):
        ups = corrected([up[block, f] for f in range(FRAMES)], normed, one, block, a0, a1)
        write_result(ups, natural, result, slots[1], block)
        taps = tap_rows(taps_in, zero, block)
        grad_conv = [ups[f] * gate[zero, block, f] for f in range(FRAMES)]
        grads = conv_back(grad_conv, taps)
        add_taps(grad_conv, normed, zero, block, taps, tap_zero)
        ups = [ups[f] + inv[zero, f] * grads[f] for f in range(FRAMES)]
        ups = corrected(ups, normed, zero, block, b0, b1)
        write_result(ups, natural, result, slots[0], block)
        return carry

    lax.fori_loop(0, BLOCKS, block_step, 0)

    wide[...] = jnp.zeros_like(wide)
    for target in range(DP):
        for section, source in enumerate((tap_zero, tap_one, tap_two, tap_three)):
            row = target // 2
            if row < KERNEL:
                for piece in range(5):
                    start = ((target % 2) * 5 + piece) * LANES
                    wide[target * SECTIONS + section, piece : piece + 1, :] = source[
                        row : row + 1, start : start + LANES
                    ]
            wide[target * SECTIONS + section, 5:7, :] = pair_parts[target]
    half = DP * SECTIONS // 2
    message[...] = wide[...].reshape(2 * half * PAD, LANES).astype(BF16)


FRAME_MAJOR = (BLOCKS, FRAMES, PAD, LANES)
ROW_TILE = pltpu.VMEM((FRAMES, PAD, LANES), F32)
NATURAL = pltpu.VMEM((LANES, LANES), F32)
MATRIX_ROWS = 64
SMEM = pl.BlockSpec(memory_space=pltpu.SMEM)


def shape(dims, dtype=F32):
    return jax.ShapeDtypeStruct(dims, dtype)


def cost(flops, moved):
    return pl.CostEstimate(flops=flops, bytes_accessed=moved, transcendentals=0)


def local_call(kernel, hops, operands, outs, scratch, name, estimate=None):
    return pl.pallas_call(
        kernel,
        out_shape=outs,
        in_specs=[SMEM] + [VMEM] * len(operands),
        out_specs=[VMEM] * len(outs),
        scratch_shapes=scratch,
        compiler_params=PARAMS,
        cost_estimate=estimate,
        name=name,
    )(hops, *operands)


def rotate(value, steps):
    pairs = [(source, (source + steps) % SECTIONS) for source in range(SECTIONS)]
    return lax.ppermute(value, "section", pairs)


def per_device(
    saved_inputs, norm_gains, conv_taps, head_weight, queries, key_embeds, positives, pair_weights
):
    section_now = lax.axis_index("section")
    hops = [(section_now - t) % SECTIONS for t in range(SECTIONS)] + [section_now]
    hops = jnp.stack(hops).astype(jnp.int32)
    inputs_all = saved_inputs[0]

    small = jnp.concatenate([conv_taps[0], norm_gains.astype(BF16)], 0)
    sections = []
    for steps in range(SECTIONS):
        target = (section_now + steps) % SECTIONS
        block = lax.dynamic_slice_in_dim(inputs_all, OWN * target, OWN, 1)
        block = jnp.concatenate([block.reshape(ROWS, WIDE), small], 0)
        sections.append(rotate(block, steps) if steps else block)

    pairs = jnp.concatenate([key_embeds, queries], -1).reshape(MICRO * SHARD, 2 * SLICE)
    pairs = jnp.broadcast_to(pairs[None], (DP,) + pairs.shape)
    texts = lax.all_to_all(pairs, "dp", 0, 0).reshape(TEXTS, 2 * SLICE)

    own_queries = lax.dynamic_slice_in_dim(queries, OWN * section_now, OWN, 1)
    own_queries = jnp.pad(own_queries.reshape(CLIPS, SLICE), ((0, 16 - CLIPS), (0, 0)))

    parts = pl.pallas_call(
        sums_kernel,
        out_shape=shape((MP, PAD, TEXTS + LANES)),
        in_specs=[SMEM] * 3 + [VMEM] * 6,
        out_specs=VMEM,
        compiler_params=PARAMS,
        name="row_sums_and_scores",
    )(hops, positives, pair_weights, *sections, texts, own_queries)
    parts = lax.all_to_all(parts, "mp", 0, 0)

    query_grad, pair_parts = pl.pallas_call(
        softmax_kernel,
        out_shape=(shape((MP, 16, SLICE), BF16), shape((DP, MICRO, LANES))),
        in_specs=[SMEM] * 3 + [VMEM] * 2,
        out_specs=(VMEM, VMEM),
        compiler_params=PARAMS,
        name="softmax_grads",
    )(hops, positives, pair_weights, parts, texts)
    query_grad = lax.all_to_all(query_grad, "mp", 0, 0)

    normed, gate, inv, inv_row, taps = pl.pallas_call(
        forward_kernel,
        out_shape=(
            shape((SECTIONS,) + FRAME_MAJOR),
            shape((SECTIONS,) + FRAME_MAJOR),
            shape((SECTIONS, FRAMES, PAD, LANES)),
            shape((PAD, LANES)),
            shape((SECTIONS, 16, WIDE)),
        ),
        in_specs=[VMEM] * 6,
        out_specs=(VMEM,) * 5,
        scratch_shapes=[NATURAL] * 3,
        compiler_params=PARAMS,
        cost_estimate=cost(10**9, 6 * 10**6),
        name="sections_forward",
    )(query_grad, parts, *sections)
    (matrices,) = local_call(
        pair_kernel,
        hops,
        (normed, gate, taps),
        [shape((2, MATRIX_ROWS, LANES))],
        [NATURAL] * 3
        + [
            pltpu.VMEM((CLIPS * KERNEL * FRAMES, WIDE), BF16),
            pltpu.VMEM((2 * LANES, WIDE), BF16),
            pltpu.VMEM((16, WIDE), BF16),
        ],
        "pair_matrices",
        cost(3 * 10**9, 6 * 10**6),
    )

    sums_shape = shape((MP, PAD + MATRIX_ROWS, LANES))
    tap_shape = shape((16, WIDE))
    up, tap_three, sums = local_call(
        head_kernel,
        hops,
        (query_grad, head_weight, normed, gate, inv, taps, matrices),
        [shape(FRAME_MAJOR), tap_shape, sums_shape],
        [ROW_TILE] * 4 + [NATURAL],
        "head_and_sections",
    )
    sums = lax.all_to_all(sums, "mp", 0, 0)
    before, up, tap_two, tap_one, sums = local_call(
        middle_kernel,
        hops,
        (sums, up, normed, gate, inv, inv_row, taps, matrices),
        [shape((2, ROWS, WIDE), BF16), shape(FRAME_MAJOR), tap_shape, tap_shape, sums_shape],
        [ROW_TILE] * 8 + [NATURAL],
        "middle_sections",
    )
    sums = lax.all_to_all(sums, "mp", 0, 0)

    results_out, message = local_call(
        end_kernel,
        hops,
        (sums, up, normed, gate, inv, inv_row, taps, before, tap_three, tap_two, tap_one, pair_parts),
        [shape((SECTIONS, ROWS, WIDE), BF16), shape((DP * SECTIONS * PAD, LANES), BF16)],
        [ROW_TILE] * 4
        + [NATURAL, pltpu.VMEM((16, WIDE), F32), pltpu.VMEM((DP * SECTIONS, PAD, LANES), F32)],
        "end_sections",
    )
    message = lax.all_to_all(
        message.reshape(DP * SECTIONS, PAD, LANES), ("dp", "section"), 0, 0
    )

    tap_sum = jnp.sum(message[:, 0:5].astype(F32), axis=0).astype(BF16)
    tap_grads = lax.all_to_all(jnp.broadcast_to(tap_sum[None], (DP, 5, LANES)), "dp", 0, 0)
    tap_grads = tap_grads.reshape(16, WIDE)[0:KERNEL].astype(F32)

    columns = message[:, 5:7].reshape(DP, SECTIONS, MICRO, LANES)[..., : OWN * 32]
    columns = columns.reshape(DP, SECTIONS, MICRO, OWN, 32)[..., : MICRO * SHARD]
    columns = columns.transpose(0, 2, 1, 3, 4).reshape(TEXTS, MICRO * SHARD)
    key_grads = (
        lax.dot_general(
            columns, texts[:, SLICE:], (((0,), (0,)), ((), ())), preferred_element_type=F32
        )
        * SCORE_SCALE
    ).reshape(MICRO, SHARD, SLICE)

    results = jnp.broadcast_to(results_out[0, 0, 0], inputs_all.shape)
    for steps in range(SECTIONS):
        source = (section_now - steps) % SECTIONS
        block = results_out[steps]
        block = rotate(block, steps) if steps else block
        block = block.reshape(MICRO, OWN, FRAMES, WIDE)
        results = lax.dynamic_update_slice_in_dim(results, block, OWN * source, 1)
    return (results[None], tap_grads[None], key_grads)


def solution(mesh):
    return jax.shard_map(
        per_device,
        mesh=mesh,
        in_specs=(
            P("section", None, "dp", None, "mp"),
            P("section", "mp"),
            P("section", None, "mp"),
            P("mp", None),
            P(None, "dp", "mp"),
            P(None, "dp", "mp"),
            P(None, "dp"),
            P(None, "dp"),
        ),
        out_specs=(
            P("section", None, "dp", None, "mp"),
            P("section", None, "mp"),
            P(None, "dp", "mp"),
        ),
        check_vma=False,
    )
```

```python
import jax
import jax.numpy as jnp
from jax import lax
from jax.experimental import pallas as pl
from jax.experimental.pallas import tpu as pltpu
from jax.sharding import PartitionSpec as P

D = 5120
EMB = 1024
FRAMES = 16
KERNEL = 15
HALF = KERNEL // 2
SECTIONS = 4
MP = 4
DP = 32
MICRO = 2
SHARD = 12
OWN = SHARD // SECTIONS
CLIPS = MICRO * OWN
ROWS = CLIPS * FRAMES
TEXTS = DP * MICRO * SHARD
HALF_TEXTS = TEXTS // 2
WIDE = D // MP
SLICE = EMB // MP
LANES = 128
BLOCKS = WIDE // LANES
PAD = 8
SCORE_SCALE = 1.0 / 32.0
EPSILON = 1e-05
F32 = jnp.float32
BF16 = jnp.bfloat16

NT = (((1,), (1,)), ((), ()))
VMEM = pl.BlockSpec(memory_space=pltpu.VMEM)
PARAMS = pltpu.CompilerParams(vmem_limit_bytes=24 * 1024 * 1024)


def lane_sums(partial):
    ones = jnp.ones((PAD, LANES), F32)
    return lax.dot_general(
        ones, partial, NT, preferred_element_type=F32, precision=lax.Precision.HIGHEST
    )


def lanes_of(block):
    return pl.ds(pl.multiple_of(block * LANES, LANES), LANES)


def wide_rows(row):
    turned = jnp.concatenate([row, jnp.zeros((PAD - 1, LANES), F32)], 0).T
    return jnp.broadcast_to(turned[:, 0:1], (LANES, LANES))


def text_micros(rows):
    column = lax.broadcasted_iota(jnp.int32, (rows, TEXTS), 1)
    return ((column * 10923) >> 17) & 1


def sums_kernel(
    hops, positives, weights, x0, x1, x2, x3, texts, query, out
):
    rows = []
    for x in (x0, x1, x2, x3):
        total = jnp.zeros((ROWS, LANES), F32)
        square = jnp.zeros((ROWS, LANES), F32)
        for block in range(BLOCKS):
            value = x[0:ROWS, block * LANES : (block + 1) * LANES].astype(F32)
            total = total + value
            square = square + value * value
        rows.append(lane_sums(total)[0:1])
        rows.append(lane_sums(square)[0:1])
    stats = jnp.concatenate(rows, 0)
    stats = jnp.concatenate([stats, jnp.zeros((PAD, LANES - ROWS), F32)], 1)
    scores = lax.dot_general(
        query[...], texts[:, 0:SLICE], NT, preferred_element_type=F32
    )[0:PAD]
    shared = jnp.where(text_micros(OWN) == 0, scores[0:OWN], scores[OWN:CLIPS])
    for peer in range(MP):
        out[peer, 0:OWN, 0:HALF_TEXTS] = shared[:, 0:HALF_TEXTS]
        out[peer, OWN:CLIPS, 0:HALF_TEXTS] = shared[:, HALF_TEXTS:]
        out[peer, CLIPS:PAD, 0:HALF_TEXTS] = jnp.zeros((PAD - CLIPS, HALF_TEXTS), F32)
        out[peer, :, HALF_TEXTS:] = stats


def softmax_kernel(
    hops, positives, weights, parts, texts, query_grad, pair_parts
):
    shared = parts[0, :, 0:HALF_TEXTS]
    for peer in range(1, MP):
        shared = shared + parts[peer, :, 0:HALF_TEXTS]
    shared = jnp.concatenate([shared[0:OWN], shared[OWN:CLIPS]], 1)
    scores = jnp.concatenate([shared, shared, jnp.zeros((PAD - CLIPS, TEXTS), F32)], 0)
    row = lax.broadcasted_iota(jnp.int32, (PAD, TEXTS), 0)
    column = lax.broadcasted_iota(jnp.int32, (PAD, TEXTS), 1)
    clip_micro = jnp.where(row >= OWN, 1, 0)
    scores = jnp.where(text_micros(PAD) == clip_micro, scores * SCORE_SCALE, -1e30)
    exp_scores = jnp.exp(scores - jnp.max(scores, axis=1, keepdims=True))
    probs = exp_scores / jnp.sum(exp_scores, axis=1, keepdims=True)
    base = hops[SECTIONS] * OWN
    positive = jnp.full((PAD, TEXTS), -1, jnp.int32)
    weight = jnp.zeros((PAD, TEXTS), F32)
    for micro in range(MICRO):
        for own in range(OWN):
            index = positives[micro, base + own]
            owner = (index * 10923) >> 17
            index = owner * (MICRO * SHARD) + micro * SHARD + (index - owner * SHARD)
            here = row == micro * OWN + own
            positive = jnp.where(here, index, positive)
            weight = jnp.where(here, weights[micro, base + own], weight)
    hot = jnp.where(column == positive, 1.0, 0.0)
    grad = weight * (probs - hot)
    grad = jnp.concatenate([grad, jnp.zeros((PAD, TEXTS), F32)], 0).astype(BF16)
    result = jnp.dot(grad, texts[:, 0:SLICE], preferred_element_type=F32) * SCORE_SCALE
    result = result.astype(BF16)
    for peer in range(MP):
        query_grad[peer] = result
    grad = grad.astype(F32)
    gap = jnp.zeros((1, 32 - MICRO * SHARD), F32)
    tail = jnp.zeros((1, LANES - OWN * 32), F32)
    for target in range(DP):
        start = target * MICRO * SHARD
        for micro in range(MICRO):
            pieces = []
            for own in range(OWN):
                clip = micro * OWN + own
                pieces += [grad[clip : clip + 1, start : start + MICRO * SHARD], gap]
            pair_parts[target, micro : micro + 1, :] = jnp.concatenate(pieces + [tail], 1)


def spread(row, rows_out, natural):
    natural[...] = wide_rows(row)
    for f in range(FRAMES):
        rows_out[f] = natural[pl.ds(f, PAD, stride=FRAMES), :]


def forward_kernel(
    query_grad, parts, x0, x1, x2, x3,
    normed_out, gate_out, inv_out, inv_row_out, taps_out, rows_out,
    natural, mean_rows, inv_rows,
):
    stats = parts[0, :, HALF_TEXTS:]
    for peer in range(1, MP):
        stats = stats + parts[peer, :, HALF_TEXTS:]
    natural[...] = jnp.zeros_like(natural)
    for hop, x in enumerate((x0, x1, x2, x3)):
        mean = stats[2 * hop : 2 * hop + 1] / D
        variance = stats[2 * hop + 1 : 2 * hop + 2] / D - mean * mean
        inv = lax.rsqrt(variance + EPSILON)
        inv_row_out[hop : hop + 1, :] = inv
        mean_rows[...] = wide_rows(mean)
        inv_rows[...] = wide_rows(inv)
        for f in range(FRAMES):
            inv_out[hop, f] = inv_rows[pl.ds(f, PAD, stride=FRAMES), :]

        def block_step(block, carry, hop=hop, x=x):
            lanes = lanes_of(block)
            value = x[0:ROWS, lanes].astype(F32)
            value = (value - mean_rows[0:ROWS, :]) * inv_rows[0:ROWS, :]
            natural[0:ROWS, :] = value
            rows_out[hop, :, lanes] = value
            weights = x[ROWS : ROWS + 16, lanes].astype(F32)
            taps_out[hop, :, lanes] = weights
            taps = [
                jnp.broadcast_to(weights[k : k + 1], (PAD, LANES)) for k in range(KERNEL + 1)
            ]
            hidden = []
            for f in range(FRAMES):
                normed = natural[pl.ds(f, PAD, stride=FRAMES), :]
                normed_out[hop, block, f] = normed
                hidden.append(normed * taps[KERNEL])
            for f in range(FRAMES):
                conv = None
                for k in range(KERNEL):
                    if 0 <= f + k - HALF < FRAMES:
                        term = taps[k] * hidden[f + k - HALF]
                        conv = term if conv is None else conv + term
                gate = jax.nn.sigmoid(conv)
                gate_out[hop, block, f] = gate * (1.0 + conv * (1.0 - gate))
            return carry

        lax.fori_loop(0, BLOCKS, block_step, 0)


def pair_kernel(
    hops, normed_rows, gate, taps_in, out, gate_rows, left, right, plain
):
    frame = lax.broadcasted_iota(jnp.int32, (FRAMES, 2 * LANES), 0)
    lane = lax.broadcasted_iota(jnp.int32, (FRAMES, 2 * LANES), 1)
    lane_frame = lane & (FRAMES - 1)
    lane_clip = (lane & (LANES - 1)) >> 4
    for pair, section in enumerate((2, 0)):
        here = hops[section]
        above = hops[section + 1]

        def block_step(block, carry, here=here, above=above):
            lanes = lanes_of(block)
            weights = taps_in[here, :, lanes]
            weights = weights * weights[KERNEL : KERNEL + 1]
            plain[:, lanes] = weights.astype(BF16)
            for f in range(FRAMES):
                gate_rows[pl.ds(f, PAD, stride=FRAMES), :] = gate[here, block, f]
            right[0:LANES, lanes] = gate_rows[...].astype(BF16)
            right[LANES : LANES + ROWS, lanes] = (
                gate_rows[0:ROWS, :] * normed_rows[above, :, lanes]
            ).astype(BF16)
            right[LANES + ROWS :, lanes] = jnp.zeros((LANES - ROWS, LANES), BF16)
            for c in range(CLIPS):
                value = normed_rows[here, c * FRAMES : (c + 1) * FRAMES, lanes]
                for k in range(KERNEL):
                    start = (c * KERNEL + k) * FRAMES
                    left[start : start + FRAMES, lanes] = (value * weights[k : k + 1]).astype(
                        BF16
                    )
            return carry

        lax.fori_loop(0, BLOCKS, block_step, 0)
        columns = right[...]
        sums = lax.dot_general(plain[...], columns, NT, preferred_element_type=F32)
        first = jnp.zeros((FRAMES, 2 * LANES), F32)
        second = jnp.zeros((FRAMES, 2 * LANES), F32)
        for k in range(KERNEL):
            first = first + jnp.where(lane_frame == frame - k + HALF, sums[k : k + 1], 0.0)
        for c in range(CLIPS):
            start = c * KERNEL * FRAMES
            sums = lax.dot_general(
                left[start : start + KERNEL * FRAMES, :], columns, NT, preferred_element_type=F32
            )
            total = jnp.zeros((FRAMES, 2 * LANES), F32)
            for k in range(KERNEL):
                total = total + jnp.where(
                    lane_frame == frame - k + HALF, sums[k * FRAMES : (k + 1) * FRAMES], 0.0
                )
            second = second + jnp.where(lane_clip == c, total, 0.0)
        out[pair, 0:16, :] = first[:, 0:LANES]
        out[pair, 16:32, :] = second[:, 0:LANES]
        out[pair, 32:48, :] = first[:, LANES:]
        out[pair, 48:64, :] = second[:, LANES:]


def tap_rows(taps_in, hop, block):
    weights = taps_in[hop, :, lanes_of(block)]
    return [jnp.broadcast_to(weights[k : k + 1], (PAD, LANES)) for k in range(KERNEL + 1)]


def conv_back(grad_conv, taps):
    out = []
    for f in range(FRAMES):
        conv = None
        for k in range(KERNEL):
            if 0 <= f - k + HALF < FRAMES:
                term = taps[k] * grad_conv[f - k + HALF]
                conv = term if conv is None else conv + term
        out.append(conv * taps[KERNEL])
    return out


def add_taps(grad_conv, normed, hop, block, taps, tap_out):
    hidden = [normed[hop, block, f] * taps[KERNEL] for f in range(FRAMES)]
    for k in range(KERNEL):
        total = None
        for f in range(FRAMES):
            if 0 <= f + k - HALF < FRAMES:
                term = grad_conv[f] * hidden[f + k - HALF]
                total = term if total is None else total + term
        tap_out[k : k + 1, lanes_of(block)] = jnp.sum(total, axis=0, keepdims=True)


def add_sums(grads, normed, hop, block, first, second):
    for f in range(FRAMES):
        first[f] += grads[f]
        second[f] += grads[f] * normed[hop, block, f]


def write_sums(sums, matrices, out, natural):
    row = lax.broadcasted_iota(jnp.int32, (PAD, LANES), 0)
    packed = jnp.zeros((PAD, LANES), F32)
    for index, total in enumerate(sums):
        for f in range(FRAMES):
            natural[pl.ds(f, PAD, stride=FRAMES), :] = total[f]
        packed = jnp.where(row == index, lane_sums(natural[...]), packed)
    for peer in range(MP):
        out[peer, 0:PAD, :] = packed
        out[peer, PAD:, :] = matrices


def read_sums(parts, inv_row, above, here, natural, above_first, above_second, here_first, here_second):
    total = parts[0]
    for peer in range(1, MP):
        total = total + parts[peer]
    scale = inv_row[pl.ds(above, 1), :] / D
    first = total[0:1] * scale
    second = total[1:2] * scale
    matrix = total[PAD:]
    products = matrix[0:32] * first + matrix[32:64] * second
    row = lax.broadcasted_iota(jnp.int32, (LANES, LANES), 0)
    column = lax.broadcasted_iota(jnp.int32, (LANES, LANES), 1)
    same = jnp.where((row >> 4) == (column >> 4), 1.0, 0.0)
    products = jnp.dot(
        products, same, preferred_element_type=F32, precision=lax.Precision.HIGHEST
    )
    keep = (row & (FRAMES - 1)) == (column & (FRAMES - 1))
    keep = keep[0:FRAMES]
    change_first = jnp.sum(jnp.where(keep, products[0:16], 0.0), axis=0, keepdims=True)
    change_second = jnp.sum(jnp.where(keep, products[16:32], 0.0), axis=0, keepdims=True)
    spread(first, above_first, natural)
    spread(second, above_second, natural)
    scale = inv_row[pl.ds(here, 1), :] / D
    spread((total[2:3] - change_first) * scale, here_first, natural)
    spread((total[3:4] - change_second) * scale, here_second, natural)


def write_result(values, natural, result, index, block):
    for f in range(FRAMES):
        natural[pl.ds(f, PAD, stride=FRAMES), :] = values[f]
    result[index, :, lanes_of(block)] = natural[0:ROWS, :].astype(BF16)


def head_kernel(
    hops, query_grad, weight, normed, gate, inv, taps_in, matrices,
    up_out, tap_out, sums_out,
    s0, s1, s2, s3, natural,
):
    for total in (s0, s1, s2, s3):
        total[...] = jnp.zeros_like(total)
    three, two = hops[3], hops[2]

    def block_step(block, carry):
        rows = weight[pl.ds(pl.multiple_of(block * LANES, LANES), LANES), :]
        pooled = None
        for peer in range(MP):
            term = lax.dot_general(
                query_grad[peer],
                rows[:, peer * SLICE : (peer + 1) * SLICE],
                NT,
                preferred_element_type=F32,
            )
            pooled = term if pooled is None else pooled + term
        head = (pooled[0:PAD] / FRAMES).astype(BF16).astype(F32)
        taps = tap_rows(taps_in, three, block)
        grad_conv = [head * gate[three, block, f] for f in range(FRAMES)]
        grads = conv_back(grad_conv, taps)
        add_taps(grad_conv, normed, three, block, taps, tap_out)
        add_sums(grads, normed, three, block, s0, s1)
        ups = [head + inv[three, f] * grads[f] for f in range(FRAMES)]
        for f in range(FRAMES):
            up_out[block, f] = ups[f]
        grads = conv_back(
            [ups[f] * gate[two, block, f] for f in range(FRAMES)], tap_rows(taps_in, two, block)
        )
        add_sums(grads, normed, two, block, s2, s3)
        return carry

    lax.fori_loop(0, BLOCKS, block_step, 0)
    write_sums((s0, s1, s2, s3), matrices[0], sums_out, natural)


def corrected(up, normed, hop, block, first_rows, second_rows):
    return [
        up[f] - first_rows[f] - normed[hop, block, f] * second_rows[f] for f in range(FRAMES)
    ]


def middle_kernel(
    hops, parts, up, normed, gate, inv, inv_row, taps_in, matrices,
    result, up_out, tap_two, tap_one, sums_out,
    s0, s1, s2, s3, a0, a1, b0, b1, natural,
):
    for total in (s0, s1, s2, s3):
        total[...] = jnp.zeros_like(total)
    three, two, one, zero = hops[3], hops[2], hops[1], hops[0]
    read_sums(parts, inv_row, three, two, natural, a0, a1, b0, b1)

    def block_step(block, carry):
        ups = corrected([up[block, f] for f in range(FRAMES)], normed, three, block, a0, a1)
        write_result(ups, natural, result, 0, block)
        taps = tap_rows(taps_in, two, block)
        grad_conv = [ups[f] * gate[two, block, f] for f in range(FRAMES)]
        grads = conv_back(grad_conv, taps)
        add_taps(grad_conv, normed, two, block, taps, tap_two)
        ups = [ups[f] + inv[two, f] * grads[f] for f in range(FRAMES)]
        ups = corrected(ups, normed, two, block, b0, b1)
        write_result(ups, natural, result, 1, block)
        taps = tap_rows(taps_in, one, block)
        grad_conv = [ups[f] * gate[one, block, f] for f in range(FRAMES)]
        grads = conv_back(grad_conv, taps)
        add_taps(grad_conv, normed, one, block, taps, tap_one)
        add_sums(grads, normed, one, block, s0, s1)
        ups = [ups[f] + inv[one, f] * grads[f] for f in range(FRAMES)]
        for f in range(FRAMES):
            up_out[block, f] = ups[f]
        grads = conv_back(
            [ups[f] * gate[zero, block, f] for f in range(FRAMES)],
            tap_rows(taps_in, zero, block),
        )
        add_sums(grads, normed, zero, block, s2, s3)
        return carry

    lax.fori_loop(0, BLOCKS, block_step, 0)
    write_sums((s0, s1, s2, s3), matrices[1], sums_out, natural)


def end_kernel(
    hops, parts, up, normed, gate, inv, inv_row, taps_in,
    tap_three, tap_two, tap_one, pair_parts,
    result, message,
    a0, a1, b0, b1, natural, tap_zero, wide,
):
    three, two, one, zero = hops[3], hops[2], hops[1], hops[0]
    read_sums(parts, inv_row, one, zero, natural, a0, a1, b0, b1)

    def block_step(block, carry):
        ups = corrected([up[block, f] for f in range(FRAMES)], normed, one, block, a0, a1)
        write_result(ups, natural, result, 1, block)
        taps = tap_rows(taps_in, zero, block)
        grad_conv = [ups[f] * gate[zero, block, f] for f in range(FRAMES)]
        grads = conv_back(grad_conv, taps)
        add_taps(grad_conv, normed, zero, block, taps, tap_zero)
        ups = [ups[f] + inv[zero, f] * grads[f] for f in range(FRAMES)]
        ups = corrected(ups, normed, zero, block, b0, b1)
        write_result(ups, natural, result, 0, block)
        return carry

    lax.fori_loop(0, BLOCKS, block_step, 0)

    wide[...] = jnp.zeros_like(wide)
    for target in range(DP):
        for section, source in enumerate((tap_zero, tap_one, tap_two, tap_three)):
            row = target // 2
            if row < KERNEL:
                for piece in range(5):
                    start = ((target % 2) * 5 + piece) * LANES
                    wide[target * SECTIONS + section, piece : piece + 1, :] = source[
                        row : row + 1, start : start + LANES
                    ]
            wide[target * SECTIONS + section, 5:7, :] = pair_parts[target]
    half = DP * SECTIONS // 2
    message[...] = wide[...].reshape(2 * half * PAD, LANES).astype(BF16)


def order_kernel(hops, last, before, *outs):
    for section in range(SECTIONS):
        steps = (SECTIONS - hops[section]) & (SECTIONS - 1)
        for target in range(SECTIONS):

            @pl.when(steps == target)
            def _(section=section, target=target):
                outs[target][...] = last[section] if section < 2 else before[3 - section]


def assemble_kernel(hops, own, first, second, third, tap_sum, out, sems):
    copies = []
    for steps, part in enumerate((own, first, second, third)):
        source = (hops[SECTIONS] + SECTIONS - steps) & (SECTIONS - 1)
        for micro in range(MICRO):
            copies.append(
                pltpu.make_async_copy(
                    part.at[pl.ds(micro * OWN, OWN)],
                    out.at[micro, pl.ds(source * OWN, OWN)],
                    sems.at[steps * MICRO + micro],
                )
            )
    for copy in copies:
        copy.start()
    for copy in copies:
        copy.wait()


FRAME_MAJOR = (BLOCKS, FRAMES, PAD, LANES)
ROW_TILE = pltpu.VMEM((FRAMES, PAD, LANES), F32)
NATURAL = pltpu.VMEM((LANES, LANES), F32)
MATRIX_ROWS = 64
SMEM = pl.BlockSpec(memory_space=pltpu.SMEM)


def shape(dims, dtype=F32):
    return jax.ShapeDtypeStruct(dims, dtype)


def cost(flops, moved):
    return pl.CostEstimate(flops=flops, bytes_accessed=moved, transcendentals=0)


def local_call(kernel, hops, operands, outs, scratch, name, estimate=None):
    return pl.pallas_call(
        kernel,
        out_shape=outs,
        in_specs=[SMEM] + [VMEM] * len(operands),
        out_specs=[VMEM] * len(outs),
        scratch_shapes=scratch,
        compiler_params=PARAMS,
        cost_estimate=estimate,
        name=name,
    )(hops, *operands)


def rotate(value, steps):
    pairs = [(source, (source + steps) % SECTIONS) for source in range(SECTIONS)]
    return lax.ppermute(value, "section", pairs)


def per_device(
    saved_inputs, norm_gains, conv_taps, head_weight, queries, key_embeds, positives, pair_weights
):
    section_now = lax.axis_index("section")
    hops = [(section_now - t) % SECTIONS for t in range(SECTIONS)] + [section_now]
    hops = jnp.stack(hops).astype(jnp.int32)
    inputs_all = saved_inputs[0]

    small = jnp.concatenate([conv_taps[0], norm_gains.astype(BF16)], 0)
    sections = []
    for steps in range(SECTIONS):
        target = (section_now + steps) % SECTIONS
        block = lax.dynamic_slice_in_dim(inputs_all, OWN * target, OWN, 1)
        block = jnp.concatenate([block.reshape(ROWS, WIDE), small], 0)
        sections.append(rotate(block, steps) if steps else block)

    pairs = jnp.concatenate([key_embeds, queries], -1).reshape(MICRO * SHARD, 2 * SLICE)
    pairs = jnp.broadcast_to(pairs[None], (DP,) + pairs.shape)
    texts = lax.all_to_all(pairs, "dp", 0, 0).reshape(TEXTS, 2 * SLICE)

    own_queries = lax.dynamic_slice_in_dim(queries, OWN * section_now, OWN, 1)
    own_queries = jnp.pad(own_queries.reshape(CLIPS, SLICE), ((0, 16 - CLIPS), (0, 0)))

    parts = pl.pallas_call(
        sums_kernel,
        out_shape=shape((MP, PAD, HALF_TEXTS + LANES)),
        in_specs=[SMEM] * 3 + [VMEM] * 6,
        out_specs=VMEM,
        compiler_params=PARAMS,
        name="row_sums_and_scores",
    )(hops, positives, pair_weights, *sections, texts, own_queries)
    parts = lax.all_to_all(parts, "mp", 0, 0)

    query_grad, pair_parts = pl.pallas_call(
        softmax_kernel,
        out_shape=(shape((MP, 16, SLICE), BF16), shape((DP, MICRO, LANES))),
        in_specs=[SMEM] * 3 + [VMEM] * 2,
        out_specs=(VMEM, VMEM),
        compiler_params=PARAMS,
        name="softmax_grads",
    )(hops, positives, pair_weights, parts, texts)
    query_grad = lax.all_to_all(query_grad, "mp", 0, 0)

    normed, gate, inv, inv_row, taps, normed_rows = pl.pallas_call(
        forward_kernel,
        out_shape=(
            shape((SECTIONS,) + FRAME_MAJOR),
            shape((SECTIONS,) + FRAME_MAJOR),
            shape((SECTIONS, FRAMES, PAD, LANES)),
            shape((PAD, LANES)),
            shape((SECTIONS, 16, WIDE)),
            shape((SECTIONS, ROWS, WIDE)),
        ),
        in_specs=[VMEM] * 6,
        out_specs=(VMEM,) * 6,
        scratch_shapes=[NATURAL] * 3,
        compiler_params=PARAMS,
        cost_estimate=cost(10**9, 6 * 10**6),
        name="sections_forward",
    )(query_grad, parts, *sections)
    (matrices,) = local_call(
        pair_kernel,
        hops,
        (normed_rows, gate, taps),
        [shape((2, MATRIX_ROWS, LANES))],
        [NATURAL]
        + [
            pltpu.VMEM((CLIPS * KERNEL * FRAMES, WIDE), BF16),
            pltpu.VMEM((2 * LANES, WIDE), BF16),
            pltpu.VMEM((16, WIDE), BF16),
        ],
        "pair_matrices",
        cost(3 * 10**9, 6 * 10**6),
    )

    sums_shape = shape((MP, PAD + MATRIX_ROWS, LANES))
    tap_shape = shape((16, WIDE))
    up, tap_three, sums = local_call(
        head_kernel,
        hops,
        (query_grad, head_weight, normed, gate, inv, taps, matrices),
        [shape(FRAME_MAJOR), tap_shape, sums_shape],
        [ROW_TILE] * 4 + [NATURAL],
        "head_and_sections",
    )
    sums = lax.all_to_all(sums, "mp", 0, 0)
    before, up, tap_two, tap_one, sums = local_call(
        middle_kernel,
        hops,
        (sums, up, normed, gate, inv, inv_row, taps, matrices),
        [shape((2, ROWS, WIDE), BF16), shape(FRAME_MAJOR), tap_shape, tap_shape, sums_shape],
        [ROW_TILE] * 8 + [NATURAL],
        "middle_sections",
    )
    sums = lax.all_to_all(sums, "mp", 0, 0)

    last, message = local_call(
        end_kernel,
        hops,
        (sums, up, normed, gate, inv, inv_row, taps, tap_three, tap_two, tap_one, pair_parts),
        [shape((2, ROWS, WIDE), BF16), shape((DP * SECTIONS * PAD, LANES), BF16)],
        [ROW_TILE] * 4
        + [NATURAL, pltpu.VMEM((16, WIDE), F32), pltpu.VMEM((DP * SECTIONS, PAD, LANES), F32)],
        "end_sections",
    )
    message = lax.all_to_all(
        message.reshape(DP * SECTIONS, PAD, LANES), ("dp", "section"), 0, 0
    )

    tap_sum = jnp.sum(message[:, 0:5].astype(F32), axis=0).astype(BF16)
    tap_grads = lax.all_to_all(jnp.broadcast_to(tap_sum[None], (DP, 5, LANES)), "dp", 0, 0)
    tap_grads = tap_grads.reshape(16, WIDE)[0:KERNEL].astype(F32)

    columns = message[:, 5:7].reshape(DP, SECTIONS, MICRO, LANES)[..., : OWN * 32]
    columns = columns.reshape(DP, SECTIONS, MICRO, OWN, 32)[..., : MICRO * SHARD]
    columns = columns.transpose(0, 2, 1, 3, 4).reshape(TEXTS, MICRO * SHARD)
    key_grads = (
        lax.dot_general(
            columns, texts[:, SLICE:], (((0,), (0,)), ((), ())), preferred_element_type=F32
        )
        * SCORE_SCALE
    ).reshape(MICRO, SHARD, SLICE)

    ordered = local_call(
        order_kernel,
        hops,
        (last, before),
        [shape((ROWS, WIDE), BF16)] * SECTIONS,
        [],
        "order_results",
        cost(10**9, 2 * 10**6),
    )
    pieces = [rotate(part, steps) if steps else part for steps, part in enumerate(ordered)]
    pieces = [part.reshape(CLIPS, FRAMES, WIDE) for part in pieces]
    results = pl.pallas_call(
        assemble_kernel,
        out_shape=shape((MICRO, SHARD, FRAMES, WIDE), BF16),
        in_specs=[SMEM] + [pl.BlockSpec(memory_space=pl.ANY)] * 5,
        out_specs=pl.BlockSpec(memory_space=pl.ANY),
        scratch_shapes=[pltpu.SemaphoreType.DMA((SECTIONS * MICRO,))],
        compiler_params=PARAMS,
        cost_estimate=cost(10**10, 10**7),
        name="assemble_results",
    )(hops, *pieces, tap_sum)
    return (results[None], tap_grads[None], key_grads)


def solution(mesh):
    return jax.shard_map(
        per_device,
        mesh=mesh,
        in_specs=(
            P("section", None, "dp", None, "mp"),
            P("section", "mp"),
            P("section", None, "mp"),
            P("mp", None),
            P(None, "dp", "mp"),
            P(None, "dp", "mp"),
            P(None, "dp"),
            P(None, "dp"),
        ),
        out_specs=(
            P("section", None, "dp", None, "mp"),
            P("section", None, "mp"),
            P(None, "dp", "mp"),
        ),
        check_vma=False,
    )
```

```python
import jax
import jax.numpy as jnp
from jax import lax
from jax.experimental import pallas as pl
from jax.experimental.pallas import tpu as pltpu
from jax.sharding import PartitionSpec as P

D = 5120
EMB = 1024
FRAMES = 16
KERNEL = 15
HALF = KERNEL // 2
SECTIONS = 4
MP = 4
DP = 32
MICRO = 2
SHARD = 12
OWN = SHARD // SECTIONS
CLIPS = MICRO * OWN
ROWS = CLIPS * FRAMES
TEXTS = DP * MICRO * SHARD
HALF_TEXTS = TEXTS // 2
WIDE = D // MP
SLICE = EMB // MP
LANES = 128
BLOCKS = WIDE // LANES
PAD = 8
SCORE_SCALE = 1.0 / 32.0
EPSILON = 1e-05
F32 = jnp.float32
BF16 = jnp.bfloat16

NT = (((1,), (1,)), ((), ()))
VMEM = pl.BlockSpec(memory_space=pltpu.VMEM)
PARAMS = pltpu.CompilerParams(vmem_limit_bytes=24 * 1024 * 1024)


def lane_sums(partial):
    ones = jnp.ones((PAD, LANES), F32)
    return lax.dot_general(
        ones, partial, NT, preferred_element_type=F32, precision=lax.Precision.HIGHEST
    )


def split_halves(value):
    high = value.astype(BF16)
    return high, (value - high.astype(F32)).astype(BF16)


def lanes_of(block):
    return pl.ds(pl.multiple_of(block * LANES, LANES), LANES)


def wide_rows(rows):
    rows = list(rows)
    turned = jnp.concatenate(rows + [jnp.zeros((PAD - len(rows), LANES), F32)], 0).T
    return [
        jnp.broadcast_to(turned[:, index : index + 1], (LANES, LANES))
        for index in range(len(rows))
    ]


def text_micros(rows):
    column = lax.broadcasted_iota(jnp.int32, (rows, TEXTS), 1)
    return ((column * 10923) >> 17) & 1


def scores_kernel(texts, others, query, x1, x3, out):
    scores = [
        lax.dot_general(query[...], part[:, 0:SLICE], NT, preferred_element_type=F32)
        for part in (texts, others)
    ]
    scores = jnp.concatenate(scores, 1)
    shared = jnp.where(text_micros(OWN) == 0, scores[0:OWN], scores[OWN:CLIPS])
    for peer in range(MP):
        out[peer, 0:OWN, :] = shared[:, 0:HALF_TEXTS]
        out[peer, OWN:CLIPS, :] = shared[:, HALF_TEXTS:]
        out[peer, CLIPS:PAD, :] = jnp.zeros((PAD - CLIPS, HALF_TEXTS), F32)


def softmax_kernel(
    hops, positives, weights, parts, texts, others, x0, x1, x2, x3, message, pair_parts
):
    rows = []
    for x in (x0, x1, x2, x3):
        total = jnp.zeros((ROWS, LANES), F32)
        square = jnp.zeros((ROWS, LANES), F32)
        for block in range(BLOCKS):
            value = x[0:ROWS, block * LANES : (block + 1) * LANES].astype(F32)
            total = total + value
            square = square + value * value
        rows.append(lane_sums(total)[0:1])
        rows.append(lane_sums(square)[0:1])
    stats = jnp.concatenate(rows, 0)
    stats = jnp.concatenate([stats, jnp.zeros((PAD, LANES - ROWS), F32)], 1)

    shared = parts[0]
    for peer in range(1, MP):
        shared = shared + parts[peer]
    shared = jnp.concatenate([shared[0:OWN], shared[OWN:CLIPS]], 1)
    scores = jnp.concatenate([shared, shared, jnp.zeros((PAD - CLIPS, TEXTS), F32)], 0)
    row = lax.broadcasted_iota(jnp.int32, (PAD, TEXTS), 0)
    column = lax.broadcasted_iota(jnp.int32, (PAD, TEXTS), 1)
    clip_micro = jnp.where(row >= OWN, 1, 0)
    scores = jnp.where(text_micros(PAD) == clip_micro, scores * SCORE_SCALE, -1e30)
    exp_scores = jnp.exp(scores - jnp.max(scores, axis=1, keepdims=True))
    probs = exp_scores / jnp.sum(exp_scores, axis=1, keepdims=True)
    base = hops[SECTIONS] * OWN
    positive = jnp.full((PAD, TEXTS), -1, jnp.int32)
    weight = jnp.zeros((PAD, TEXTS), F32)
    for micro in range(MICRO):
        for own in range(OWN):
            index = positives[micro, base + own]
            owner = (index * 10923) >> 17
            place = ((owner & 1) ^ hops[SECTIONS + 1]) * (DP // 2) + (owner >> 1)
            index = place * (MICRO * SHARD) + micro * SHARD + (index - owner * SHARD)
            here = row == micro * OWN + own
            positive = jnp.where(here, index, positive)
            weight = jnp.where(here, weights[micro, base + own], weight)
    hot = jnp.where(column == positive, 1.0, 0.0)
    grad = weight * (probs - hot)
    grad = jnp.concatenate([grad, jnp.zeros((PAD, TEXTS), F32)], 0).astype(BF16)
    result = jnp.dot(grad[:, 0:HALF_TEXTS], texts[:, 0:SLICE], preferred_element_type=F32)
    result = result + jnp.dot(
        grad[:, HALF_TEXTS:], others[:, 0:SLICE], preferred_element_type=F32
    )
    result = (result * SCORE_SCALE)[0:PAD]
    for peer in range(MP):
        message[peer, 0:PAD, :] = result[:, 0:LANES]
        message[peer, PAD : 2 * PAD, :] = result[:, LANES:]
        message[peer, 2 * PAD :, :] = stats
    grad = grad.astype(F32)
    gap = jnp.zeros((1, 32 - MICRO * SHARD), F32)
    tail = jnp.zeros((1, LANES - OWN * 32), F32)
    for place in range(DP):
        start = place * MICRO * SHARD
        half = hops[SECTIONS + 1] ^ (place // (DP // 2))
        target = (place % (DP // 2)) * 2 + half
        for micro in range(MICRO):
            pieces = []
            for own in range(OWN):
                clip = micro * OWN + own
                pieces += [grad[clip : clip + 1, start : start + MICRO * SHARD], gap]
            pair_parts[target, micro : micro + 1, :] = jnp.concatenate(pieces + [tail], 1)


def spread(rows, outs, naturals):
    for value, natural in zip(wide_rows(rows), naturals):
        natural[...] = value
    for rows_out, natural in zip(outs, naturals):
        for f in range(FRAMES):
            rows_out[f] = natural[pl.ds(f, PAD, stride=FRAMES), :]


def forward_kernel(
    parts, x0, x1, x2, x3,
    normed_out, gate_out, inv_out, inv_row_out, taps_out, rows_out,
    natural, mean_rows, inv_rows,
):
    stats = parts[0, 2 * PAD :, :]
    for peer in range(1, MP):
        stats = stats + parts[peer, 2 * PAD :, :]
    natural[...] = jnp.zeros_like(natural)
    for hop, x in enumerate((x0, x1, x2, x3)):
        mean = stats[2 * hop : 2 * hop + 1] / D
        variance = stats[2 * hop + 1 : 2 * hop + 2] / D - mean * mean
        inv = lax.rsqrt(variance + EPSILON)
        inv_row_out[hop : hop + 1, :] = inv
        mean_rows[...], inv_rows[...] = wide_rows((mean, inv))
        for f in range(FRAMES):
            inv_out[hop, f] = inv_rows[pl.ds(f, PAD, stride=FRAMES), :]

        def block_step(block, carry, hop=hop, x=x):
            lanes = lanes_of(block)
            value = x[0:ROWS, lanes].astype(F32)
            value = (value - mean_rows[0:ROWS, :]) * inv_rows[0:ROWS, :]
            natural[0:ROWS, :] = value
            rows_out[hop, :, lanes] = value
            weights = x[ROWS : ROWS + 16, lanes].astype(F32)
            taps_out[hop, :, lanes] = weights
            taps = [
                jnp.broadcast_to(weights[k : k + 1], (PAD, LANES)) for k in range(KERNEL + 1)
            ]
            hidden = []
            for f in range(FRAMES):
                normed = natural[pl.ds(f, PAD, stride=FRAMES), :]
                normed_out[hop, block, f] = normed
                hidden.append(normed * taps[KERNEL])
            for f in range(FRAMES):
                conv = None
                for k in range(KERNEL):
                    if 0 <= f + k - HALF < FRAMES:
                        term = taps[k] * hidden[f + k - HALF]
                        conv = term if conv is None else conv + term
                gate = jax.nn.sigmoid(conv)
                gate_out[hop, block, f] = gate * (1.0 + conv * (1.0 - gate))
            return carry

        lax.fori_loop(0, BLOCKS, block_step, 0)


def pair_kernel(
    hops, normed_rows, gate, taps_in, out, gate_rows, left, right, plain
):
    frame = lax.broadcasted_iota(jnp.int32, (FRAMES, 2 * LANES), 0)
    lane = lax.broadcasted_iota(jnp.int32, (FRAMES, 2 * LANES), 1)
    lane_frame = lane & (FRAMES - 1)
    lane_clip = (lane & (LANES - 1)) >> 4
    for pair, section in enumerate((2, 0)):
        here = hops[section]
        above = hops[section + 1]

        def block_step(block, carry, here=here, above=above):
            lanes = lanes_of(block)
            weights = taps_in[here, :, lanes]
            weights = weights * weights[KERNEL : KERNEL + 1]
            plain[:, lanes] = weights.astype(BF16)
            for f in range(FRAMES):
                gate_rows[pl.ds(f, PAD, stride=FRAMES), :] = gate[here, block, f]
            right[0:LANES, lanes] = gate_rows[...].astype(BF16)
            right[LANES : LANES + ROWS, lanes] = (
                gate_rows[0:ROWS, :] * normed_rows[above, :, lanes]
            ).astype(BF16)
            right[LANES + ROWS :, lanes] = jnp.zeros((LANES - ROWS, LANES), BF16)
            for c in range(CLIPS):
                value = normed_rows[here, c * FRAMES : (c + 1) * FRAMES, lanes]
                for k in range(KERNEL):
                    start = (c * KERNEL + k) * FRAMES
                    left[start : start + FRAMES, lanes] = (value * weights[k : k + 1]).astype(
                        BF16
                    )
            return carry

        lax.fori_loop(0, BLOCKS, block_step, 0)
        columns = right[...]
        sums = lax.dot_general(plain[...], columns, NT, preferred_element_type=F32)
        first = jnp.zeros((FRAMES, 2 * LANES), F32)
        second = jnp.zeros((FRAMES, 2 * LANES), F32)
        for k in range(KERNEL):
            first = first + jnp.where(lane_frame == frame - k + HALF, sums[k : k + 1], 0.0)
        for c in range(CLIPS):
            start = c * KERNEL * FRAMES
            sums = lax.dot_general(
                left[start : start + KERNEL * FRAMES, :], columns, NT, preferred_element_type=F32
            )
            total = jnp.zeros((FRAMES, 2 * LANES), F32)
            for k in range(KERNEL):
                total = total + jnp.where(
                    lane_frame == frame - k + HALF, sums[k * FRAMES : (k + 1) * FRAMES], 0.0
                )
            second = second + jnp.where(lane_clip == c, total, 0.0)
        out[pair, 0:16, :] = first[:, 0:LANES]
        out[pair, 16:32, :] = second[:, 0:LANES]
        out[pair, 32:48, :] = first[:, LANES:]
        out[pair, 48:64, :] = second[:, LANES:]


def tap_rows(taps_in, hop, block):
    weights = taps_in[hop, :, lanes_of(block)]
    return [jnp.broadcast_to(weights[k : k + 1], (PAD, LANES)) for k in range(KERNEL + 1)]


def conv_back(grad_conv, taps):
    out = []
    for f in range(FRAMES):
        conv = None
        for k in range(KERNEL):
            if 0 <= f - k + HALF < FRAMES:
                term = taps[k] * grad_conv[f - k + HALF]
                conv = term if conv is None else conv + term
        out.append(conv * taps[KERNEL])
    return out


def add_taps(grad_conv, normed, hop, block, taps, tap_out):
    hidden = [normed[hop, block, f] * taps[KERNEL] for f in range(FRAMES)]
    for k in range(KERNEL):
        total = None
        for f in range(FRAMES):
            if 0 <= f + k - HALF < FRAMES:
                term = grad_conv[f] * hidden[f + k - HALF]
                total = term if total is None else total + term
        tap_out[k : k + 1, lanes_of(block)] = jnp.sum(total, axis=0, keepdims=True)


def add_sums(grads, normed, hop, block, first, second):
    for f in range(FRAMES):
        first[f] += grads[f]
        second[f] += grads[f] * normed[hop, block, f]


def write_sums(sums, matrices, out, stacked):
    for index, total in enumerate(sums):
        for f in range(FRAMES):
            stacked[pl.ds(index * LANES + f, PAD, stride=FRAMES), :] = total[f]
    high, low = split_halves(stacked[...])
    ones = jnp.ones((16, LANES), BF16)
    packed = lax.dot_general(ones, high, NT, preferred_element_type=F32)
    packed = packed + lax.dot_general(ones, low, NT, preferred_element_type=F32)
    packed = [packed[0:1, index * LANES : (index + 1) * LANES] for index in range(len(sums))]
    packed = jnp.concatenate(packed + [jnp.zeros((PAD - len(sums), LANES), F32)], 0)
    for peer in range(MP):
        out[peer, 0:PAD, :] = packed
        out[peer, PAD:, :] = matrices


def read_sums(parts, inv_row, above, here, stacked, outs):
    total = parts[0]
    for peer in range(1, MP):
        total = total + parts[peer]
    scale = inv_row[pl.ds(above, 1), :] / D
    first = total[0:1] * scale
    second = total[1:2] * scale
    matrix = total[PAD:]
    high, low = split_halves(matrix[0:32] * first + matrix[32:64] * second)
    row = lax.broadcasted_iota(jnp.int32, (LANES, LANES), 0)
    column = lax.broadcasted_iota(jnp.int32, (LANES, LANES), 1)
    same = jnp.where((row >> 4) == (column >> 4), 1.0, 0.0).astype(BF16)
    products = jnp.dot(high, same, preferred_element_type=F32)
    products = products + jnp.dot(low, same, preferred_element_type=F32)
    keep = (row & (FRAMES - 1)) == (column & (FRAMES - 1))
    keep = keep[0:FRAMES]
    change_first = jnp.sum(jnp.where(keep, products[0:16], 0.0), axis=0, keepdims=True)
    change_second = jnp.sum(jnp.where(keep, products[16:32], 0.0), axis=0, keepdims=True)
    scale = inv_row[pl.ds(here, 1), :] / D
    rows = (
        first,
        second,
        (total[2:3] - change_first) * scale,
        (total[3:4] - change_second) * scale,
    )
    naturals = [stacked.at[pl.ds(index * LANES, LANES)] for index in range(len(rows))]
    spread(rows, outs, naturals)


def write_result(values, natural, result, index, block):
    for f in range(FRAMES):
        natural[pl.ds(f, PAD, stride=FRAMES), :] = values[f]
    result[index, :, lanes_of(block)] = natural[0:ROWS, :].astype(BF16)


def head_kernel(
    hops, parts, weight, normed, gate, inv, taps_in, matrices,
    up_out, tap_out, sums_out,
    s0, s1, s2, s3, stacked, full_grad, head_rows,
):
    full_grad[...] = jnp.zeros_like(full_grad)
    for peer in range(MP):
        for piece in range(2):
            start = peer * SLICE + piece * LANES
            value = parts[peer, piece * PAD : (piece + 1) * PAD, :]
            value = jnp.concatenate([value, jnp.zeros((PAD, LANES), F32)], 0)
            full_grad[:, start : start + LANES] = value.astype(BF16)
    pooled = lax.dot_general(full_grad[...], weight[...], NT, preferred_element_type=F32)
    head_rows[...] = (pooled[0:PAD] / FRAMES).astype(BF16).astype(F32)
    for total in (s0, s1, s2, s3):
        total[...] = jnp.zeros_like(total)
    three, two = hops[3], hops[2]

    def block_step(block, carry):
        head = head_rows[:, lanes_of(block)]
        taps = tap_rows(taps_in, three, block)
        grad_conv = [head * gate[three, block, f] for f in range(FRAMES)]
        grads = conv_back(grad_conv, taps)
        add_taps(grad_conv, normed, three, block, taps, tap_out)
        add_sums(grads, normed, three, block, s0, s1)
        ups = [head + inv[three, f] * grads[f] for f in range(FRAMES)]
        for f in range(FRAMES):
            up_out[block, f] = ups[f]
        grads = conv_back(
            [ups[f] * gate[two, block, f] for f in range(FRAMES)], tap_rows(taps_in, two, block)
        )
        add_sums(grads, normed, two, block, s2, s3)
        return carry

    lax.fori_loop(0, BLOCKS, block_step, 0)
    write_sums((s0, s1, s2, s3), matrices[0], sums_out, stacked)


def corrected(up, normed, hop, block, first_rows, second_rows):
    return [
        up[f] - first_rows[f] - normed[hop, block, f] * second_rows[f] for f in range(FRAMES)
    ]


def middle_kernel(
    hops, parts, up, normed, gate, inv, inv_row, taps_in, matrices,
    result, up_out, tap_two, tap_one, sums_out,
    s0, s1, s2, s3, a0, a1, b0, b1, natural, stacked,
):
    for total in (s0, s1, s2, s3):
        total[...] = jnp.zeros_like(total)
    three, two, one, zero = hops[3], hops[2], hops[1], hops[0]
    read_sums(parts, inv_row, three, two, stacked, (a0, a1, b0, b1))

    def block_step(block, carry):
        ups = corrected([up[block, f] for f in range(FRAMES)], normed, three, block, a0, a1)
        write_result(ups, natural, result, 0, block)
        taps = tap_rows(taps_in, two, block)
        grad_conv = [ups[f] * gate[two, block, f] for f in range(FRAMES)]
        grads = conv_back(grad_conv, taps)
        add_taps(grad_conv, normed, two, block, taps, tap_two)
        ups = [ups[f] + inv[two, f] * grads[f] for f in range(FRAMES)]
        ups = corrected(ups, normed, two, block, b0, b1)
        write_result(ups, natural, result, 1, block)
        taps = tap_rows(taps_in, one, block)
        grad_conv = [ups[f] * gate[one, block, f] for f in range(FRAMES)]
        grads = conv_back(grad_conv, taps)
        add_taps(grad_conv, normed, one, block, taps, tap_one)
        add_sums(grads, normed, one, block, s0, s1)
        ups = [ups[f] + inv[one, f] * grads[f] for f in range(FRAMES)]
        for f in range(FRAMES):
            up_out[block, f] = ups[f]
        grads = conv_back(
            [ups[f] * gate[zero, block, f] for f in range(FRAMES)],
            tap_rows(taps_in, zero, block),
        )
        add_sums(grads, normed, zero, block, s2, s3)
        return carry

    lax.fori_loop(0, BLOCKS, block_step, 0)
    write_sums((s0, s1, s2, s3), matrices[1], sums_out, stacked)


def end_kernel(
    hops, parts, up, normed, gate, inv, inv_row, taps_in,
    tap_three, tap_two, tap_one, pair_parts,
    result, message,
    a0, a1, b0, b1, natural, stacked, tap_zero, wide,
):
    three, two, one, zero = hops[3], hops[2], hops[1], hops[0]
    read_sums(parts, inv_row, one, zero, stacked, (a0, a1, b0, b1))

    def block_step(block, carry):
        ups = corrected([up[block, f] for f in range(FRAMES)], normed, one, block, a0, a1)
        write_result(ups, natural, result, 1, block)
        taps = tap_rows(taps_in, zero, block)
        grad_conv = [ups[f] * gate[zero, block, f] for f in range(FRAMES)]
        grads = conv_back(grad_conv, taps)
        add_taps(grad_conv, normed, zero, block, taps, tap_zero)
        ups = [ups[f] + inv[zero, f] * grads[f] for f in range(FRAMES)]
        ups = corrected(ups, normed, zero, block, b0, b1)
        write_result(ups, natural, result, 0, block)
        return carry

    lax.fori_loop(0, BLOCKS, block_step, 0)

    wide[...] = jnp.zeros_like(wide)
    for target in range(DP):
        for section, source in enumerate((tap_zero, tap_one, tap_two, tap_three)):
            row = target // 2
            if row < KERNEL:
                for piece in range(5):
                    start = ((target % 2) * 5 + piece) * LANES
                    wide[target * SECTIONS + section, piece : piece + 1, :] = source[
                        row : row + 1, start : start + LANES
                    ]
            wide[target * SECTIONS + section, 5:7, :] = pair_parts[target]
    half = DP * SECTIONS // 2
    message[...] = wide[...].reshape(2 * half * PAD, LANES).astype(BF16)


def order_kernel(hops, last, before, *outs):
    for section in range(SECTIONS):
        steps = (SECTIONS - hops[section]) & (SECTIONS - 1)
        for target in range(SECTIONS):

            @pl.when(steps == target)
            def _(section=section, target=target):
                outs[target][...] = last[section] if section < 2 else before[3 - section]


def tap_sum_kernel(message, out):
    total = jnp.sum(message[...].astype(F32), axis=0).astype(BF16)
    out[...] = jnp.broadcast_to(total[None], out.shape)


def assemble_kernel(hops, own, first, second, third, tap_sum, out, sems):
    copies = []
    for steps, part in enumerate((own, first, second, third)):
        source = (hops[SECTIONS] + SECTIONS - steps) & (SECTIONS - 1)
        for micro in range(MICRO):
            copies.append(
                pltpu.make_async_copy(
                    part.at[pl.ds(micro * OWN, OWN)],
                    out.at[micro, pl.ds(source * OWN, OWN)],
                    sems.at[steps * MICRO + micro],
                )
            )
    for copy in copies:
        copy.start()
    for copy in copies:
        copy.wait()


FRAME_MAJOR = (BLOCKS, FRAMES, PAD, LANES)
ROW_TILE = pltpu.VMEM((FRAMES, PAD, LANES), F32)
NATURAL = pltpu.VMEM((LANES, LANES), F32)
STACKED = pltpu.VMEM((4 * LANES, LANES), F32)
MATRIX_ROWS = 64
SMEM = pl.BlockSpec(memory_space=pltpu.SMEM)


def shape(dims, dtype=F32):
    return jax.ShapeDtypeStruct(dims, dtype)


def cost(flops, moved):
    return pl.CostEstimate(flops=flops, bytes_accessed=moved, transcendentals=0)


def local_call(kernel, hops, operands, outs, scratch, name, estimate=None):
    return pl.pallas_call(
        kernel,
        out_shape=outs,
        in_specs=[SMEM] + [VMEM] * len(operands),
        out_specs=[VMEM] * len(outs),
        scratch_shapes=scratch,
        compiler_params=PARAMS,
        cost_estimate=estimate,
        name=name,
    )(hops, *operands)


def rotate(value, steps):
    pairs = [(source, (source + steps) % SECTIONS) for source in range(SECTIONS)]
    return lax.ppermute(value, "section", pairs)


def per_device(
    saved_inputs, norm_gains, conv_taps, head_weight, queries, key_embeds, positives, pair_weights
):
    section_now = lax.axis_index("section")
    hops = [(section_now - t) % SECTIONS for t in range(SECTIONS)]
    core = lax.axis_index("dp") % 2
    hops += [section_now, core]
    hops = jnp.stack(hops).astype(jnp.int32)
    inputs_all = saved_inputs[0]

    small = jnp.concatenate([conv_taps[0], norm_gains.astype(BF16)], 0)
    sections = []
    for steps in range(SECTIONS):
        target = (section_now + steps) % SECTIONS
        block = lax.dynamic_slice_in_dim(inputs_all, OWN * target, OWN, 1)
        block = jnp.concatenate([block.reshape(ROWS, WIDE), small], 0)
        sections.append(rotate(block, steps) if steps else block)

    pairs = jnp.concatenate([key_embeds, queries], -1).reshape(MICRO * SHARD, 2 * SLICE)
    pairs = jnp.broadcast_to(pairs[None], (DP // 2,) + pairs.shape)
    same_core = [list(range(core, DP, 2)) for core in range(2)]
    texts = lax.all_to_all(pairs, "dp", 0, 0, axis_index_groups=same_core)
    texts = texts.reshape(HALF_TEXTS, 2 * SLICE)
    texts, sections[1], sections[3] = lax.optimization_barrier((texts, sections[1], sections[3]))
    others = lax.ppermute(texts, "dp", [(source, source ^ 1) for source in range(DP)])

    own_queries = lax.dynamic_slice_in_dim(queries, OWN * section_now, OWN, 1)
    own_queries = jnp.pad(own_queries.reshape(CLIPS, SLICE), ((0, 16 - CLIPS), (0, 0)))

    parts = pl.pallas_call(
        scores_kernel,
        out_shape=shape((MP, PAD, HALF_TEXTS)),
        in_specs=[VMEM] * 5,
        out_specs=VMEM,
        compiler_params=PARAMS,
        name="partial_scores",
    )(texts, others, own_queries, sections[1], sections[3])
    parts = lax.all_to_all(parts, "mp", 0, 0)

    parts, pair_parts = pl.pallas_call(
        softmax_kernel,
        out_shape=(shape((MP, 3 * PAD, LANES)), shape((DP, MICRO, LANES))),
        in_specs=[SMEM] * 3 + [VMEM] * 7,
        out_specs=(VMEM, VMEM),
        compiler_params=PARAMS,
        name="softmax_grads_and_row_sums",
    )(hops, positives, pair_weights, parts, texts, others, *sections)
    parts = lax.all_to_all(parts, "mp", 0, 0)

    normed, gate, inv, inv_row, taps, normed_rows = pl.pallas_call(
        forward_kernel,
        out_shape=(
            shape((SECTIONS,) + FRAME_MAJOR),
            shape((SECTIONS,) + FRAME_MAJOR),
            shape((SECTIONS, FRAMES, PAD, LANES)),
            shape((PAD, LANES)),
            shape((SECTIONS, 16, WIDE)),
            shape((SECTIONS, ROWS, WIDE)),
        ),
        in_specs=[VMEM] * 5,
        out_specs=(VMEM,) * 6,
        scratch_shapes=[NATURAL] * 3,
        compiler_params=PARAMS,
        cost_estimate=cost(10**9, 6 * 10**6),
        name="sections_forward",
    )(parts, *sections)
    (matrices,) = local_call(
        pair_kernel,
        hops,
        (normed_rows, gate, taps),
        [shape((2, MATRIX_ROWS, LANES))],
        [NATURAL]
        + [
            pltpu.VMEM((CLIPS * KERNEL * FRAMES, WIDE), BF16),
            pltpu.VMEM((2 * LANES, WIDE), BF16),
            pltpu.VMEM((16, WIDE), BF16),
        ],
        "pair_matrices",
        cost(3 * 10**9, 6 * 10**6),
    )

    sums_shape = shape((MP, PAD + MATRIX_ROWS, LANES))
    tap_shape = shape((16, WIDE))
    up, tap_three, sums = local_call(
        head_kernel,
        hops,
        (parts, head_weight, normed, gate, inv, taps, matrices),
        [shape(FRAME_MAJOR), tap_shape, sums_shape],
        [ROW_TILE] * 4
        + [STACKED, pltpu.VMEM((16, EMB), BF16), pltpu.VMEM((PAD, WIDE), F32)],
        "head_and_sections",
    )
    sums = lax.all_to_all(sums, "mp", 0, 0)
    before, up, tap_two, tap_one, sums = local_call(
        middle_kernel,
        hops,
        (sums, up, normed, gate, inv, inv_row, taps, matrices),
        [shape((2, ROWS, WIDE), BF16), shape(FRAME_MAJOR), tap_shape, tap_shape, sums_shape],
        [ROW_TILE] * 8 + [NATURAL, STACKED],
        "middle_sections",
    )
    sums = lax.all_to_all(sums, "mp", 0, 0)

    last, message = local_call(
        end_kernel,
        hops,
        (sums, up, normed, gate, inv, inv_row, taps, tap_three, tap_two, tap_one, pair_parts),
        [shape((2, ROWS, WIDE), BF16), shape((DP * SECTIONS * PAD, LANES), BF16)],
        [ROW_TILE] * 4
        + [NATURAL, STACKED, pltpu.VMEM((16, WIDE), F32), pltpu.VMEM((DP * SECTIONS, PAD, LANES), F32)],
        "end_sections",
    )
    message = lax.all_to_all(
        message.reshape(DP * SECTIONS, PAD, LANES), ("dp", "section"), 0, 0
    )

    tap_sum = pl.pallas_call(
        tap_sum_kernel,
        out_shape=shape((DP, PAD, LANES), BF16),
        in_specs=[VMEM],
        out_specs=VMEM,
        compiler_params=PARAMS,
        name="tap_sums",
    )(message)
    tap_grads = lax.all_to_all(tap_sum, "dp", 0, 0)[:, 0:5]
    tap_grads = tap_grads.reshape(16, WIDE)[0:KERNEL].astype(F32)

    ordered = local_call(
        order_kernel,
        hops,
        (last, before),
        [shape((ROWS, WIDE), BF16)] * SECTIONS,
        [],
        "order_results",
        cost(10**9, 2 * 10**6),
    )
    pieces = [rotate(part, steps) if steps else part for steps, part in enumerate(ordered)]
    pieces = [part.reshape(CLIPS, FRAMES, WIDE) for part in pieces]
    results = pl.pallas_call(
        assemble_kernel,
        out_shape=shape((MICRO, SHARD, FRAMES, WIDE), BF16),
        in_specs=[SMEM] + [pl.BlockSpec(memory_space=pl.ANY)] * 5,
        out_specs=pl.BlockSpec(memory_space=pl.ANY),
        scratch_shapes=[pltpu.SemaphoreType.DMA((SECTIONS * MICRO,))],
        compiler_params=PARAMS,
        cost_estimate=cost(10**10, 10**7),
        name="assemble_results",
    )(hops, *pieces, tap_sum)
    message, results = lax.optimization_barrier((message, results))
    columns = message[:, 5:7].reshape(DP, SECTIONS, MICRO, LANES)[..., : OWN * 32]
    columns = columns.reshape(DP, SECTIONS, MICRO, OWN, 32)[..., : MICRO * SHARD]
    columns = columns.transpose(0, 2, 1, 3, 4).reshape(DP // 2, 2, MICRO * SHARD, MICRO * SHARD)
    key_grads = 0.0
    for half, part in enumerate((texts, others)):
        pair_grad = lax.dynamic_index_in_dim(columns, core ^ half, 1, keepdims=False)
        key_grads = key_grads + lax.dot_general(
            pair_grad.reshape(HALF_TEXTS, MICRO * SHARD),
            part[:, SLICE:],
            (((0,), (0,)), ((), ())),
            preferred_element_type=F32,
        )
    key_grads = (key_grads * SCORE_SCALE).reshape(MICRO, SHARD, SLICE)

    return (results[None], tap_grads[None], key_grads)


def solution(mesh):
    return jax.shard_map(
        per_device,
        mesh=mesh,
        in_specs=(
            P("section", None, "dp", None, "mp"),
            P("section", "mp"),
            P("section", None, "mp"),
            P("mp", None),
            P(None, "dp", "mp"),
            P(None, "dp", "mp"),
            P(None, "dp"),
            P(None, "dp"),
        ),
        out_specs=(
            P("section", None, "dp", None, "mp"),
            P("section", None, "mp"),
            P(None, "dp", "mp"),
        ),
        check_vma=False,
    )
```

```python
import jax
import jax.numpy as jnp
from jax import lax
from jax.experimental import pallas as pl
from jax.experimental.pallas import tpu as pltpu
from jax.sharding import PartitionSpec as P

D = 5120
EMB = 1024
FRAMES = 16
KERNEL = 15
HALF = KERNEL // 2
SECTIONS = 4
MP = 4
DP = 32
MICRO = 2
SHARD = 12
OWN = SHARD // SECTIONS
CLIPS = MICRO * OWN
ROWS = CLIPS * FRAMES
TEXTS = DP * MICRO * SHARD
HALF_TEXTS = TEXTS // 2
WIDE = D // MP
SLICE = EMB // MP
LANES = 128
BLOCKS = WIDE // LANES
PAD = 8
SCORE_SCALE = 1.0 / 32.0
EPSILON = 1e-05
F32 = jnp.float32
BF16 = jnp.bfloat16

NT = (((1,), (1,)), ((), ()))
VMEM = pl.BlockSpec(memory_space=pltpu.VMEM)
PARAMS = pltpu.CompilerParams(vmem_limit_bytes=24 * 1024 * 1024)


def lane_sums(partial):
    ones = jnp.ones((PAD, LANES), F32)
    return lax.dot_general(
        ones, partial, NT, preferred_element_type=F32, precision=lax.Precision.HIGHEST
    )


def split_halves(value):
    high = value.astype(BF16)
    return high, (value - high.astype(F32)).astype(BF16)


def lanes_of(block):
    return pl.ds(pl.multiple_of(block * LANES, LANES), LANES)


def wide_rows(rows):
    rows = list(rows)
    turned = jnp.concatenate(rows + [jnp.zeros((PAD - len(rows), LANES), F32)], 0).T
    return [
        jnp.broadcast_to(turned[:, index : index + 1], (LANES, LANES))
        for index in range(len(rows))
    ]


def text_micros(rows):
    column = lax.broadcasted_iota(jnp.int32, (rows, TEXTS), 1)
    return ((column * 10923) >> 17) & 1


def scores_kernel(texts, query, out):
    scores = lax.dot_general(query[...], texts[:, 0:SLICE], NT, preferred_element_type=F32)
    shared = jnp.where(text_micros(OWN) == 0, scores[0:OWN], scores[OWN:CLIPS])
    for peer in range(MP):
        out[peer, 0:OWN, :] = shared[:, 0:HALF_TEXTS]
        out[peer, OWN:CLIPS, :] = shared[:, HALF_TEXTS:]
        out[peer, CLIPS:PAD, :] = jnp.zeros((PAD - CLIPS, HALF_TEXTS), F32)


def softmax_kernel(
    hops, positives, weights, parts, texts, x0, x1, x2, x3, message, pair_parts
):
    rows = []
    for x in (x0, x1, x2, x3):
        total = jnp.zeros((ROWS, LANES), F32)
        square = jnp.zeros((ROWS, LANES), F32)
        for block in range(BLOCKS):
            value = x[0:ROWS, block * LANES : (block + 1) * LANES].astype(F32)
            total = total + value
            square = square + value * value
        rows.append(lane_sums(total)[0:1])
        rows.append(lane_sums(square)[0:1])
    stats = jnp.concatenate(rows, 0)
    stats = jnp.concatenate([stats, jnp.zeros((PAD, LANES - ROWS), F32)], 1)

    shared = parts[0]
    for peer in range(1, MP):
        shared = shared + parts[peer]
    shared = jnp.concatenate([shared[0:OWN], shared[OWN:CLIPS]], 1)
    scores = jnp.concatenate([shared, shared, jnp.zeros((PAD - CLIPS, TEXTS), F32)], 0)
    row = lax.broadcasted_iota(jnp.int32, (PAD, TEXTS), 0)
    column = lax.broadcasted_iota(jnp.int32, (PAD, TEXTS), 1)
    clip_micro = jnp.where(row >= OWN, 1, 0)
    scores = jnp.where(text_micros(PAD) == clip_micro, scores * SCORE_SCALE, -1e30)
    exp_scores = jnp.exp(scores - jnp.max(scores, axis=1, keepdims=True))
    probs = exp_scores / jnp.sum(exp_scores, axis=1, keepdims=True)
    base = hops[SECTIONS] * OWN
    positive = jnp.full((PAD, TEXTS), -1, jnp.int32)
    weight = jnp.zeros((PAD, TEXTS), F32)
    for micro in range(MICRO):
        for own in range(OWN):
            index = positives[micro, base + own]
            owner = (index * 10923) >> 17
            index = owner * (MICRO * SHARD) + micro * SHARD + (index - owner * SHARD)
            here = row == micro * OWN + own
            positive = jnp.where(here, index, positive)
            weight = jnp.where(here, weights[micro, base + own], weight)
    hot = jnp.where(column == positive, 1.0, 0.0)
    grad = weight * (probs - hot)
    grad = jnp.concatenate([grad, jnp.zeros((PAD, TEXTS), F32)], 0).astype(BF16)
    result = jnp.dot(grad, texts[:, 0:SLICE], preferred_element_type=F32)
    result = (result * SCORE_SCALE)[0:PAD]
    for peer in range(MP):
        message[peer, 0:PAD, :] = result[:, 0:LANES]
        message[peer, PAD : 2 * PAD, :] = result[:, LANES:]
        message[peer, 2 * PAD :, :] = stats
    grad = grad.astype(F32)
    gap = jnp.zeros((1, 32 - MICRO * SHARD), F32)
    tail = jnp.zeros((1, LANES - OWN * 32), F32)
    for target in range(DP):
        start = target * MICRO * SHARD
        for micro in range(MICRO):
            pieces = []
            for own in range(OWN):
                clip = micro * OWN + own
                pieces += [grad[clip : clip + 1, start : start + MICRO * SHARD], gap]
            pair_parts[target, micro : micro + 1, :] = jnp.concatenate(pieces + [tail], 1)


def spread(rows, outs, naturals):
    for value, natural in zip(wide_rows(rows), naturals):
        natural[...] = value
    for rows_out, natural in zip(outs, naturals):
        for f in range(FRAMES):
            rows_out[f] = natural[pl.ds(f, PAD, stride=FRAMES), :]


def forward_kernel(
    parts, x0, x1, x2, x3,
    normed_out, gate_out, inv_out, inv_row_out, taps_out, rows_out,
    natural, mean_rows, inv_rows,
):
    stats = parts[0, 2 * PAD :, :]
    for peer in range(1, MP):
        stats = stats + parts[peer, 2 * PAD :, :]
    natural[...] = jnp.zeros_like(natural)
    for hop, x in enumerate((x0, x1, x2, x3)):
        mean = stats[2 * hop : 2 * hop + 1] / D
        variance = stats[2 * hop + 1 : 2 * hop + 2] / D - mean * mean
        inv = lax.rsqrt(variance + EPSILON)
        inv_row_out[hop : hop + 1, :] = inv
        mean_rows[...], inv_rows[...] = wide_rows((mean, inv))
        for f in range(FRAMES):
            inv_out[hop, f] = inv_rows[pl.ds(f, PAD, stride=FRAMES), :]

        def block_step(block, carry, hop=hop, x=x):
            lanes = lanes_of(block)
            value = x[0:ROWS, lanes].astype(F32)
            value = (value - mean_rows[0:ROWS, :]) * inv_rows[0:ROWS, :]
            natural[0:ROWS, :] = value
            rows_out[hop, :, lanes] = value
            weights = x[ROWS : ROWS + 16, lanes].astype(F32)
            taps_out[hop, :, lanes] = weights
            taps = [
                jnp.broadcast_to(weights[k : k + 1], (PAD, LANES)) for k in range(KERNEL + 1)
            ]
            hidden = []
            for f in range(FRAMES):
                normed = natural[pl.ds(f, PAD, stride=FRAMES), :]
                normed_out[hop, block, f] = normed
                hidden.append(normed * taps[KERNEL])
            for f in range(FRAMES):
                conv = None
                for k in range(KERNEL):
                    if 0 <= f + k - HALF < FRAMES:
                        term = taps[k] * hidden[f + k - HALF]
                        conv = term if conv is None else conv + term
                gate = jax.nn.sigmoid(conv)
                gate_out[hop, block, f] = gate * (1.0 + conv * (1.0 - gate))
            return carry

        lax.fori_loop(0, BLOCKS, block_step, 0)


def pair_kernel(
    hops, normed_rows, gate, taps_in, out, gate_rows, left, right, plain
):
    frame = lax.broadcasted_iota(jnp.int32, (FRAMES, 2 * LANES), 0)
    lane = lax.broadcasted_iota(jnp.int32, (FRAMES, 2 * LANES), 1)
    lane_frame = lane & (FRAMES - 1)
    lane_clip = (lane & (LANES - 1)) >> 4
    for pair, section in enumerate((2, 0)):
        here = hops[section]
        above = hops[section + 1]

        def block_step(block, carry, here=here, above=above):
            lanes = lanes_of(block)
            weights = taps_in[here, :, lanes]
            weights = weights * weights[KERNEL : KERNEL + 1]
            plain[:, lanes] = weights.astype(BF16)
            for f in range(FRAMES):
                gate_rows[pl.ds(f, PAD, stride=FRAMES), :] = gate[here, block, f]
            right[0:LANES, lanes] = gate_rows[...].astype(BF16)
            right[LANES : LANES + ROWS, lanes] = (
                gate_rows[0:ROWS, :] * normed_rows[above, :, lanes]
            ).astype(BF16)
            right[LANES + ROWS :, lanes] = jnp.zeros((LANES - ROWS, LANES), BF16)
            taps = [
                jnp.broadcast_to(weights[k : k + 1], (FRAMES, LANES)).astype(BF16)
                for k in range(KERNEL)
            ]
            for c in range(CLIPS):
                value = normed_rows[here, c * FRAMES : (c + 1) * FRAMES, lanes].astype(BF16)
                for k in range(KERNEL):
                    start = (c * KERNEL + k) * FRAMES
                    left[start : start + FRAMES, lanes] = value * taps[k]
            return carry

        lax.fori_loop(0, BLOCKS, block_step, 0)
        columns = right[...]
        sums = lax.dot_general(plain[...], columns, NT, preferred_element_type=F32)
        first = jnp.zeros((FRAMES, 2 * LANES), F32)
        second = jnp.zeros((FRAMES, 2 * LANES), F32)
        for k in range(KERNEL):
            first = first + jnp.where(lane_frame == frame - k + HALF, sums[k : k + 1], 0.0)
        for c in range(CLIPS):
            start = c * KERNEL * FRAMES
            sums = lax.dot_general(
                left[start : start + KERNEL * FRAMES, :], columns, NT, preferred_element_type=F32
            )
            total = jnp.zeros((FRAMES, 2 * LANES), F32)
            for k in range(KERNEL):
                total = total + jnp.where(
                    lane_frame == frame - k + HALF, sums[k * FRAMES : (k + 1) * FRAMES], 0.0
                )
            second = second + jnp.where(lane_clip == c, total, 0.0)
        out[pair, 0:16, :] = first[:, 0:LANES]
        out[pair, 16:32, :] = second[:, 0:LANES]
        out[pair, 32:48, :] = first[:, LANES:]
        out[pair, 48:64, :] = second[:, LANES:]


def tap_rows(taps_in, hop, block):
    weights = taps_in[hop, :, lanes_of(block)]
    return [jnp.broadcast_to(weights[k : k + 1], (PAD, LANES)) for k in range(KERNEL + 1)]


def conv_back(grad_conv, taps):
    out = []
    for f in range(FRAMES):
        conv = None
        for k in range(KERNEL):
            if 0 <= f - k + HALF < FRAMES:
                term = taps[k] * grad_conv[f - k + HALF]
                conv = term if conv is None else conv + term
        out.append(conv * taps[KERNEL])
    return out


def add_taps(grad_conv, normed, hop, block, taps, tap_out):
    hidden = [normed[hop, block, f] * taps[KERNEL] for f in range(FRAMES)]
    for k in range(KERNEL):
        total = None
        for f in range(FRAMES):
            if 0 <= f + k - HALF < FRAMES:
                term = grad_conv[f] * hidden[f + k - HALF]
                total = term if total is None else total + term
        tap_out[k : k + 1, lanes_of(block)] = jnp.sum(total, axis=0, keepdims=True)


def add_sums(grads, normed, hop, block, first, second):
    for f in range(FRAMES):
        first[f] += grads[f]
        second[f] += grads[f] * normed[hop, block, f]


def write_sums(sums, matrices, out, stacked):
    for index, total in enumerate(sums):
        for f in range(FRAMES):
            stacked[pl.ds(index * LANES + f, PAD, stride=FRAMES), :] = total[f]
    high, low = split_halves(stacked[...])
    ones = jnp.ones((16, LANES), BF16)
    packed = lax.dot_general(ones, high, NT, preferred_element_type=F32)
    packed = packed + lax.dot_general(ones, low, NT, preferred_element_type=F32)
    packed = [packed[0:1, index * LANES : (index + 1) * LANES] for index in range(len(sums))]
    packed = jnp.concatenate(packed + [jnp.zeros((PAD - len(sums), LANES), F32)], 0)
    for peer in range(MP):
        out[peer, 0:PAD, :] = packed
        out[peer, PAD:, :] = matrices


def read_sums(parts, inv_row, above, here, stacked, outs):
    total = parts[0]
    for peer in range(1, MP):
        total = total + parts[peer]
    scale = inv_row[pl.ds(above, 1), :] / D
    first = total[0:1] * scale
    second = total[1:2] * scale
    matrix = total[PAD:]
    high, low = split_halves(matrix[0:32] * first + matrix[32:64] * second)
    row = lax.broadcasted_iota(jnp.int32, (LANES, LANES), 0)
    column = lax.broadcasted_iota(jnp.int32, (LANES, LANES), 1)
    same = jnp.where((row >> 4) == (column >> 4), 1.0, 0.0).astype(BF16)
    products = jnp.dot(high, same, preferred_element_type=F32)
    products = products + jnp.dot(low, same, preferred_element_type=F32)
    keep = (row & (FRAMES - 1)) == (column & (FRAMES - 1))
    keep = keep[0:FRAMES]
    change_first = jnp.sum(jnp.where(keep, products[0:16], 0.0), axis=0, keepdims=True)
    change_second = jnp.sum(jnp.where(keep, products[16:32], 0.0), axis=0, keepdims=True)
    scale = inv_row[pl.ds(here, 1), :] / D
    rows = (
        first,
        second,
        (total[2:3] - change_first) * scale,
        (total[3:4] - change_second) * scale,
    )
    naturals = [stacked.at[pl.ds(index * LANES, LANES)] for index in range(len(rows))]
    spread(rows, outs, naturals)


def write_result(values, natural, result, index, block):
    for f in range(FRAMES):
        natural[pl.ds(f, PAD, stride=FRAMES), :] = values[f]
    result[index, :, lanes_of(block)] = natural[0:ROWS, :].astype(BF16)


def head_kernel(
    hops, parts, weight, normed, gate, inv, taps_in, matrices,
    up_out, tap_out, sums_out,
    s0, s1, s2, s3, stacked, full_grad, head_rows,
):
    full_grad[...] = jnp.zeros_like(full_grad)
    for peer in range(MP):
        for piece in range(2):
            start = peer * SLICE + piece * LANES
            value = parts[peer, piece * PAD : (piece + 1) * PAD, :]
            value = jnp.concatenate([value, jnp.zeros((PAD, LANES), F32)], 0)
            full_grad[:, start : start + LANES] = value.astype(BF16)
    pooled = lax.dot_general(full_grad[...], weight[...], NT, preferred_element_type=F32)
    head_rows[...] = (pooled[0:PAD] / FRAMES).astype(BF16).astype(F32)
    for total in (s0, s1, s2, s3):
        total[...] = jnp.zeros_like(total)
    three, two = hops[3], hops[2]

    def block_step(block, carry):
        head = head_rows[:, lanes_of(block)]
        taps = tap_rows(taps_in, three, block)
        grad_conv = [head * gate[three, block, f] for f in range(FRAMES)]
        grads = conv_back(grad_conv, taps)
        add_taps(grad_conv, normed, three, block, taps, tap_out)
        add_sums(grads, normed, three, block, s0, s1)
        ups = [head + inv[three, f] * grads[f] for f in range(FRAMES)]
        for f in range(FRAMES):
            up_out[block, f] = ups[f]
        grads = conv_back(
            [ups[f] * gate[two, block, f] for f in range(FRAMES)], tap_rows(taps_in, two, block)
        )
        add_sums(grads, normed, two, block, s2, s3)
        return carry

    lax.fori_loop(0, BLOCKS, block_step, 0)
    write_sums((s0, s1, s2, s3), matrices[0], sums_out, stacked)


def corrected(up, normed, hop, block, first_rows, second_rows):
    return [
        up[f] - first_rows[f] - normed[hop, block, f] * second_rows[f] for f in range(FRAMES)
    ]


def middle_kernel(
    hops, parts, up, normed, gate, inv, inv_row, taps_in, matrices,
    result, up_out, tap_two, tap_one, sums_out,
    s0, s1, s2, s3, a0, a1, b0, b1, natural, stacked,
):
    for total in (s0, s1, s2, s3):
        total[...] = jnp.zeros_like(total)
    three, two, one, zero = hops[3], hops[2], hops[1], hops[0]
    read_sums(parts, inv_row, three, two, stacked, (a0, a1, b0, b1))

    def block_step(block, carry):
        ups = corrected([up[block, f] for f in range(FRAMES)], normed, three, block, a0, a1)
        write_result(ups, natural, result, 0, block)
        taps = tap_rows(taps_in, two, block)
        grad_conv = [ups[f] * gate[two, block, f] for f in range(FRAMES)]
        grads = conv_back(grad_conv, taps)
        add_taps(grad_conv, normed, two, block, taps, tap_two)
        ups = [ups[f] + inv[two, f] * grads[f] for f in range(FRAMES)]
        ups = corrected(ups, normed, two, block, b0, b1)
        write_result(ups, natural, result, 1, block)
        taps = tap_rows(taps_in, one, block)
        grad_conv = [ups[f] * gate[one, block, f] for f in range(FRAMES)]
        grads = conv_back(grad_conv, taps)
        add_taps(grad_conv, normed, one, block, taps, tap_one)
        add_sums(grads, normed, one, block, s0, s1)
        ups = [ups[f] + inv[one, f] * grads[f] for f in range(FRAMES)]
        for f in range(FRAMES):
            up_out[block, f] = ups[f]
        grads = conv_back(
            [ups[f] * gate[zero, block, f] for f in range(FRAMES)],
            tap_rows(taps_in, zero, block),
        )
        add_sums(grads, normed, zero, block, s2, s3)
        return carry

    lax.fori_loop(0, BLOCKS, block_step, 0)
    write_sums((s0, s1, s2, s3), matrices[1], sums_out, stacked)


def end_kernel(
    hops, parts, up, normed, gate, inv, inv_row, taps_in,
    tap_three, tap_two, tap_one, pair_parts,
    result, message,
    a0, a1, b0, b1, natural, stacked, tap_zero, wide,
):
    three, two, one, zero = hops[3], hops[2], hops[1], hops[0]
    read_sums(parts, inv_row, one, zero, stacked, (a0, a1, b0, b1))

    def block_step(block, carry):
        ups = corrected([up[block, f] for f in range(FRAMES)], normed, one, block, a0, a1)
        write_result(ups, natural, result, 1, block)
        taps = tap_rows(taps_in, zero, block)
        grad_conv = [ups[f] * gate[zero, block, f] for f in range(FRAMES)]
        grads = conv_back(grad_conv, taps)
        add_taps(grad_conv, normed, zero, block, taps, tap_zero)
        ups = [ups[f] + inv[zero, f] * grads[f] for f in range(FRAMES)]
        ups = corrected(ups, normed, zero, block, b0, b1)
        write_result(ups, natural, result, 0, block)
        return carry

    lax.fori_loop(0, BLOCKS, block_step, 0)

    wide[...] = jnp.zeros_like(wide)
    for target in range(DP):
        for section, source in enumerate((tap_zero, tap_one, tap_two, tap_three)):
            row = target // 2
            if row < KERNEL:
                for piece in range(5):
                    start = ((target % 2) * 5 + piece) * LANES
                    wide[target * SECTIONS + section, piece : piece + 1, :] = source[
                        row : row + 1, start : start + LANES
                    ]
            wide[target * SECTIONS + section, 5:7, :] = pair_parts[target]
    half = DP * SECTIONS // 2
    message[...] = wide[...].reshape(2 * half * PAD, LANES).astype(BF16)


def order_kernel(hops, last, before, *outs):
    for section in range(SECTIONS):
        steps = (SECTIONS - hops[section]) & (SECTIONS - 1)
        for target in range(SECTIONS):

            @pl.when(steps == target)
            def _(section=section, target=target):
                outs[target][...] = last[section] if section < 2 else before[3 - section]


def tap_sum_kernel(message, out):
    total = jnp.sum(message[...].astype(F32), axis=0).astype(BF16)
    out[...] = jnp.broadcast_to(total[None], out.shape)


def assemble_kernel(hops, own, first, second, third, tap_sum, out, sems):
    copies = []
    for steps, part in enumerate((own, first, second, third)):
        source = (hops[SECTIONS] + SECTIONS - steps) & (SECTIONS - 1)
        for micro in range(MICRO):
            copies.append(
                pltpu.make_async_copy(
                    part.at[pl.ds(micro * OWN, OWN)],
                    out.at[micro, pl.ds(source * OWN, OWN)],
                    sems.at[steps * MICRO + micro],
                )
            )
    for copy in copies:
        copy.start()
    for copy in copies:
        copy.wait()


FRAME_MAJOR = (BLOCKS, FRAMES, PAD, LANES)
ROW_TILE = pltpu.VMEM((FRAMES, PAD, LANES), F32)
NATURAL = pltpu.VMEM((LANES, LANES), F32)
STACKED = pltpu.VMEM((4 * LANES, LANES), F32)
MATRIX_ROWS = 64
SMEM = pl.BlockSpec(memory_space=pltpu.SMEM)


def shape(dims, dtype=F32):
    return jax.ShapeDtypeStruct(dims, dtype)


def cost(flops, moved):
    return pl.CostEstimate(flops=flops, bytes_accessed=moved, transcendentals=0)


def local_call(kernel, hops, operands, outs, scratch, name, estimate=None):
    return pl.pallas_call(
        kernel,
        out_shape=outs,
        in_specs=[SMEM] + [VMEM] * len(operands),
        out_specs=[VMEM] * len(outs),
        scratch_shapes=scratch,
        compiler_params=PARAMS,
        cost_estimate=estimate,
        name=name,
    )(hops, *operands)


def rotate(value, steps):
    pairs = [(source, (source + steps) % SECTIONS) for source in range(SECTIONS)]
    return lax.ppermute(value, "section", pairs)


def per_device(
    saved_inputs, norm_gains, conv_taps, head_weight, queries, key_embeds, positives, pair_weights
):
    section_now = lax.axis_index("section")
    hops = [(section_now - t) % SECTIONS for t in range(SECTIONS)]
    hops += [section_now]
    hops = jnp.stack(hops).astype(jnp.int32)
    inputs_all = saved_inputs[0]

    small = jnp.concatenate([conv_taps[0], norm_gains.astype(BF16)], 0)
    sections = [None] * SECTIONS
    for steps in (0, 1, 2, 3):
        target = (section_now + steps) % SECTIONS
        block = lax.dynamic_slice_in_dim(inputs_all, OWN * target, OWN, 1)
        block = jnp.concatenate([block.reshape(ROWS, WIDE), small], 0)
        sections[steps] = rotate(block, steps) if steps else block

    pairs = jnp.concatenate([key_embeds, queries], -1).reshape(MICRO * SHARD, 2 * SLICE)
    pairs = jnp.broadcast_to(pairs[None], (DP,) + pairs.shape)
    texts = lax.all_to_all(pairs, "dp", 0, 0).reshape(TEXTS, 2 * SLICE)
    texts, *sections = lax.optimization_barrier((texts, *sections[::-1]))
    sections = sections[::-1]

    own_queries = lax.dynamic_slice_in_dim(queries, OWN * section_now, OWN, 1)
    own_queries = jnp.pad(own_queries.reshape(CLIPS, SLICE), ((0, 16 - CLIPS), (0, 0)))

    parts = pl.pallas_call(
        scores_kernel,
        out_shape=shape((MP, PAD, HALF_TEXTS)),
        in_specs=[VMEM] * 2,
        out_specs=VMEM,
        compiler_params=PARAMS,
        name="partial_scores",
    )(texts, own_queries)
    parts = lax.all_to_all(parts, "mp", 0, 0)

    parts, pair_parts = pl.pallas_call(
        softmax_kernel,
        out_shape=(shape((MP, 3 * PAD, LANES)), shape((DP, MICRO, LANES))),
        in_specs=[SMEM] * 3 + [VMEM] * 6,
        out_specs=(VMEM, VMEM),
        compiler_params=PARAMS,
        name="softmax_grads_and_row_sums",
    )(hops, positives, pair_weights, parts, texts, *sections)
    parts = lax.all_to_all(parts, "mp", 0, 0)

    normed, gate, inv, inv_row, taps, normed_rows = pl.pallas_call(
        forward_kernel,
        out_shape=(
            shape((SECTIONS,) + FRAME_MAJOR),
            shape((SECTIONS,) + FRAME_MAJOR),
            shape((SECTIONS, FRAMES, PAD, LANES)),
            shape((PAD, LANES)),
            shape((SECTIONS, 16, WIDE)),
            shape((SECTIONS, ROWS, WIDE)),
        ),
        in_specs=[VMEM] * 5,
        out_specs=(VMEM,) * 6,
        scratch_shapes=[NATURAL] * 3,
        compiler_params=PARAMS,
        cost_estimate=cost(10**9, 6 * 10**6),
        name="sections_forward",
    )(parts, *sections)
    (matrices,) = local_call(
        pair_kernel,
        hops,
        (normed_rows, gate, taps),
        [shape((2, MATRIX_ROWS, LANES))],
        [NATURAL]
        + [
            pltpu.VMEM((CLIPS * KERNEL * FRAMES, WIDE), BF16),
            pltpu.VMEM((2 * LANES, WIDE), BF16),
            pltpu.VMEM((16, WIDE), BF16),
        ],
        "pair_matrices",
        cost(3 * 10**9, 6 * 10**6),
    )

    sums_shape = shape((MP, PAD + MATRIX_ROWS, LANES))
    tap_shape = shape((16, WIDE))
    up, tap_three, sums = local_call(
        head_kernel,
        hops,
        (parts, head_weight, normed, gate, inv, taps, matrices),
        [shape(FRAME_MAJOR), tap_shape, sums_shape],
        [ROW_TILE] * 4
        + [STACKED, pltpu.VMEM((16, EMB), BF16), pltpu.VMEM((PAD, WIDE), F32)],
        "head_and_sections",
    )
    sums = lax.all_to_all(sums, "mp", 0, 0)
    before, up, tap_two, tap_one, sums = local_call(
        middle_kernel,
        hops,
        (sums, up, normed, gate, inv, inv_row, taps, matrices),
        [shape((2, ROWS, WIDE), BF16), shape(FRAME_MAJOR), tap_shape, tap_shape, sums_shape],
        [ROW_TILE] * 8 + [NATURAL, STACKED],
        "middle_sections",
    )
    sums = lax.all_to_all(sums, "mp", 0, 0)

    last, message = local_call(
        end_kernel,
        hops,
        (sums, up, normed, gate, inv, inv_row, taps, tap_three, tap_two, tap_one, pair_parts),
        [shape((2, ROWS, WIDE), BF16), shape((DP * SECTIONS * PAD, LANES), BF16)],
        [ROW_TILE] * 4
        + [NATURAL, STACKED, pltpu.VMEM((16, WIDE), F32), pltpu.VMEM((DP * SECTIONS, PAD, LANES), F32)],
        "end_sections",
    )
    message = lax.all_to_all(
        message.reshape(DP * SECTIONS, PAD, LANES), ("dp", "section"), 0, 0
    )

    tap_sum = pl.pallas_call(
        tap_sum_kernel,
        out_shape=shape((DP, PAD, LANES), BF16),
        in_specs=[VMEM],
        out_specs=VMEM,
        compiler_params=PARAMS,
        name="tap_sums",
    )(message)
    tap_grads = lax.all_to_all(tap_sum, "dp", 0, 0)[:, 0:5]
    tap_grads = tap_grads.reshape(16, WIDE)[0:KERNEL].astype(F32)

    ordered = local_call(
        order_kernel,
        hops,
        (last, before),
        [shape((ROWS, WIDE), BF16)] * SECTIONS,
        [],
        "order_results",
        cost(10**9, 2 * 10**6),
    )
    pieces = [rotate(part, steps) if steps else part for steps, part in enumerate(ordered)]
    pieces = [part.reshape(CLIPS, FRAMES, WIDE) for part in pieces]
    results = pl.pallas_call(
        assemble_kernel,
        out_shape=shape((MICRO, SHARD, FRAMES, WIDE), BF16),
        in_specs=[SMEM] + [pl.BlockSpec(memory_space=pl.ANY)] * 5,
        out_specs=pl.BlockSpec(memory_space=pl.ANY),
        scratch_shapes=[pltpu.SemaphoreType.DMA((SECTIONS * MICRO,))],
        compiler_params=PARAMS,
        cost_estimate=cost(10**10, 10**7),
        name="assemble_results",
    )(hops, *pieces, tap_sum)
    message, results = lax.optimization_barrier((message, results))
    columns = message[:, 5:7].reshape(DP, SECTIONS, MICRO, LANES)[..., : OWN * 32]
    columns = columns.reshape(DP, SECTIONS, MICRO, OWN, 32)[..., : MICRO * SHARD]
    columns = columns.transpose(0, 2, 1, 3, 4).reshape(TEXTS, MICRO * SHARD)
    key_grads = lax.dot_general(
        columns, texts[:, SLICE:], (((0,), (0,)), ((), ())), preferred_element_type=F32
    )
    key_grads = (key_grads * SCORE_SCALE).reshape(MICRO, SHARD, SLICE)
    return (results[None], tap_grads[None], key_grads)


def solution(mesh):
    return jax.shard_map(
        per_device,
        mesh=mesh,
        in_specs=(
            P("section", None, "dp", None, "mp"),
            P("section", "mp"),
            P("section", None, "mp"),
            P("mp", None),
            P(None, "dp", "mp"),
            P(None, "dp", "mp"),
            P(None, "dp"),
            P(None, "dp"),
        ),
        out_specs=(
            P("section", None, "dp", None, "mp"),
            P("section", None, "mp"),
            P(None, "dp", "mp"),
        ),
        check_vma=False,
    )
```

```python
import jax
import jax.numpy as jnp
from jax import lax
from jax.experimental import pallas as pl
from jax.experimental.pallas import tpu as pltpu
from jax.sharding import PartitionSpec as P

D = 5120
EMB = 1024
FRAMES = 16
KERNEL = 15
HALF = KERNEL // 2
SECTIONS = 4
MP = 4
DP = 32
MICRO = 2
SHARD = 12
OWN = SHARD // SECTIONS
CLIPS = MICRO * OWN
ROWS = CLIPS * FRAMES
TEXTS = DP * MICRO * SHARD
HALF_TEXTS = TEXTS // 2
WIDE = D // MP
SLICE = EMB // MP
LANES = 128
BLOCKS = WIDE // LANES
PAD = 8
SCORE_SCALE = 1.0 / 32.0
EPSILON = 1e-05
F32 = jnp.float32
BF16 = jnp.bfloat16

NT = (((1,), (1,)), ((), ()))
VMEM = pl.BlockSpec(memory_space=pltpu.VMEM)
PARAMS = pltpu.CompilerParams(vmem_limit_bytes=24 * 1024 * 1024)


def lane_sums(partial):
    ones = jnp.ones((PAD, LANES), F32)
    return lax.dot_general(
        ones, partial, NT, preferred_element_type=F32, precision=lax.Precision.HIGHEST
    )


def split_halves(value):
    high = value.astype(BF16)
    return high, (value - high.astype(F32)).astype(BF16)


def over_blocks(block_step):
    def two_blocks(pair, carry):
        block_step(2 * pair, carry)
        return block_step(2 * pair + 1, carry)

    lax.fori_loop(0, BLOCKS // 2, two_blocks, 0)


def lanes_of(block):
    return pl.ds(pl.multiple_of(block * LANES, LANES), LANES)


def wide_rows(rows):
    rows = list(rows)
    turned = jnp.concatenate(rows + [jnp.zeros((PAD - len(rows), LANES), F32)], 0).T
    return [
        jnp.broadcast_to(turned[:, index : index + 1], (LANES, LANES))
        for index in range(len(rows))
    ]


def text_micros(rows):
    column = lax.broadcasted_iota(jnp.int32, (rows, TEXTS), 1)
    return ((column * 10923) >> 17) & 1


def scores_kernel(texts, query, out):
    scores = lax.dot_general(query[...], texts[:, 0:SLICE], NT, preferred_element_type=F32)
    shared = jnp.where(text_micros(OWN) == 0, scores[0:OWN], scores[OWN:CLIPS])
    for peer in range(MP):
        out[peer, 0:OWN, :] = shared[:, 0:HALF_TEXTS]
        out[peer, OWN:CLIPS, :] = shared[:, HALF_TEXTS:]
        out[peer, CLIPS:PAD, :] = jnp.zeros((PAD - CLIPS, HALF_TEXTS), F32)


def softmax_kernel(
    hops, positives, weights, parts, texts, x0, x1, x2, x3, message, pair_parts
):
    rows = []
    for x in (x0, x1, x2, x3):
        total = jnp.zeros((ROWS, LANES), F32)
        square = jnp.zeros((ROWS, LANES), F32)
        for block in range(BLOCKS):
            value = x[0:ROWS, block * LANES : (block + 1) * LANES].astype(F32)
            total = total + value
            square = square + value * value
        rows.append(lane_sums(total)[0:1])
        rows.append(lane_sums(square)[0:1])
    stats = jnp.concatenate(rows, 0)
    stats = jnp.concatenate([stats, jnp.zeros((PAD, LANES - ROWS), F32)], 1)

    shared = parts[0]
    for peer in range(1, MP):
        shared = shared + parts[peer]
    shared = jnp.concatenate([shared[0:OWN], shared[OWN:CLIPS]], 1)
    scores = jnp.concatenate([shared, shared, jnp.zeros((PAD - CLIPS, TEXTS), F32)], 0)
    row = lax.broadcasted_iota(jnp.int32, (PAD, TEXTS), 0)
    column = lax.broadcasted_iota(jnp.int32, (PAD, TEXTS), 1)
    clip_micro = jnp.where(row >= OWN, 1, 0)
    scores = jnp.where(text_micros(PAD) == clip_micro, scores * SCORE_SCALE, -1e30)
    exp_scores = jnp.exp(scores - jnp.max(scores, axis=1, keepdims=True))
    probs = exp_scores / jnp.sum(exp_scores, axis=1, keepdims=True)
    base = hops[SECTIONS] * OWN
    positive = jnp.full((PAD, TEXTS), -1, jnp.int32)
    weight = jnp.zeros((PAD, TEXTS), F32)
    for micro in range(MICRO):
        for own in range(OWN):
            index = positives[micro, base + own]
            owner = (index * 10923) >> 17
            index = owner * (MICRO * SHARD) + micro * SHARD + (index - owner * SHARD)
            here = row == micro * OWN + own
            positive = jnp.where(here, index, positive)
            weight = jnp.where(here, weights[micro, base + own], weight)
    hot = jnp.where(column == positive, 1.0, 0.0)
    grad = weight * (probs - hot)
    grad = jnp.concatenate([grad, jnp.zeros((PAD, TEXTS), F32)], 0).astype(BF16)
    result = jnp.dot(grad, texts[:, 0:SLICE], preferred_element_type=F32)
    result = (result * SCORE_SCALE)[0:PAD]
    for peer in range(MP):
        message[peer, 0:PAD, :] = result[:, 0:LANES]
        message[peer, PAD : 2 * PAD, :] = result[:, LANES:]
        message[peer, 2 * PAD :, :] = stats
    grad = grad.astype(F32)
    gap = jnp.zeros((1, 32 - MICRO * SHARD), F32)
    tail = jnp.zeros((1, LANES - OWN * 32), F32)
    for target in range(DP):
        start = target * MICRO * SHARD
        for micro in range(MICRO):
            pieces = []
            for own in range(OWN):
                clip = micro * OWN + own
                pieces += [grad[clip : clip + 1, start : start + MICRO * SHARD], gap]
            pair_parts[target, micro : micro + 1, :] = jnp.concatenate(pieces + [tail], 1)


def spread(rows, outs, naturals):
    for value, natural in zip(wide_rows(rows), naturals):
        natural[...] = value
    for rows_out, natural in zip(outs, naturals):
        for f in range(FRAMES):
            rows_out[f] = natural[pl.ds(f, PAD, stride=FRAMES), :]


def forward_kernel(
    parts, x0, x1, x2, x3,
    normed_out, gate_out, inv_out, inv_row_out, taps_out, rows_out,
    natural, mean_rows, inv_rows,
):
    stats = parts[0, 2 * PAD :, :]
    for peer in range(1, MP):
        stats = stats + parts[peer, 2 * PAD :, :]
    natural[...] = jnp.zeros_like(natural)
    for hop, x in enumerate((x0, x1, x2, x3)):
        mean = stats[2 * hop : 2 * hop + 1] / D
        variance = stats[2 * hop + 1 : 2 * hop + 2] / D - mean * mean
        inv = lax.rsqrt(variance + EPSILON)
        inv_row_out[hop : hop + 1, :] = inv
        mean_rows[...], inv_rows[...] = wide_rows((mean, inv))
        for f in range(FRAMES):
            inv_out[hop, f] = inv_rows[pl.ds(f, PAD, stride=FRAMES), :]

        def block_step(block, carry, hop=hop, x=x):
            lanes = lanes_of(block)
            value = x[0:ROWS, lanes].astype(F32)
            value = (value - mean_rows[0:ROWS, :]) * inv_rows[0:ROWS, :]
            natural[0:ROWS, :] = value
            rows_out[hop, :, lanes] = value
            weights = x[ROWS : ROWS + 16, lanes].astype(F32)
            taps_out[hop, :, lanes] = weights
            taps = [
                jnp.broadcast_to(weights[k : k + 1], (PAD, LANES)) for k in range(KERNEL + 1)
            ]
            hidden = []
            for f in range(FRAMES):
                normed = natural[pl.ds(f, PAD, stride=FRAMES), :]
                normed_out[hop, block, f] = normed
                hidden.append(normed * taps[KERNEL])
            for f in range(FRAMES):
                conv = None
                for k in range(KERNEL):
                    if 0 <= f + k - HALF < FRAMES:
                        term = taps[k] * hidden[f + k - HALF]
                        conv = term if conv is None else conv + term
                gate = jax.nn.sigmoid(conv)
                gate_out[hop, block, f] = gate * (1.0 + conv * (1.0 - gate))
            return carry

        over_blocks(block_step)


def pair_kernel(
    hops, normed_rows, gate, taps_in, out, gate_rows, left, right, plain
):
    frame = lax.broadcasted_iota(jnp.int32, (FRAMES, 2 * LANES), 0)
    lane = lax.broadcasted_iota(jnp.int32, (FRAMES, 2 * LANES), 1)
    lane_frame = lane & (FRAMES - 1)
    lane_clip = (lane & (LANES - 1)) >> 4
    for pair, section in enumerate((2, 0)):
        here = hops[section]
        above = hops[section + 1]

        def block_step(block, carry, here=here, above=above):
            lanes = lanes_of(block)
            weights = taps_in[here, :, lanes]
            weights = weights * weights[KERNEL : KERNEL + 1]
            plain[:, lanes] = weights.astype(BF16)
            for f in range(FRAMES):
                gate_rows[pl.ds(f, PAD, stride=FRAMES), :] = gate[here, block, f]
            right[0:LANES, lanes] = gate_rows[...].astype(BF16)
            right[LANES : LANES + ROWS, lanes] = (
                gate_rows[0:ROWS, :] * normed_rows[above, :, lanes]
            ).astype(BF16)
            right[LANES + ROWS :, lanes] = jnp.zeros((LANES - ROWS, LANES), BF16)
            taps = [
                jnp.broadcast_to(weights[k : k + 1], (FRAMES, LANES)).astype(BF16)
                for k in range(KERNEL)
            ]
            for c in range(CLIPS):
                value = normed_rows[here, c * FRAMES : (c + 1) * FRAMES, lanes].astype(BF16)
                for k in range(KERNEL):
                    start = (c * KERNEL + k) * FRAMES
                    left[start : start + FRAMES, lanes] = value * taps[k]
            return carry

        over_blocks(block_step)
        columns = right[...]
        sums = lax.dot_general(plain[...], columns, NT, preferred_element_type=F32)
        first = jnp.zeros((FRAMES, 2 * LANES), F32)
        second = jnp.zeros((FRAMES, 2 * LANES), F32)
        for k in range(KERNEL):
            first = first + jnp.where(lane_frame == frame - k + HALF, sums[k : k + 1], 0.0)
        for c in range(CLIPS):
            start = c * KERNEL * FRAMES
            sums = lax.dot_general(
                left[start : start + KERNEL * FRAMES, :], columns, NT, preferred_element_type=F32
            )
            total = jnp.zeros((FRAMES, 2 * LANES), F32)
            for k in range(KERNEL):
                total = total + jnp.where(
                    lane_frame == frame - k + HALF, sums[k * FRAMES : (k + 1) * FRAMES], 0.0
                )
            second = second + jnp.where(lane_clip == c, total, 0.0)
        out[pair, 0:16, :] = first[:, 0:LANES]
        out[pair, 16:32, :] = second[:, 0:LANES]
        out[pair, 32:48, :] = first[:, LANES:]
        out[pair, 48:64, :] = second[:, LANES:]


def tap_rows(taps_in, hop, block):
    weights = taps_in[hop, :, lanes_of(block)]
    return [jnp.broadcast_to(weights[k : k + 1], (PAD, LANES)) for k in range(KERNEL + 1)]


def conv_back(grad_conv, taps):
    out = []
    for f in range(FRAMES):
        conv = None
        for k in range(KERNEL):
            if 0 <= f - k + HALF < FRAMES:
                term = taps[k] * grad_conv[f - k + HALF]
                conv = term if conv is None else conv + term
        out.append(conv * taps[KERNEL])
    return out


def add_taps(grad_conv, normed, hop, block, taps, tap_out):
    hidden = [normed[hop, block, f] * taps[KERNEL] for f in range(FRAMES)]
    for k in range(KERNEL):
        total = None
        for f in range(FRAMES):
            if 0 <= f + k - HALF < FRAMES:
                term = grad_conv[f] * hidden[f + k - HALF]
                total = term if total is None else total + term
        tap_out[k : k + 1, lanes_of(block)] = jnp.sum(total, axis=0, keepdims=True)


def add_sums(grads, normed, hop, block, first, second):
    for f in range(FRAMES):
        first[f] += grads[f]
        second[f] += grads[f] * normed[hop, block, f]


def write_sums(sums, matrices, out, stacked):
    for index, total in enumerate(sums):
        for f in range(FRAMES):
            stacked[pl.ds(index * LANES + f, PAD, stride=FRAMES), :] = total[f]
    high, low = split_halves(stacked[...])
    ones = jnp.ones((16, LANES), BF16)
    packed = lax.dot_general(ones, high, NT, preferred_element_type=F32)
    packed = packed + lax.dot_general(ones, low, NT, preferred_element_type=F32)
    packed = [packed[0:1, index * LANES : (index + 1) * LANES] for index in range(len(sums))]
    packed = jnp.concatenate(packed + [jnp.zeros((PAD - len(sums), LANES), F32)], 0)
    for peer in range(MP):
        out[peer, 0:PAD, :] = packed
        out[peer, PAD:, :] = matrices


def read_sums(parts, inv_row, above, here, stacked, outs):
    total = parts[0]
    for peer in range(1, MP):
        total = total + parts[peer]
    scale = inv_row[pl.ds(above, 1), :] / D
    first = total[0:1] * scale
    second = total[1:2] * scale
    matrix = total[PAD:]
    high, low = split_halves(matrix[0:32] * first + matrix[32:64] * second)
    row = lax.broadcasted_iota(jnp.int32, (LANES, LANES), 0)
    column = lax.broadcasted_iota(jnp.int32, (LANES, LANES), 1)
    same = jnp.where((row >> 4) == (column >> 4), 1.0, 0.0).astype(BF16)
    products = jnp.dot(high, same, preferred_element_type=F32)
    products = products + jnp.dot(low, same, preferred_element_type=F32)
    keep = (row & (FRAMES - 1)) == (column & (FRAMES - 1))
    keep = keep[0:FRAMES]
    change_first = jnp.sum(jnp.where(keep, products[0:16], 0.0), axis=0, keepdims=True)
    change_second = jnp.sum(jnp.where(keep, products[16:32], 0.0), axis=0, keepdims=True)
    scale = inv_row[pl.ds(here, 1), :] / D
    rows = (
        first,
        second,
        (total[2:3] - change_first) * scale,
        (total[3:4] - change_second) * scale,
    )
    naturals = [stacked.at[pl.ds(index * LANES, LANES)] for index in range(len(rows))]
    spread(rows, outs, naturals)


def write_result(values, natural, result, index, block):
    for f in range(FRAMES):
        natural[pl.ds(f, PAD, stride=FRAMES), :] = values[f]
    result[index, :, lanes_of(block)] = natural[0:ROWS, :].astype(BF16)


def head_kernel(
    hops, parts, weight, normed, gate, inv, taps_in, matrices,
    up_out, tap_out, sums_out,
    s0, s1, s2, s3, stacked, full_grad, head_rows,
):
    full_grad[...] = jnp.zeros_like(full_grad)
    for peer in range(MP):
        for piece in range(2):
            start = peer * SLICE + piece * LANES
            value = parts[peer, piece * PAD : (piece + 1) * PAD, :]
            value = jnp.concatenate([value, jnp.zeros((PAD, LANES), F32)], 0)
            full_grad[:, start : start + LANES] = value.astype(BF16)
    pooled = lax.dot_general(full_grad[...], weight[...], NT, preferred_element_type=F32)
    head_rows[...] = (pooled[0:PAD] / FRAMES).astype(BF16).astype(F32)
    for total in (s0, s1, s2, s3):
        total[...] = jnp.zeros_like(total)
    three, two = hops[3], hops[2]

    def block_step(block, carry):
        head = head_rows[:, lanes_of(block)]
        taps = tap_rows(taps_in, three, block)
        grad_conv = [head * gate[three, block, f] for f in range(FRAMES)]
        grads = conv_back(grad_conv, taps)
        add_taps(grad_conv, normed, three, block, taps, tap_out)
        add_sums(grads, normed, three, block, s0, s1)
        ups = [head + inv[three, f] * grads[f] for f in range(FRAMES)]
        for f in range(FRAMES):
            up_out[block, f] = ups[f]
        grads = conv_back(
            [ups[f] * gate[two, block, f] for f in range(FRAMES)], tap_rows(taps_in, two, block)
        )
        add_sums(grads, normed, two, block, s2, s3)
        return carry

    lax.fori_loop(0, BLOCKS, block_step, 0)
    write_sums((s0, s1, s2, s3), matrices[0], sums_out, stacked)


def corrected(up, normed, hop, block, first_rows, second_rows):
    return [
        up[f] - first_rows[f] - normed[hop, block, f] * second_rows[f] for f in range(FRAMES)
    ]


def middle_kernel(
    hops, parts, up, normed, gate, inv, inv_row, taps_in, matrices,
    result, up_out, tap_two, tap_one, sums_out,
    s0, s1, s2, s3, a0, a1, b0, b1, natural, stacked,
):
    for total in (s0, s1, s2, s3):
        total[...] = jnp.zeros_like(total)
    three, two, one, zero = hops[3], hops[2], hops[1], hops[0]
    read_sums(parts, inv_row, three, two, stacked, (a0, a1, b0, b1))

    def block_step(block, carry):
        ups = corrected([up[block, f] for f in range(FRAMES)], normed, three, block, a0, a1)
        write_result(ups, natural, result, 0, block)
        taps = tap_rows(taps_in, two, block)
        grad_conv = [ups[f] * gate[two, block, f] for f in range(FRAMES)]
        grads = conv_back(grad_conv, taps)
        add_taps(grad_conv, normed, two, block, taps, tap_two)
        ups = [ups[f] + inv[two, f] * grads[f] for f in range(FRAMES)]
        ups = corrected(ups, normed, two, block, b0, b1)
        write_result(ups, natural, result, 1, block)
        taps = tap_rows(taps_in, one, block)
        grad_conv = [ups[f] * gate[one, block, f] for f in range(FRAMES)]
        grads = conv_back(grad_conv, taps)
        add_taps(grad_conv, normed, one, block, taps, tap_one)
        add_sums(grads, normed, one, block, s0, s1)
        ups = [ups[f] + inv[one, f] * grads[f] for f in range(FRAMES)]
        for f in range(FRAMES):
            up_out[block, f] = ups[f]
        grads = conv_back(
            [ups[f] * gate[zero, block, f] for f in range(FRAMES)],
            tap_rows(taps_in, zero, block),
        )
        add_sums(grads, normed, zero, block, s2, s3)
        return carry

    lax.fori_loop(0, BLOCKS, block_step, 0)
    write_sums((s0, s1, s2, s3), matrices[1], sums_out, stacked)


def end_kernel(
    hops, parts, up, normed, gate, inv, inv_row, taps_in,
    tap_three, tap_two, tap_one, pair_parts,
    result, message,
    a0, a1, b0, b1, natural, stacked, tap_zero, wide,
):
    three, two, one, zero = hops[3], hops[2], hops[1], hops[0]
    read_sums(parts, inv_row, one, zero, stacked, (a0, a1, b0, b1))

    def block_step(block, carry):
        ups = corrected([up[block, f] for f in range(FRAMES)], normed, one, block, a0, a1)
        write_result(ups, natural, result, 1, block)
        taps = tap_rows(taps_in, zero, block)
        grad_conv = [ups[f] * gate[zero, block, f] for f in range(FRAMES)]
        grads = conv_back(grad_conv, taps)
        add_taps(grad_conv, normed, zero, block, taps, tap_zero)
        ups = [ups[f] + inv[zero, f] * grads[f] for f in range(FRAMES)]
        ups = corrected(ups, normed, zero, block, b0, b1)
        write_result(ups, natural, result, 0, block)
        return carry

    lax.fori_loop(0, BLOCKS, block_step, 0)

    wide[...] = jnp.zeros_like(wide)
    for target in range(DP):
        for section, source in enumerate((tap_zero, tap_one, tap_two, tap_three)):
            row = target // 2
            if row < KERNEL:
                for piece in range(5):
                    start = ((target % 2) * 5 + piece) * LANES
                    wide[target * SECTIONS + section, piece : piece + 1, :] = source[
                        row : row + 1, start : start + LANES
                    ]
            wide[target * SECTIONS + section, 5:7, :] = pair_parts[target]
    half = DP * SECTIONS // 2
    message[...] = wide[...].reshape(2 * half * PAD, LANES).astype(BF16)


def order_kernel(hops, last, before, *outs):
    for section in range(SECTIONS):
        steps = (SECTIONS - hops[section]) & (SECTIONS - 1)
        for target in range(SECTIONS):

            @pl.when(steps == target)
            def _(section=section, target=target):
                outs[target][...] = last[section] if section < 2 else before[3 - section]


def tap_sum_kernel(message, out):
    total = jnp.sum(message[...].astype(F32), axis=0).astype(BF16)
    out[...] = jnp.broadcast_to(total[None], out.shape)


def assemble_kernel(hops, third, second, first, own, tap_sum, out, sems):
    copies = []
    for steps, part in enumerate((own, first, second, third)):
        source = (hops[SECTIONS] + SECTIONS - steps) & (SECTIONS - 1)
        for micro in range(MICRO):
            copies.append(
                pltpu.make_async_copy(
                    part.at[pl.ds(micro * OWN, OWN)],
                    out.at[micro, pl.ds(source * OWN, OWN)],
                    sems.at[steps * MICRO + micro],
                )
            )
    for copy in copies:
        copy.start()
    for copy in copies:
        copy.wait()


FRAME_MAJOR = (BLOCKS, FRAMES, PAD, LANES)
ROW_TILE = pltpu.VMEM((FRAMES, PAD, LANES), F32)
NATURAL = pltpu.VMEM((LANES, LANES), F32)
STACKED = pltpu.VMEM((4 * LANES, LANES), F32)
MATRIX_ROWS = 64
SMEM = pl.BlockSpec(memory_space=pltpu.SMEM)


def shape(dims, dtype=F32):
    return jax.ShapeDtypeStruct(dims, dtype)


def cost(flops, moved):
    return pl.CostEstimate(flops=flops, bytes_accessed=moved, transcendentals=0)


def local_call(kernel, hops, operands, outs, scratch, name, estimate=None):
    return pl.pallas_call(
        kernel,
        out_shape=outs,
        in_specs=[SMEM] + [VMEM] * len(operands),
        out_specs=[VMEM] * len(outs),
        scratch_shapes=scratch,
        compiler_params=PARAMS,
        cost_estimate=estimate,
        name=name,
    )(hops, *operands)


def rotate(value, steps):
    pairs = [(source, (source + steps) % SECTIONS) for source in range(SECTIONS)]
    return lax.ppermute(value, "section", pairs)


def per_device(
    saved_inputs, norm_gains, conv_taps, head_weight, queries, key_embeds, positives, pair_weights
):
    section_now = lax.axis_index("section")
    hops = [(section_now - t) % SECTIONS for t in range(SECTIONS)]
    hops += [section_now]
    hops = jnp.stack(hops).astype(jnp.int32)
    inputs_all = saved_inputs[0]

    small = jnp.concatenate([conv_taps[0], norm_gains.astype(BF16)], 0)
    sections = [None] * SECTIONS
    for steps in (0, 1, 2, 3):
        target = (section_now + steps) % SECTIONS
        block = lax.dynamic_slice_in_dim(inputs_all, OWN * target, OWN, 1)
        block = jnp.concatenate([block.reshape(ROWS, WIDE), small], 0)
        sections[steps] = rotate(block, steps) if steps else block

    pairs = jnp.concatenate([key_embeds, queries], -1).reshape(MICRO * SHARD, 2 * SLICE)
    pairs = jnp.broadcast_to(pairs[None], (DP,) + pairs.shape)
    texts = lax.all_to_all(pairs, "dp", 0, 0).reshape(TEXTS, 2 * SLICE)
    texts, *sections = lax.optimization_barrier((texts, *sections[::-1]))
    sections = sections[::-1]

    own_queries = lax.dynamic_slice_in_dim(queries, OWN * section_now, OWN, 1)
    own_queries = jnp.pad(own_queries.reshape(CLIPS, SLICE), ((0, 16 - CLIPS), (0, 0)))

    parts = pl.pallas_call(
        scores_kernel,
        out_shape=shape((MP, PAD, HALF_TEXTS)),
        in_specs=[VMEM] * 2,
        out_specs=VMEM,
        compiler_params=PARAMS,
        name="partial_scores",
    )(texts, own_queries)
    parts = lax.all_to_all(parts, "mp", 0, 0)

    parts, pair_parts = pl.pallas_call(
        softmax_kernel,
        out_shape=(shape((MP, 3 * PAD, LANES)), shape((DP, MICRO, LANES))),
        in_specs=[SMEM] * 3 + [VMEM] * 6,
        out_specs=(VMEM, VMEM),
        compiler_params=PARAMS,
        name="softmax_grads_and_row_sums",
    )(hops, positives, pair_weights, parts, texts, *sections)
    parts = lax.all_to_all(parts, "mp", 0, 0)

    normed, gate, inv, inv_row, taps, normed_rows = pl.pallas_call(
        forward_kernel,
        out_shape=(
            shape((SECTIONS,) + FRAME_MAJOR),
            shape((SECTIONS,) + FRAME_MAJOR),
            shape((SECTIONS, FRAMES, PAD, LANES)),
            shape((PAD, LANES)),
            shape((SECTIONS, 16, WIDE)),
            shape((SECTIONS, ROWS, WIDE)),
        ),
        in_specs=[VMEM] * 5,
        out_specs=(VMEM,) * 6,
        scratch_shapes=[NATURAL] * 3,
        compiler_params=PARAMS,
        cost_estimate=cost(10**9, 6 * 10**6),
        name="sections_forward",
    )(parts, *sections)
    (matrices,) = local_call(
        pair_kernel,
        hops,
        (normed_rows, gate, taps),
        [shape((2, MATRIX_ROWS, LANES))],
        [NATURAL]
        + [
            pltpu.VMEM((CLIPS * KERNEL * FRAMES, WIDE), BF16),
            pltpu.VMEM((2 * LANES, WIDE), BF16),
            pltpu.VMEM((16, WIDE), BF16),
        ],
        "pair_matrices",
        cost(3 * 10**9, 6 * 10**6),
    )

    sums_shape = shape((MP, PAD + MATRIX_ROWS, LANES))
    tap_shape = shape((16, WIDE))
    up, tap_three, sums = local_call(
        head_kernel,
        hops,
        (parts, head_weight, normed, gate, inv, taps, matrices),
        [shape(FRAME_MAJOR), tap_shape, sums_shape],
        [ROW_TILE] * 4
        + [STACKED, pltpu.VMEM((16, EMB), BF16), pltpu.VMEM((PAD, WIDE), F32)],
        "head_and_sections",
    )
    sums = lax.all_to_all(sums, "mp", 0, 0)
    before, up, tap_two, tap_one, sums = local_call(
        middle_kernel,
        hops,
        (sums, up, normed, gate, inv, inv_row, taps, matrices),
        [shape((2, ROWS, WIDE), BF16), shape(FRAME_MAJOR), tap_shape, tap_shape, sums_shape],
        [ROW_TILE] * 8 + [NATURAL, STACKED],
        "middle_sections",
    )
    sums = lax.all_to_all(sums, "mp", 0, 0)

    last, message = local_call(
        end_kernel,
        hops,
        (sums, up, normed, gate, inv, inv_row, taps, tap_three, tap_two, tap_one, pair_parts),
        [shape((2, ROWS, WIDE), BF16), shape((DP * SECTIONS * PAD, LANES), BF16)],
        [ROW_TILE] * 4
        + [NATURAL, STACKED, pltpu.VMEM((16, WIDE), F32), pltpu.VMEM((DP * SECTIONS, PAD, LANES), F32)],
        "end_sections",
    )
    message = lax.all_to_all(
        message.reshape(DP * SECTIONS, PAD, LANES), ("dp", "section"), 0, 0
    )

    tap_sum = pl.pallas_call(
        tap_sum_kernel,
        out_shape=shape((DP, PAD, LANES), BF16),
        in_specs=[VMEM],
        out_specs=VMEM,
        compiler_params=PARAMS,
        name="tap_sums",
    )(message)
    tap_grads = lax.all_to_all(tap_sum, "dp", 0, 0)[:, 0:5]
    tap_grads = tap_grads.reshape(16, WIDE)[0:KERNEL].astype(F32)

    ordered = local_call(
        order_kernel,
        hops,
        (last, before),
        [shape((ROWS, WIDE), BF16)] * SECTIONS,
        [],
        "order_results",
        cost(10**9, 2 * 10**6),
    )
    pieces = [rotate(part, steps) if steps else part for steps, part in enumerate(ordered)]
    pieces = [part.reshape(CLIPS, FRAMES, WIDE) for part in pieces]
    results = pl.pallas_call(
        assemble_kernel,
        out_shape=shape((MICRO, SHARD, FRAMES, WIDE), BF16),
        in_specs=[SMEM] + [pl.BlockSpec(memory_space=pl.ANY)] * 5,
        out_specs=pl.BlockSpec(memory_space=pl.ANY),
        scratch_shapes=[pltpu.SemaphoreType.DMA((SECTIONS * MICRO,))],
        compiler_params=PARAMS,
        cost_estimate=cost(10**10, 10**7),
        name="assemble_results",
    )(hops, *pieces[::-1], tap_sum)
    message, results = lax.optimization_barrier((message, results))
    columns = message[:, 5:7].reshape(DP, SECTIONS, MICRO, LANES)[..., : OWN * 32]
    columns = columns.reshape(DP, SECTIONS, MICRO, OWN, 32)[..., : MICRO * SHARD]
    columns = columns.transpose(0, 2, 1, 3, 4).reshape(TEXTS, MICRO * SHARD)
    key_grads = lax.dot_general(
        columns, texts[:, SLICE:], (((0,), (0,)), ((), ())), preferred_element_type=F32
    )
    key_grads = (key_grads * SCORE_SCALE).reshape(MICRO, SHARD, SLICE)
    return (results[None], tap_grads[None], key_grads)


def solution(mesh):
    return jax.shard_map(
        per_device,
        mesh=mesh,
        in_specs=(
            P("section", None, "dp", None, "mp"),
            P("section", "mp"),
            P("section", None, "mp"),
            P("mp", None),
            P(None, "dp", "mp"),
            P(None, "dp", "mp"),
            P(None, "dp"),
            P(None, "dp"),
        ),
        out_specs=(
            P("section", None, "dp", None, "mp"),
            P("section", None, "mp"),
            P(None, "dp", "mp"),
        ),
        check_vma=False,
    )
```
